128 devices in a mesh: grp: 8 (over x_lo, z), dp: 16 (over y, x_hi, core).
Axes of the slice: x: 4 (x_hi: 2, x_lo: 2; x = x_hi * 2 + x_lo), y: 4, z: 4, core: 2. Of those that a mesh axis runs over, the one named last changes fastest.
Arguments:
- hidden: bfloat16 [16, 1024, 4096], P('dp', 'grp'), may hold values from -8 to 8
- queries: bfloat16 [16, 1024, 4096], P('dp', 'grp'), may hold values from -12 to 12
- out_grad: bfloat16 [16, 1024, 4096], P('dp', 'grp'), may hold values from -6 to 6
- key_weight: bfloat16 [4096, 512], replicated, may hold values from -0.25 to 0.25
- value_weight: bfloat16 [4096, 512], replicated, may hold values from -0.09375 to 0.09375
- seq_lengths: int32 [16, 8], P('dp'), may hold values from 0 to 1024, as said below
- seq_group: int32 [16, 8], P('dp'), may hold values from 0 to 7, as said below
- loader_offsets: int32 [16, 8], P('dp'), may hold values from 0 to 1024, as said below
Outputs:
- grad_query: bfloat16 [16, 1024, 4096], P('dp', 'grp')
- grad_hidden: bfloat16 [16, 1024, 4096], P('dp', 'grp')
- grad_key_weight: bfloat16 [4096, 512], P(('grp', 'dp'))
- grad_value_weight: bfloat16 [4096, 512], P(('grp', 'dp'))
The draws below stay inside these ranges and needn't reach their ends.
Inputs may be any that keep to these rules, and one draw needn't show every extreme that they name: `seq_lengths`: slot lengths are multiples of 128; the slots holding a sequence come first and their lengths sum to 1024; other slots have length 0. In every draw some replica holds a single sequence of 1024 rows. `seq_group`: group numbers give the order of the groups; a group may hold several sequences or none. `loader_offsets`: the loader stream of a replica holds its sequences end to end in some order, and an offset is the first row of its sequence there; slots of length 0 have offset 1024.
All inputs are finite; a program needn't handle non-finite values.
Results may differ from the reference program's by a relative error of at most 0.02.
The reference program's roundings to bfloat16 on the way (of `weights_low` and `dscore`) count: a program that leaves them out, or rounds other values in their place, can miss the bound.
Values may be sent and summed in bfloat16 or wider, within the bound.
A program may use at most 128 MiB of HBM per device.

```python
import math
import jax
import jax.numpy as jnp
from jax import lax

D = 4096
HQ = 32
KVH = 4
HD = 128
TOK_DEV = 128
QW = 4096
KVW = 512
SEQS = 8
ROWS = 1024
REPLICAS = 16
ALL_ROWS = 16384


def layout_draw(key):
    cut_bits = jax.random.randint(jax.random.fold_in(key, 200), (REPLICAS, SEQS - 1), 0, 2)
    heavy_index = jax.random.randint(jax.random.fold_in(key, 201), (), 0, REPLICAS)
    is_heavy = jnp.arange(REPLICAS) == heavy_index
    cut_bits = jnp.where(is_heavy[:, None], 0, cut_bits)
    slot_of_shard = jnp.concatenate([jnp.zeros((REPLICAS, 1), jnp.int32), jnp.cumsum(cut_bits, axis=1).astype(jnp.int32)], axis=1)
    slot_ids = jnp.arange(SEQS, dtype=jnp.int32)
    lengths = TOK_DEV * jnp.sum((slot_of_shard[:, :, None] == slot_ids[None, None, :]).astype(jnp.int32), axis=1)
    groups = jax.random.randint(jax.random.fold_in(key, 202), (REPLICAS, SEQS), 0, SEQS)
    heavy_groups = jnp.where(slot_ids == 0, 0, SEQS - 1)
    groups = jnp.where(is_heavy[:, None], heavy_groups[None, :], groups)
    rank_keys = jax.random.randint(jax.random.fold_in(key, 203), (REPLICAS, SEQS), 0, 1 << 20) * SEQS + slot_ids[None, :]
    before = (rank_keys[:, None, :] < rank_keys[:, :, None]).astype(jnp.int32)
    offsets = jnp.sum(before * lengths[:, None, :], axis=2)
    offsets = jnp.where(lengths > 0, offsets, ROWS)
    return (lengths.astype(jnp.int32), groups.astype(jnp.int32), offsets.astype(jnp.int32))


def draw_seq_lengths(key, part):
    drawn = layout_draw(key)
    return drawn[0]


def draw_seq_group(key, part):
    drawn = layout_draw(key)
    return drawn[1]


def draw_loader_offsets(key, part):
    drawn = layout_draw(key)
    return drawn[2]


def draw_hidden(key, part):
    key = jax.random.fold_in(key, 1)
    values = jnp.clip(jax.random.normal(key, (REPLICAS, ROWS, D), jnp.float32), -6.0, 6.0)
    return values.astype(jnp.bfloat16)


def draw_key_weight(key, part):
    key = jax.random.fold_in(key, 2)
    values = jnp.clip(jax.random.normal(key, (D, KVW), jnp.float32), -2.0, 2.0) * D ** (-0.5)
    return values.astype(jnp.bfloat16)


def draw_queries(key, part):
    key = jax.random.fold_in(key, 3)
    values = jnp.clip(jax.random.normal(key, (REPLICAS, ROWS, QW), jnp.float32), -6.0, 6.0)
    return values.astype(jnp.bfloat16)


def levels(stream_key, dims, split, least, high):
    gain = 1.0
    for dim, shards_of in split:
        heights = jax.random.uniform(jax.random.fold_in(jax.random.fold_in(stream_key, 6), dim), (shards_of,), jnp.float32, least / len(split), high / len(split))
        gain = gain * jnp.repeat(jnp.exp(heights), dims[dim] // shards_of).reshape((-1,) + (1,) * (len(dims) - 1 - dim))
    return gain


def scatter_about(stream_key, dims, deviation, limit, cuts=(), held_as=jnp.bfloat16):
    level = levels(stream_key, dims, cuts, -0.22, 0.18) if cuts else 1.0
    values = jax.random.normal(stream_key, dims, jnp.float32) * deviation * level
    return jnp.minimum(jnp.maximum(values, -limit), limit).astype(held_as)


def setup_inputs(seed: int = 0) -> dict:
    keys = jax.random.split(jax.random.key(seed), 9)
    hidden = draw_hidden(jax.random.fold_in(keys[8], 71), 0)
    queries = draw_queries(jax.random.fold_in(keys[8], 71), 0)
    out_grad = scatter_about(keys[2], (REPLICAS, ROWS, QW), 1.0, 6.0, ((0, 16), (1, 8)))
    key_weight = draw_key_weight(jax.random.fold_in(keys[8], 71), 0)
    value_weight = scatter_about(keys[4], (D, KVW), D ** -0.5, 0.09375)
    seq_lengths = draw_seq_lengths(jax.random.fold_in(keys[8], 71), 0)
    seq_group = draw_seq_group(jax.random.fold_in(keys[8], 71), 0)
    loader_offsets = draw_loader_offsets(jax.random.fold_in(keys[8], 71), 0)
    return {"hidden": hidden, "queries": queries, "out_grad": out_grad, "key_weight": key_weight, "value_weight": value_weight, "seq_lengths": seq_lengths, "seq_group": seq_group, "loader_offsets": loader_offsets}


def layout_tables(lengths, groups, offsets, total_rows):
    slot_count = lengths.shape[0]
    slot_ids = jnp.arange(slot_count, dtype=jnp.int32)
    sort_keys = groups * slot_count + slot_ids
    earlier = (sort_keys[None, :] < sort_keys[:, None]).astype(jnp.int32)
    starts = lax.optimization_barrier(jnp.sum(earlier * lengths[None, :], axis=1)).astype(jnp.int32)
    row_ids = jnp.arange(total_rows, dtype=jnp.int32)
    inside = (row_ids[:, None] >= starts[None, :]) & (row_ids[:, None] < (starts + lengths)[None, :])
    seq_begin = lax.optimization_barrier(jnp.sum(jnp.where(inside, starts[None, :], 0), axis=1)).astype(jnp.int32)
    row_shift = lax.optimization_barrier(jnp.sum(jnp.where(inside, (offsets - starts)[None, :], 0), axis=1)).astype(jnp.int32)
    return (seq_begin, row_ids + row_shift)

def reference(hidden, queries, out_grad, key_weight, value_weight, seq_lengths, seq_group, loader_offsets):
    inv_root = 1.0 / math.sqrt(HD)
    per_group = HQ // KVH

    def one_replica(totals, inputs):
        tokens, query_rows, grad_rows, lengths, groups, offsets = inputs
        seq_begin, source = layout_tables(lengths, groups, offsets, ROWS)
        tokens = jnp.take(tokens, source, axis=0)
        query_rows = jnp.take(query_rows, source, axis=0)
        grad_rows = jnp.take(grad_rows, source, axis=0)
        key_rows = jnp.dot(tokens, key_weight, preferred_element_type=jnp.float32).astype(jnp.bfloat16)
        value_rows = jnp.dot(tokens, value_weight, preferred_element_type=jnp.float32).astype(jnp.bfloat16)
        row_ids = jnp.arange(ROWS, dtype=jnp.int32)
        visible = (row_ids[None, :] <= row_ids[:, None]) & (row_ids[None, :] >= seq_begin[:, None])

        def one_head(running, head_index):
            key_grad, value_grad = running
            group_col = head_index // per_group * HD
            query_head = lax.dynamic_slice_in_dim(query_rows, head_index * HD, HD, 1)
            grad_head = lax.dynamic_slice_in_dim(grad_rows, head_index * HD, HD, 1)
            key_head = lax.dynamic_slice_in_dim(key_rows, group_col, HD, 1)
            value_head = lax.dynamic_slice_in_dim(value_rows, group_col, HD, 1)
            scores = jnp.dot(query_head, key_head.T, preferred_element_type=jnp.float32) * inv_root
            row_top = lax.optimization_barrier(jnp.max(jnp.where(visible, scores, -1e+30), axis=1, keepdims=True))
            exp_terms = jnp.where(visible, jnp.exp(scores - row_top), 0.0)
            weights = exp_terms / lax.optimization_barrier(jnp.sum(exp_terms, axis=1, keepdims=True))
            weights_low = weights.astype(jnp.bfloat16)
            attended = jnp.dot(weights_low, value_head, preferred_element_type=jnp.float32)
            row_delta = lax.optimization_barrier(jnp.sum(grad_head.astype(jnp.float32) * attended, axis=1, keepdims=True))
            prob_grad = jnp.dot(grad_head, value_head.T, preferred_element_type=jnp.float32)
            dscore = (weights * (prob_grad - row_delta)).astype(jnp.bfloat16)
            query_grad = jnp.dot(dscore, key_head, preferred_element_type=jnp.float32) * inv_root
            key_part = jnp.dot(dscore.T, query_head, preferred_element_type=jnp.float32) * inv_root
            value_part = jnp.dot(weights_low.T, grad_head, preferred_element_type=jnp.float32)
            key_grad = lax.dynamic_update_slice_in_dim(key_grad, lax.dynamic_slice_in_dim(key_grad, group_col, HD, 1) + key_part, group_col, 1)
            value_grad = lax.dynamic_update_slice_in_dim(value_grad, lax.dynamic_slice_in_dim(value_grad, group_col, HD, 1) + value_part, group_col, 1)
            return ((key_grad, value_grad), query_grad)
        zero_grads = (jnp.zeros((ROWS, KVW), jnp.float32), jnp.zeros((ROWS, KVW), jnp.float32))
        (key_grad, value_grad), query_grads = lax.scan(one_head, zero_grads, jnp.arange(HQ, dtype=jnp.int32))
        grad_query = jnp.transpose(query_grads, (1, 0, 2)).reshape(ROWS, QW).astype(jnp.bfloat16)
        key_low = key_grad.astype(jnp.bfloat16)
        value_low = value_grad.astype(jnp.bfloat16)
        grad_hidden = (jnp.dot(key_low, key_weight.T, preferred_element_type=jnp.float32) + jnp.dot(value_low, value_weight.T, preferred_element_type=jnp.float32)).astype(jnp.bfloat16)
        key_total = totals[0] + jnp.dot(tokens.T, key_low, preferred_element_type=jnp.float32)
        value_total = totals[1] + jnp.dot(tokens.T, value_low, preferred_element_type=jnp.float32)
        return ((key_total, value_total), (grad_query, grad_hidden))
    start_totals = (jnp.zeros((D, KVW), jnp.float32), jnp.zeros((D, KVW), jnp.float32))
    (key_total, value_total), (grad_query, grad_hidden) = lax.scan(one_replica, start_totals, (hidden, queries, out_grad, seq_lengths, seq_group, loader_offsets))
    norm_factor = 1.0 / math.sqrt(ALL_ROWS)
    return (grad_query, grad_hidden, (key_total * norm_factor).astype(jnp.bfloat16), (value_total * norm_factor).astype(jnp.bfloat16))
```

```python
import math

import jax
import jax.numpy as jnp
from jax import lax
from jax.experimental import pallas as pl
from jax.experimental.pallas import tpu as pltpu
from jax.sharding import PartitionSpec as P

HQ = 32
KVH = 4
HD = 128
SLOTS = 8
QBLK = 256
LOW = jnp.bfloat16
FULL = jnp.float32
MESH = pl.DeviceIdType.MESH
NT = (((1,), (1,)), ((), ()))


def each(first, last, step):
    def body(i, carry):
        step(i)
        return carry

    lax.fori_loop(first, last, body, 0)


def layer_kernel(
    group_size,
    replica_count,
    lengths,
    groups,
    offsets,
    hidden,
    queries,
    out_grad,
    key_weight,
    value_weight,
    grad_query,
    grad_hidden,
    grad_key,
    grad_value,
    hid_v,
    kw_v,
    vw_v,
    q_r,
    do_r,
    kv_s,
    kv_r,
    kt_v,
    hid_r,
    hid_t,
    s_v,
    pg_v,
    wl_v,
    ds_v,
    acc,
    dq_s,
    dq_g,
    ex_s,
    ex_r,
    dkv_g,
    prod,
    prod_s,
    rs_r,
    gh_v,
    begin_v,
    load_sem,
    own_sem,
    q_send,
    q_recv,
    do_send,
    do_recv,
    kv_send,
    kv_recv,
    hid_send,
    hid_recv,
    dq_send,
    dq_recv,
    dq_own,
    ex_send,
    ex_recv,
    ag_send,
    ag_recv,
    rs_send,
    rs_recv,
    gh_sem,
):
    me = lax.axis_index("grp")
    rep = lax.axis_index("dp")
    rows = hidden.shape[0]
    total = rows * group_size
    heads = HQ // group_size
    wide = heads * HD
    chunk = hidden.shape[1] // group_size
    piece = chunk // replica_count
    half = me // KVH
    partner = lax.rem(me + KVH, group_size)
    inv_root = 1.0 / math.sqrt(HD)
    exp_scale = inv_root / math.log(2.0)
    blocks = total // QBLK
    per_block = QBLK // rows

    def peer(o):
        return lax.rem(me + o, group_size)

    def origin(o):
        return lax.rem(me - o + group_size, group_size)

    def first_col(device):
        return lax.rem(device, KVH) * (2 * wide) + (device // KVH) * wide

    def rows_of(block):
        return pl.ds(pl.multiple_of(block * rows, rows), rows)

    def cols(at, n):
        return pl.ds(pl.multiple_of(at, n), n)

    load_hid = pltpu.make_async_copy(hidden, hid_v, load_sem.at[0])
    load_kw = pltpu.make_async_copy(key_weight, kw_v, load_sem.at[1])
    load_vw = pltpu.make_async_copy(value_weight, vw_v, load_sem.at[2])
    load_hid.start()
    load_kw.start()
    load_vw.start()

    barrier = pltpu.get_barrier_semaphore()
    each(
        1,
        group_size,
        lambda o: pl.semaphore_signal(
            barrier, inc=1, device_id={"grp": peer(o)}, device_id_type=MESH
        ),
    )
    each(
        1,
        replica_count,
        lambda o: pl.semaphore_signal(
            barrier,
            inc=1,
            device_id={"dp": lax.rem(rep + o, replica_count)},
            device_id_type=MESH,
        ),
    )

    def q_copy(h, o, to):
        dest = peer(o)
        at = rows_of(me if to else origin(o))
        return pltpu.make_async_remote_copy(
            src_ref=queries.at[:, cols(first_col(dest) + h * HD, HD)],
            dst_ref=q_r.at[h, at, :],
            send_sem=q_send.at[h, o],
            recv_sem=q_recv.at[h, o],
            device_id={"grp": dest},
            device_id_type=MESH,
        )

    def do_copy(h, o, to):
        dest = peer(o)
        at = rows_of(me if to else origin(o))
        return pltpu.make_async_remote_copy(
            src_ref=out_grad.at[:, cols(first_col(dest) + h * HD, HD)],
            dst_ref=do_r.at[h, at, :],
            send_sem=do_send.at[h, o],
            recv_sem=do_recv.at[h, o],
            device_id={"grp": dest},
            device_id_type=MESH,
        )

    def kv_copy(o, to):
        dest = peer(o)
        at = rows_of(me if to else origin(o))
        return pltpu.make_async_remote_copy(
            src_ref=kv_s.at[lax.rem(dest, KVH)],
            dst_ref=kv_r.at[:, at, :],
            send_sem=kv_send.at[o],
            recv_sem=kv_recv.at[o],
            device_id={"grp": dest},
            device_id_type=MESH,
        )

    def hid_copy(o, to):
        dest = peer(o)
        at = rows_of(me if to else origin(o))
        return pltpu.make_async_remote_copy(
            src_ref=hidden.at[:, cols(dest * chunk, chunk)],
            dst_ref=hid_r.at[at, :],
            send_sem=hid_send.at[o],
            recv_sem=hid_recv.at[o],
            device_id={"grp": dest},
            device_id_type=MESH,
        )

    def dq_copy(h, o, to):
        dest = peer(o)
        at = first_col(me if to else origin(o)) + h * HD
        return pltpu.make_async_remote_copy(
            src_ref=dq_g.at[h, rows_of(dest), :],
            dst_ref=grad_query.at[:, cols(at, HD)],
            send_sem=dq_send.at[h, o],
            recv_sem=dq_recv.at[h, o],
            device_id={"grp": dest},
            device_id_type=MESH,
        )

    def dq_stay(h):
        return pltpu.make_async_copy(
            dq_g.at[h, rows_of(me), :],
            grad_query.at[:, cols(first_col(me) + h * HD, HD)],
            dq_own.at[h],
        )

    def ex_copy(b):
        at = pl.ds(b * QBLK, QBLK)
        return pltpu.make_async_remote_copy(
            src_ref=ex_s.at[at, :],
            dst_ref=ex_r.at[at, :],
            send_sem=ex_send.at[b],
            recv_sem=ex_recv.at[b],
            device_id={"grp": partner},
            device_id_type=MESH,
        )

    def ag_copy(b, o, to):
        dest = peer(o)
        at = pl.ds(b * per_block, per_block)
        return pltpu.make_async_remote_copy(
            src_ref=dkv_g.at[at, :, cols(me * HD, HD)],
            dst_ref=dkv_g.at[at, :, cols((me if to else origin(o)) * HD, HD)],
            send_sem=ag_send.at[b, o],
            recv_sem=ag_recv.at[b, o],
            device_id={"grp": dest},
            device_id_type=MESH,
        )

    def rs_copy(o):
        dest = lax.rem(rep + o, replica_count)
        return pltpu.make_async_remote_copy(
            src_ref=prod_s.at[pl.ds(pl.multiple_of(dest * piece, piece), piece), :],
            dst_ref=rs_r.at[o],
            send_sem=rs_send.at[o],
            recv_sem=rs_recv.at[o],
            device_id={"dp": dest},
            device_id_type=MESH,
        )

    def own_q(h):
        return pltpu.make_async_copy(
            queries.at[:, cols(first_col(me) + h * HD, HD)],
            q_r.at[h, rows_of(me), :],
            own_sem.at[0, h],
        )

    def own_do(h):
        return pltpu.make_async_copy(
            out_grad.at[:, cols(first_col(me) + h * HD, HD)],
            do_r.at[h, rows_of(me), :],
            own_sem.at[1, h],
        )

    own_hid = pltpu.make_async_copy(
        hidden.at[:, cols(me * chunk, chunk)], hid_r.at[rows_of(me), :], load_sem.at[3]
    )

    def send_heads(first, last):
        def one(i):
            h = i // (group_size - 1)
            o = lax.rem(i, group_size - 1) + 1
            q_copy(h, o, True).start()
            do_copy(h, o, True).start()

        each(first * (group_size - 1), last * (group_size - 1), one)

    pl.semaphore_wait(barrier, group_size - 1 + replica_count - 1)

    send_heads(0, 2)
    for h in range(heads):
        own_q(h).start()
        own_do(h).start()
    own_hid.start()

    load_hid.wait()
    load_kw.wait()
    hid_rows = hid_v[...]

    def project(weight, which):
        for g in range(0, KVH, 2):
            both = jnp.dot(
                hid_rows, weight[:, g * HD : (g + 2) * HD], preferred_element_type=FULL
            ).astype(LOW)
            kv_s[g, which] = both[:, :HD]
            kv_s[g + 1, which] = both[:, HD:]

    project(kw_v, 0)
    load_vw.wait()
    project(vw_v, 1)
    each(1, group_size, lambda o: kv_copy(o, True).start())
    send_heads(2, heads)
    each(1, group_size, lambda o: hid_copy(o, True).start())
    kv_r[:, rows_of(me), :] = kv_s[lax.rem(me, KVH)]

    row_ids = lax.broadcasted_iota(jnp.int32, (1, total), 1)
    begin = jnp.zeros((1, total), jnp.int32)
    for s in range(SLOTS):
        at, size = offsets[0, s], lengths[0, s]
        begin = jnp.where((row_ids >= at) & (row_ids < at + size), at, begin)
    begin_v[...] = begin
    starts = []
    for s in range(SLOTS):
        start = jnp.int32(0)
        for t in range(SLOTS):
            if t < s:
                before = groups[0, t] <= groups[0, s]
            else:
                before = groups[0, t] < groups[0, s]
            if t != s:
                start = start + jnp.where(before, lengths[0, t], 0)
        starts.append(start)

    def source_row(row):
        found = jnp.int32(0)
        for s in range(SLOTS):
            inside = (row >= starts[s]) & (row < starts[s] + lengths[0, s])
            found = found + jnp.where(inside, offsets[0, s] + row - starts[s], 0)
        return found // rows

    sources = [source_row(b * rows) for b in range(group_size)]

    acc[...] = jnp.zeros_like(acc)
    each(1, group_size, lambda o: kv_copy(o, False).wait_recv())
    kt_v[...] = kv_r[0].T

    scale_other = jnp.where(half == 1, inv_root, 1.0).astype(FULL)
    scale_mine = jnp.where(half == 0, inv_root, 1.0).astype(FULL)
    key_ids = lax.broadcasted_iota(jnp.int32, (HD, QBLK), 0)
    lane_ids = lax.broadcasted_iota(jnp.int32, (HD, QBLK), 1)

    def fold(tile):
        return tile.reshape(HD // 8, 8, QBLK)

    def attend(h, b):
        r0 = b * QBLK
        keys = r0 + QBLK
        tiles = keys // HD
        q_blk = q_r[h, r0 : r0 + QBLK, :]
        do_blk = do_r[h, r0 : r0 + QBLK, :]
        begin_row = begin_v[:, r0 : r0 + QBLK]
        s_v[0:keys, :] = lax.dot_general(
            kv_r[0, 0:keys, :], q_blk, NT, preferred_element_type=FULL
        )
        pg_v[0:keys, :] = lax.dot_general(
            kv_r[1, 0:keys, :], do_blk, NT, preferred_element_type=FULL
        )
        top = jnp.full((8, QBLK), -1e30, FULL)
        for j in range(tiles):
            at = slice(j * HD, (j + 1) * HD)
            seen = key_ids + j * HD >= begin_row
            if j * HD >= r0:
                seen = seen & (key_ids + (j * HD - r0) <= lane_ids)
            tile = jnp.where(seen, s_v[at, :], -1e30)
            s_v[at, :] = tile
            top = jnp.maximum(top, jnp.max(fold(tile), axis=0))
        top = jnp.max(top, axis=0, keepdims=True)
        mass = jnp.zeros((8, QBLK), FULL)
        for j in range(tiles):
            at = slice(j * HD, (j + 1) * HD)
            tile = jnp.exp2((s_v[at, :] - top) * exp_scale)
            s_v[at, :] = tile
            mass = mass + jnp.sum(fold(tile), axis=0)
        inverse = 1.0 / jnp.sum(mass, axis=0, keepdims=True)
        delta = jnp.zeros((8, QBLK), FULL)
        for j in range(tiles):
            at = slice(j * HD, (j + 1) * HD)
            weights = s_v[at, :] * inverse
            low = weights.astype(LOW)
            s_v[at, :] = weights
            wl_v[at, :] = low
            delta = delta + jnp.sum(fold(low.astype(FULL) * pg_v[at, :]), axis=0)
        delta = jnp.sum(delta, axis=0, keepdims=True)
        for j in range(tiles):
            at = slice(j * HD, (j + 1) * HD)
            ds_v[at, :] = (s_v[at, :] * (pg_v[at, :] - delta)).astype(LOW)
        acc[1, 0:keys, :] += jnp.dot(wl_v[0:keys, :], do_blk, preferred_element_type=FULL)
        acc[0, 0:keys, :] += jnp.dot(ds_v[0:keys, :], q_blk, preferred_element_type=FULL)
        grad_t = jnp.dot(kt_v[:, 0:keys], ds_v[0:keys, :], preferred_element_type=FULL)
        grad_rows = (grad_t * inv_root).T.astype(LOW)
        for j in range(QBLK // rows):
            dq_s[r0 // rows + j] = grad_rows[j * rows : (j + 1) * rows, :]

    def one_head(h):
        own_q(h).wait()
        own_do(h).wait()

        def arrive(o):
            q_copy(h, o, False).wait_recv()
            do_copy(h, o, False).wait_recv()

        each(1, group_size, arrive)
        for b in reversed(range(blocks)):
            attend(h, b)

            @pl.when(h == heads - 1)
            def _():
                at = slice(b * QBLK, (b + 1) * QBLK)
                ex_s[at, :] = (acc[1 - half, at, :] * scale_other).astype(LOW)
                ex_copy(b).start()

        for b in range(group_size):
            dq_g[h, b * rows : (b + 1) * rows, :] = dq_s[sources[b]]
        each(1, group_size, lambda o: dq_copy(h, o, True).start())
        dq_stay(h).start()

    each(0, heads, one_head)

    for b in reversed(range(blocks)):
        at = slice(b * QBLK, (b + 1) * QBLK)
        ex_copy(b).wait_recv()
        merged = (acc[half, at, :] * scale_mine + ex_r[at, :].astype(FULL)).astype(LOW)
        for j in range(per_block):
            dkv_g[b * per_block + j, :, cols(me * HD, HD)] = merged[
                j * rows : (j + 1) * rows, :
            ]
        each(1, group_size, lambda o: ag_copy(b, o, True).start())

    own_hid.wait()
    each(1, group_size, lambda o: hid_copy(o, False).wait_recv())
    hid_t[...] = hid_r[...].T

    for b in reversed(range(blocks)):
        at = slice(b * QBLK, (b + 1) * QBLK)
        each(1, group_size, lambda o: ag_copy(b, o, False).wait_recv())
        grads = dkv_g[b * per_block : (b + 1) * per_block].reshape(QBLK, 2 * KVH * HD)
        term = jnp.dot(hid_t[:, at], grads, preferred_element_type=FULL)
        if b == blocks - 1:
            prod[...] = term
        elif b > 0:
            prod[...] += term
        else:
            term = prod[...] + term
            prod[...] = term
            prod_s[...] = term.astype(LOW)
    each(1, replica_count, lambda o: rs_copy(o).start())

    mine = sources[0]
    for b in range(1, group_size):
        mine = jnp.where(me == b, sources[b], mine)
    kvw = KVH * HD
    dk_rows = dkv_g[mine, :, 0:kvw]
    dv_rows = dkv_g[mine, :, kvw : 2 * kvw]

    def hidden_tile(t):
        at = pl.ds(pl.multiple_of(t * 512, 512), 512)
        tile = lax.dot_general(
            dk_rows, kw_v[at, :], NT, preferred_element_type=FULL
        ) + lax.dot_general(dv_rows, vw_v[at, :], NT, preferred_element_type=FULL)
        gh_v[:, at] = tile.astype(LOW)

    each(0, hidden.shape[1] // 512, hidden_tile)
    gh_out = pltpu.make_async_copy(gh_v, grad_hidden, gh_sem)
    gh_out.start()

    norm = 1.0 / math.sqrt(total * replica_count)
    own = pl.ds(pl.multiple_of(rep * piece, piece), piece)
    each(1, replica_count, lambda o: rs_copy(o).wait_recv())
    summed = prod[own, :]
    for o in range(1, replica_count):
        summed = summed + rs_r[o].astype(FULL)
    summed = (summed * norm).astype(LOW)
    grad_key[...] = summed[:, 0:kvw]
    grad_value[...] = summed[:, kvw : 2 * kvw]

    gh_out.wait()
    each(1, replica_count, lambda o: rs_copy(o).wait_send())

    def close(o):
        kv_copy(o, True).wait_send()
        hid_copy(o, True).wait_send()
        for h in range(heads):
            q_copy(h, o, True).wait_send()
            do_copy(h, o, True).wait_send()
            dq_copy(h, o, True).wait_send()
            dq_copy(h, o, False).wait_recv()
        for b in range(blocks):
            ag_copy(b, o, True).wait_send()

    each(1, group_size, close)
    for h in range(heads):
        dq_stay(h).wait()
    for b in range(blocks):
        ex_copy(b).wait_send()


def on_device(
    hidden, queries, out_grad, key_weight, value_weight, seq_lengths, seq_group, loader_offsets
):
    group_size = lax.axis_size("grp")
    replica_count = lax.axis_size("dp")
    rows, width = hidden.shape[1:]
    total = rows * group_size
    heads = HQ // group_size
    kvw = KVH * HD
    chunk = width // group_size
    piece = chunk // replica_count
    blocks = total // QBLK
    dma = pltpu.SemaphoreType.DMA
    scratch = [
        pltpu.VMEM((rows, width), LOW),
        pltpu.VMEM((width, kvw), LOW),
        pltpu.VMEM((width, kvw), LOW),
        pltpu.VMEM((heads, total, HD), LOW),
        pltpu.VMEM((heads, total, HD), LOW),
        pltpu.VMEM((KVH, 2, rows, HD), LOW),
        pltpu.VMEM((2, total, HD), LOW),
        pltpu.VMEM((HD, total), LOW),
        pltpu.VMEM((total, chunk), LOW),
        pltpu.VMEM((chunk, total), LOW),
        pltpu.VMEM((total, QBLK), FULL),
        pltpu.VMEM((total, QBLK), FULL),
        pltpu.VMEM((total, QBLK), LOW),
        pltpu.VMEM((total, QBLK), LOW),
        pltpu.VMEM((2, total, HD), FULL),
        pltpu.VMEM((group_size, rows, HD), LOW),
        pltpu.VMEM((heads, total, HD), LOW),
        pltpu.VMEM((total, HD), LOW),
        pltpu.VMEM((total, HD), LOW),
        pltpu.VMEM((group_size, rows, 2 * kvw), LOW),
        pltpu.VMEM((chunk, 2 * kvw), FULL),
        pltpu.VMEM((chunk, 2 * kvw), LOW),
        pltpu.VMEM((replica_count, piece, 2 * kvw), LOW),
        pltpu.VMEM((rows, width), LOW),
        pltpu.VMEM((1, total), jnp.int32),
        dma((4,)),
        dma((2, heads)),
        dma((heads, group_size)),
        dma((heads, group_size)),
        dma((heads, group_size)),
        dma((heads, group_size)),
        dma((group_size,)),
        dma((group_size,)),
        dma((group_size,)),
        dma((group_size,)),
        dma((heads, group_size)),
        dma((heads, group_size)),
        dma((heads,)),
        dma((blocks,)),
        dma((blocks,)),
        dma((blocks, group_size)),
        dma((blocks, group_size)),
        dma((replica_count,)),
        dma((replica_count,)),
        dma,
    ]
    smem = pl.BlockSpec(memory_space=pltpu.SMEM)
    vmem = pl.BlockSpec(memory_space=pltpu.VMEM)
    anywhere = pl.BlockSpec(memory_space=pl.ANY)

    def kernel(*refs):
        layer_kernel(group_size, replica_count, *refs)

    grad_query, grad_hidden, grad_key, grad_value = pl.pallas_call(
        kernel,
        out_shape=(
            jax.ShapeDtypeStruct((rows, HQ * HD), LOW),
            jax.ShapeDtypeStruct((rows, width), LOW),
            jax.ShapeDtypeStruct((piece, kvw), LOW),
            jax.ShapeDtypeStruct((piece, kvw), LOW),
        ),
        in_specs=[smem, smem, smem] + [anywhere] * 5,
        out_specs=(anywhere, anywhere, vmem, vmem),
        scratch_shapes=scratch,
        compiler_params=pltpu.CompilerParams(
            collective_id=0, has_side_effects=True, vmem_limit_bytes=56 * 1024 * 1024
        ),
        name="layer",
    )(
        seq_lengths,
        seq_group,
        loader_offsets,
        hidden[0],
        queries[0],
        out_grad[0],
        key_weight,
        value_weight,
    )
    return (grad_query[None], grad_hidden[None], grad_key, grad_value)


def solution(mesh):
    placed = (
        P("dp", "grp", None),
        P("dp", "grp", None),
        P("dp", "grp", None),
        P(),
        P(),
        P("dp", None),
        P("dp", None),
        P("dp", None),
    )
    return jax.shard_map(
        on_device,
        mesh=mesh,
        in_specs=placed,
        out_specs=(
            P("dp", "grp", None),
            P("dp", "grp", None),
            P(("grp", "dp"), None),
            P(("grp", "dp"), None),
        ),
        check_vma=False,
    )
```

```python
import math

import jax
import jax.numpy as jnp
from jax import lax
from jax.experimental import pallas as pl
from jax.experimental.pallas import tpu as pltpu
from jax.sharding import PartitionSpec as P

HQ = 32
KVH = 4
HD = 128
SLOTS = 8
QBLK = 256
ZS = 4
LOW = jnp.bfloat16
FULL = jnp.float32
MESH = pl.DeviceIdType.MESH
NT = (((1,), (1,)), ((), ()))


def each(first, last, step):
    def body(i, carry):
        step(i)
        return carry

    lax.fori_loop(first, last, body, 0)


def layer_kernel(
    group_size,
    replica_count,
    lengths,
    groups,
    offsets,
    hidden,
    queries,
    out_grad,
    key_weight,
    value_weight,
    grad_query,
    grad_hidden,
    grad_key,
    grad_value,
    hid_v,
    kw_v,
    vw_v,
    q_r,
    do_r,
    kv_s,
    kv_r,
    kt_v,
    hid_s,
    hid_t,
    s_v,
    pg_v,
    wl_v,
    ds_v,
    acc,
    dq_s,
    dq_g,
    dl_s,
    dl_r,
    dg_s,
    dg_r,
    dkv_all,
    prod,
    prod_s,
    rs_r,
    gh_v,
    begin_v,
    load_sem,
    own_sem,
    q_send,
    q_recv,
    do_send,
    do_recv,
    kv_send,
    kv_recv,
    hid_send,
    hid_recv,
    dq_send,
    dq_recv,
    dq_own,
    dl_send,
    dl_recv,
    dg_send,
    dg_recv,
    ya_send,
    ya_recv,
    yc_send,
    yc_recv,
    rs_send,
    rs_recv,
    gh_sem,
):
    me = lax.axis_index("grp")
    rep = lax.axis_index("dp")
    x_lo, z = me // ZS, lax.rem(me, ZS)
    y, x_hi, core = rep // 4, lax.rem(rep // 2, 2), lax.rem(rep, 2)
    ys = replica_count // 4
    column = 2 * ys
    summed_over = 2 * group_size
    rows = hidden.shape[0]
    width = hidden.shape[1]
    total = rows * group_size
    heads = HQ // group_size
    wide = heads * HD
    kvw = KVH * HD
    piece = width // (group_size * replica_count)
    inv_root = 1.0 / math.sqrt(HD)
    exp_scale = inv_root / math.log(2.0)
    blocks = total // QBLK
    per_block = QBLK // rows

    def peer(o):
        return lax.rem(x_lo + o // ZS, 2) * ZS + lax.rem(z + o, ZS)

    def origin(o):
        return lax.rem(x_lo + o // ZS, 2) * ZS + lax.rem(z - o + 2 * ZS, ZS)

    def place(at_y, at_x_hi, at_core):
        return (at_y * 2 + at_x_hi) * 2 + at_core

    def first_col(device):
        return lax.rem(device, KVH) * (2 * wide) + (device // KVH) * wide

    def rows_of(block):
        return pl.ds(pl.multiple_of(block * rows, rows), rows)

    def cols(at, n):
        return pl.ds(pl.multiple_of(at, n), n)

    load_hid = pltpu.make_async_copy(hidden, hid_v, load_sem.at[0])
    load_kw = pltpu.make_async_copy(key_weight, kw_v, load_sem.at[1])
    load_vw = pltpu.make_async_copy(value_weight, vw_v, load_sem.at[2])
    load_hid.start()
    load_kw.start()
    load_vw.start()

    barrier = pltpu.get_barrier_semaphore()

    def column_peer(o):
        return place(lax.rem(y + o // 2, ys), x_hi, lax.rem(core + o, 2))

    def column_origin(o):
        return lax.rem(y - o // 2 + ys, ys), lax.rem(core + o, 2)

    def sum_peer(o):
        return {
            "grp": peer(lax.rem(o, group_size)),
            "dp": place(y, lax.rem(x_hi + o // group_size, 2), core),
        }

    each(
        1,
        column,
        lambda o: pl.semaphore_signal(
            barrier, inc=1, device_id={"dp": column_peer(o)}, device_id_type=MESH
        ),
    )
    each(
        1,
        summed_over,
        lambda o: pl.semaphore_signal(
            barrier, inc=1, device_id=sum_peer(o), device_id_type=MESH
        ),
    )

    def q_copy(h, o, to):
        dest = peer(o)
        at = rows_of(me if to else origin(o))
        return pltpu.make_async_remote_copy(
            src_ref=queries.at[:, cols(first_col(dest) + h * HD, HD)],
            dst_ref=q_r.at[h, at, :],
            send_sem=q_send.at[h, o],
            recv_sem=q_recv.at[h, o],
            device_id={"grp": dest},
            device_id_type=MESH,
        )

    def do_copy(h, o, to):
        dest = peer(o)
        at = rows_of(me if to else origin(o))
        return pltpu.make_async_remote_copy(
            src_ref=out_grad.at[:, cols(first_col(dest) + h * HD, HD)],
            dst_ref=do_r.at[h, at, :],
            send_sem=do_send.at[h, o],
            recv_sem=do_recv.at[h, o],
            device_id={"grp": dest},
            device_id_type=MESH,
        )

    def kv_copy(o, to):
        dest = peer(o)
        at = rows_of(me if to else origin(o))
        return pltpu.make_async_remote_copy(
            src_ref=kv_s.at[lax.rem(dest, KVH)],
            dst_ref=kv_r.at[:, at, :],
            send_sem=kv_send.at[o],
            recv_sem=kv_recv.at[o],
            device_id={"grp": dest},
            device_id_type=MESH,
        )

    def hid_copy(o, to):
        dest_y, dest_core = lax.rem(y + o // 2, ys), lax.rem(core + o, 2)
        from_y, from_core = (y, core) if to else column_origin(o)
        return pltpu.make_async_remote_copy(
            src_ref=hid_s.at[dest_y * 2 + dest_core],
            dst_ref=hid_t.at[from_y, :, cols(from_core * rows, rows)],
            send_sem=hid_send.at[o],
            recv_sem=hid_recv.at[o],
            device_id={"dp": column_peer(o)},
            device_id_type=MESH,
        )

    def dq_copy(h, o, to):
        dest = peer(o)
        at = first_col(me if to else origin(o)) + h * HD
        return pltpu.make_async_remote_copy(
            src_ref=dq_g.at[h, rows_of(dest), :],
            dst_ref=grad_query.at[:, cols(at, HD)],
            send_sem=dq_send.at[h, o],
            recv_sem=dq_recv.at[h, o],
            device_id={"grp": dest},
            device_id_type=MESH,
        )

    def dq_stay(h):
        return pltpu.make_async_copy(
            dq_g.at[h, rows_of(me), :],
            grad_query.at[:, cols(first_col(me) + h * HD, HD)],
            dq_own.at[h],
        )

    def dl_copy(dest, source):
        return pltpu.make_async_remote_copy(
            src_ref=dl_s.at[dest],
            dst_ref=dl_r.at[source],
            send_sem=dl_send.at[dest],
            recv_sem=dl_recv.at[source],
            device_id={"grp": dest},
            device_id_type=MESH,
        )

    def dg_copy(o, to):
        dest = peer(o)
        return pltpu.make_async_remote_copy(
            src_ref=dg_s.at[dest],
            dst_ref=dg_r.at[me if to else origin(o)],
            send_sem=dg_send.at[o],
            recv_sem=dg_recv.at[o],
            device_id={"grp": dest},
            device_id_type=MESH,
        )

    def ya_copy(part, k, to):
        at = (y if to else lax.rem(y - k + ys, ys)) * 2 + core
        return pltpu.make_async_remote_copy(
            src_ref=dkv_all.at[y * 2 + core, part],
            dst_ref=dkv_all.at[at, part],
            send_sem=ya_send.at[part, k],
            recv_sem=ya_recv.at[part, k],
            device_id={"dp": place(lax.rem(y + k, ys), x_hi, core)},
            device_id_type=MESH,
        )

    def yc_copy(part, k, to):
        from_y = lax.rem(y - k + ys, ys)
        return pltpu.make_async_remote_copy(
            src_ref=dkv_all.at[from_y * 2 + core, part],
            dst_ref=dkv_all.at[from_y * 2 + (core if to else 1 - core), part],
            send_sem=yc_send.at[part, k],
            recv_sem=yc_recv.at[part, k],
            device_id={"dp": place(y, x_hi, 1 - core)},
            device_id_type=MESH,
        )

    def rs_copy(part, o):
        dest = sum_peer(o)
        at = dest["grp"] * 2 + lax.rem(x_hi + o // group_size, 2)
        return pltpu.make_async_remote_copy(
            src_ref=prod_s.at[part, pl.ds(pl.multiple_of(at * piece, piece), piece), :],
            dst_ref=rs_r.at[part, o],
            send_sem=rs_send.at[part, o],
            recv_sem=rs_recv.at[part, o],
            device_id=dest,
            device_id_type=MESH,
        )

    def own_q(h):
        return pltpu.make_async_copy(
            queries.at[:, cols(first_col(me) + h * HD, HD)],
            q_r.at[h, rows_of(me), :],
            own_sem.at[0, h],
        )

    def own_do(h):
        return pltpu.make_async_copy(
            out_grad.at[:, cols(first_col(me) + h * HD, HD)],
            do_r.at[h, rows_of(me), :],
            own_sem.at[1, h],
        )

    def send_heads(first, last):
        def one(i):
            h = i // (group_size - 1)
            o = lax.rem(i, group_size - 1) + 1
            q_copy(h, o, True).start()
            do_copy(h, o, True).start()

        each(first * (group_size - 1), last * (group_size - 1), one)

    pl.semaphore_wait(barrier, column - 1 + summed_over - 1)

    send_heads(0, 2)
    for h in range(heads):
        own_q(h).start()
        own_do(h).start()

    load_hid.wait()
    load_kw.wait()
    hid_rows = hid_v[...]

    def project(weight, which):
        for g in range(0, KVH, 2):
            both = jnp.dot(
                hid_rows, weight[:, g * HD : (g + 2) * HD], preferred_element_type=FULL
            ).astype(LOW)
            kv_s[g, which] = both[:, :HD]
            kv_s[g + 1, which] = both[:, HD:]

    project(kw_v, 0)
    load_vw.wait()
    project(vw_v, 1)
    each(1, group_size, lambda o: kv_copy(o, True).start())
    send_heads(2, heads)
    kv_r[:, rows_of(me), :] = kv_s[lax.rem(me, KVH)]

    lanes = 4 * piece

    def turn(t):
        turned = hid_v[:, cols(t * lanes, lanes)].T
        g = t // ys
        to_y = lax.rem(t, ys)
        for xh in range(2):
            at = pl.ds(pl.multiple_of((g * 2 + xh) * piece, piece), piece)
            for c in range(2):
                hid_s[to_y * 2 + c, at, :] = turned[(xh * 2 + c) * piece :][:piece]

    each(0, width // lanes, turn)
    each(1, column, lambda o: hid_copy(o, True).start())
    hid_t[y, :, cols(core * rows, rows)] = hid_s[y * 2 + core]

    row_ids = lax.broadcasted_iota(jnp.int32, (1, total), 1)
    begin = jnp.zeros((1, total), jnp.int32)
    for s in range(SLOTS):
        at, size = offsets[0, s], lengths[0, s]
        begin = jnp.where((row_ids >= at) & (row_ids < at + size), at, begin)
    begin_v[...] = begin
    starts = []
    for s in range(SLOTS):
        start = jnp.int32(0)
        for t in range(SLOTS):
            if t < s:
                before = groups[0, t] <= groups[0, s]
            else:
                before = groups[0, t] < groups[0, s]
            if t != s:
                start = start + jnp.where(before, lengths[0, t], 0)
        starts.append(start)

    def source_block(row):
        found = jnp.int32(0)
        for s in range(SLOTS):
            inside = (row >= starts[s]) & (row < starts[s] + lengths[0, s])
            found = found + jnp.where(inside, offsets[0, s] + row - starts[s], 0)
        return found // rows

    sources = [source_block(b * rows) for b in range(group_size)]

    acc[...] = jnp.zeros_like(acc)
    each(1, group_size, lambda o: kv_copy(o, False).wait_recv())
    kt_v[...] = kv_r[0].T

    key_ids = lax.broadcasted_iota(jnp.int32, (HD, QBLK), 0)
    lane_ids = lax.broadcasted_iota(jnp.int32, (HD, QBLK), 1)

    def fold(tile):
        return tile.reshape(HD // 8, 8, QBLK)

    def attend(h, b):
        r0 = b * QBLK
        keys = r0 + QBLK
        tiles = keys // HD
        q_blk = q_r[h, r0 : r0 + QBLK, :]
        do_blk = do_r[h, r0 : r0 + QBLK, :]
        begin_row = begin_v[:, r0 : r0 + QBLK]
        s_v[0:keys, :] = lax.dot_general(
            kv_r[0, 0:keys, :], q_blk, NT, preferred_element_type=FULL
        )
        pg_v[0:keys, :] = lax.dot_general(
            kv_r[1, 0:keys, :], do_blk, NT, preferred_element_type=FULL
        )
        top = jnp.full((8, QBLK), -1e30, FULL)
        for j in range(tiles):
            at = slice(j * HD, (j + 1) * HD)
            seen = key_ids + j * HD >= begin_row
            if j * HD >= r0:
                seen = seen & (key_ids + (j * HD - r0) <= lane_ids)
            tile = jnp.where(seen, s_v[at, :], -1e30)
            s_v[at, :] = tile
            top = jnp.maximum(top, jnp.max(fold(tile), axis=0))
        top = jnp.max(top, axis=0, keepdims=True)
        mass = jnp.zeros((8, QBLK), FULL)
        for j in range(tiles):
            at = slice(j * HD, (j + 1) * HD)
            tile = jnp.exp2((s_v[at, :] - top) * exp_scale)
            s_v[at, :] = tile
            mass = mass + jnp.sum(fold(tile), axis=0)
        inverse = 1.0 / jnp.sum(mass, axis=0, keepdims=True)
        delta = jnp.zeros((8, QBLK), FULL)
        for j in range(tiles):
            at = slice(j * HD, (j + 1) * HD)
            weights = s_v[at, :] * inverse
            low = weights.astype(LOW)
            s_v[at, :] = weights
            wl_v[at, :] = low
            delta = delta + jnp.sum(fold(low.astype(FULL) * pg_v[at, :]), axis=0)
        delta = jnp.sum(delta, axis=0, keepdims=True)
        for j in range(tiles):
            at = slice(j * HD, (j + 1) * HD)
            ds_v[at, :] = (s_v[at, :] * (pg_v[at, :] - delta)).astype(LOW)
        acc[1, 0:keys, :] += jnp.dot(wl_v[0:keys, :], do_blk, preferred_element_type=FULL)
        acc[0, 0:keys, :] += jnp.dot(ds_v[0:keys, :], q_blk, preferred_element_type=FULL)
        grad_t = jnp.dot(kt_v[:, 0:keys], ds_v[0:keys, :], preferred_element_type=FULL)
        grad_rows = (grad_t * inv_root).T.astype(LOW)
        for j in range(per_block):
            dq_s[r0 // rows + j] = grad_rows[j * rows : (j + 1) * rows, :]

    def send_dq(h):
        each(1, group_size, lambda o: dq_copy(h, o, True).start())
        dq_stay(h).start()

    def one_head(h):
        own_q(h).wait()
        own_do(h).wait()

        def arrive(o):
            q_copy(h, o, False).wait_recv()
            do_copy(h, o, False).wait_recv()

        each(1, group_size, arrive)

        @pl.when(h == heads - 1)
        def _():
            each(0, heads // 2, send_dq)

        for b in reversed(range(blocks)):
            attend(h, b)

            @pl.when(h == heads - 1)
            def _():
                for j in range(b * per_block, (b + 1) * per_block):
                    at = slice(j * rows, (j + 1) * rows)
                    dl_s[j, 0] = (acc[0, at, :] * inv_root).astype(LOW)
                    dl_s[j, 1] = acc[1, at, :].astype(LOW)

                    @pl.when(me != j)
                    def _():
                        dl_copy(j, me).start()

        for b in range(group_size):
            dq_g[h, b * rows : (b + 1) * rows, :] = dq_s[sources[b]]

    each(0, heads, one_head)

    for b in range(group_size):
        dg_s[b] = dl_s[sources[b]]
    each(1, group_size, lambda o: dg_copy(o, True).start())
    each(heads // 2, heads, send_dq)

    dl_r[me] = dl_s[me]
    for s in range(group_size):

        @pl.when(me != s)
        def _():
            dl_copy(s, s).wait_recv()

    def merge(received, part, g):
        return (
            received[g, part].astype(FULL) + received[KVH + g, part].astype(FULL)
        ).astype(LOW)

    for part in range(2):
        for g in range(KVH):
            dkv_all[y * 2 + core, part, :, g * HD : (g + 1) * HD] = merge(dl_r, part, g)
        each(1, ys, lambda k: ya_copy(part, k, True).start())
        yc_copy(part, 0, True).start()

    each(1, column, lambda o: hid_copy(o, False).wait_recv())
    for part in range(2):
        for k in range(1, ys):
            ya_copy(part, k, False).wait_recv()
            yc_copy(part, k, True).start()
        for k in range(ys):
            yc_copy(part, k, False).wait_recv()
            from_y = lax.rem(y - k + ys, ys)
            grads = dkv_all[pl.ds(from_y * 2, 2), part].reshape(2 * rows, kvw)
            term = jnp.dot(hid_t[from_y], grads, preferred_element_type=FULL)
            if k > 0:
                term = prod[part] + term
            prod[part] = term
            if k == ys - 1:
                prod_s[part] = term.astype(LOW)
        each(1, summed_over, lambda o: rs_copy(part, o).start())

    dg_r[me] = dg_s[me]
    each(1, group_size, lambda o: dg_copy(o, False).wait_recv())
    dk_rows = jnp.concatenate([merge(dg_r, 0, g) for g in range(KVH)], axis=1)
    dv_rows = jnp.concatenate([merge(dg_r, 1, g) for g in range(KVH)], axis=1)

    def hidden_tile(t):
        at = pl.ds(pl.multiple_of(t * 512, 512), 512)
        tile = lax.dot_general(
            dk_rows, kw_v[at, :], NT, preferred_element_type=FULL
        ) + lax.dot_general(dv_rows, vw_v[at, :], NT, preferred_element_type=FULL)
        gh_v[:, at] = tile.astype(LOW)

    each(0, width // 512, hidden_tile)
    gh_out = pltpu.make_async_copy(gh_v, grad_hidden, gh_sem)
    gh_out.start()

    norm = 1.0 / math.sqrt(total * replica_count)
    own = pl.ds(pl.multiple_of((me * 2 + x_hi) * piece, piece), piece)
    for part, result in ((0, grad_key), (1, grad_value)):
        each(1, summed_over, lambda o: rs_copy(part, o).wait_recv())
        summed = prod[part, own, :]
        for o in range(1, summed_over):
            summed = summed + rs_r[part, o].astype(FULL)
        result[...] = (summed * norm).astype(LOW)

    gh_out.wait()

    def close(o):
        kv_copy(o, True).wait_send()
        dg_copy(o, True).wait_send()
        for h in range(heads):
            q_copy(h, o, True).wait_send()
            do_copy(h, o, True).wait_send()
            dq_copy(h, o, True).wait_send()
            dq_copy(h, o, False).wait_recv()

    each(1, group_size, close)
    each(1, column, lambda o: hid_copy(o, True).wait_send())
    for s in range(group_size):

        @pl.when(me != s)
        def _():
            dl_copy(s, me).wait_send()

    for h in range(heads):
        dq_stay(h).wait()
    for part in range(2):
        each(1, ys, lambda k: ya_copy(part, k, True).wait_send())
        each(0, ys, lambda k: yc_copy(part, k, True).wait_send())
        each(1, summed_over, lambda o: rs_copy(part, o).wait_send())


def hand_over(first, second, third, fourth, *refs):
    sems = refs[4]
    copies = [
        pltpu.make_async_copy(source, refs[i], sems.at[i])
        for i, source in enumerate((first, second, third, fourth))
    ]
    for copy in copies:
        copy.start()
    for copy in copies:
        copy.wait()


def on_device(
    hidden, queries, out_grad, key_weight, value_weight, seq_lengths, seq_group, loader_offsets
):
    group_size = lax.axis_size("grp")
    replica_count = lax.axis_size("dp")
    rows, width = hidden.shape[1:]
    total = rows * group_size
    heads = HQ // group_size
    kvw = KVH * HD
    piece = width // (group_size * replica_count)
    blocks = total // QBLK
    ys = replica_count // 4
    column = 2 * ys
    chunk = width // column
    dma = pltpu.SemaphoreType.DMA
    scratch = [
        pltpu.VMEM((rows, width), LOW),
        pltpu.VMEM((width, kvw), LOW),
        pltpu.VMEM((width, kvw), LOW),
        pltpu.VMEM((heads, total, HD), LOW),
        pltpu.VMEM((heads, total, HD), LOW),
        pltpu.VMEM((KVH, 2, rows, HD), LOW),
        pltpu.VMEM((2, total, HD), LOW),
        pltpu.VMEM((HD, total), LOW),
        pltpu.VMEM((column, chunk, rows), LOW),
        pltpu.VMEM((ys, chunk, 2 * rows), LOW),
        pltpu.VMEM((total, QBLK), FULL),
        pltpu.VMEM((total, QBLK), FULL),
        pltpu.VMEM((total, QBLK), LOW),
        pltpu.VMEM((total, QBLK), LOW),
        pltpu.VMEM((2, total, HD), FULL),
        pltpu.VMEM((group_size, rows, HD), LOW),
        pltpu.VMEM((heads, total, HD), LOW),
        pltpu.VMEM((group_size, 2, rows, HD), LOW),
        pltpu.VMEM((group_size, 2, rows, HD), LOW),
        pltpu.VMEM((group_size, 2, rows, HD), LOW),
        pltpu.VMEM((group_size, 2, rows, HD), LOW),
        pltpu.VMEM((column, 2, rows, kvw), LOW),
        pltpu.VMEM((2, chunk, kvw), FULL),
        pltpu.VMEM((2, chunk, kvw), LOW),
        pltpu.VMEM((2, 2 * group_size, piece, kvw), LOW),
        pltpu.VMEM((rows, width), LOW),
        pltpu.VMEM((1, total), jnp.int32),
        dma((3,)),
        dma((2, heads)),
        dma((heads, group_size)),
        dma((heads, group_size)),
        dma((heads, group_size)),
        dma((heads, group_size)),
        dma((group_size,)),
        dma((group_size,)),
        dma((column,)),
        dma((column,)),
        dma((heads, group_size)),
        dma((heads, group_size)),
        dma((heads,)),
        dma((group_size,)),
        dma((group_size,)),
        dma((group_size,)),
        dma((group_size,)),
        dma((2, ys)),
        dma((2, ys)),
        dma((2, ys)),
        dma((2, ys)),
        dma((2, 2 * group_size)),
        dma((2, 2 * group_size)),
        dma,
    ]
    smem = pl.BlockSpec(memory_space=pltpu.SMEM)
    vmem = pl.BlockSpec(memory_space=pltpu.VMEM)
    anywhere = pl.BlockSpec(memory_space=pl.ANY)

    def kernel(*refs):
        layer_kernel(group_size, replica_count, *refs)

    out_shape = (
        jax.ShapeDtypeStruct((rows, HQ * HD), LOW),
        jax.ShapeDtypeStruct((rows, width), LOW),
        jax.ShapeDtypeStruct((piece, kvw), LOW),
        jax.ShapeDtypeStruct((piece, kvw), LOW),
    )
    results = pl.pallas_call(
        kernel,
        out_shape=out_shape,
        in_specs=[smem, smem, smem] + [anywhere] * 5,
        out_specs=(anywhere, anywhere, vmem, vmem),
        scratch_shapes=scratch,
        compiler_params=pltpu.CompilerParams(
            collective_id=0, has_side_effects=True, vmem_limit_bytes=56 * 1024 * 1024
        ),
        name="layer",
    )(
        seq_lengths,
        seq_group,
        loader_offsets,
        hidden[0],
        queries[0],
        out_grad[0],
        key_weight,
        value_weight,
    )
    grad_query, grad_hidden, grad_key, grad_value = pl.pallas_call(
        hand_over,
        out_shape=out_shape,
        in_specs=[anywhere] * 4,
        out_specs=[anywhere] * 4,
        scratch_shapes=[dma((4,))],
        name="hand_over",
    )(*results)
    return (grad_query[None], grad_hidden[None], grad_key, grad_value)


def solution(mesh):
    placed = (
        P("dp", "grp", None),
        P("dp", "grp", None),
        P("dp", "grp", None),
        P(),
        P(),
        P("dp", None),
        P("dp", None),
        P("dp", None),
    )
    return jax.shard_map(
        on_device,
        mesh=mesh,
        in_specs=placed,
        out_specs=(
            P("dp", "grp", None),
            P("dp", "grp", None),
            P(("grp", "dp"), None),
            P(("grp", "dp"), None),
        ),
        check_vma=False,
    )
```

```python
import math

import jax
import jax.numpy as jnp
from jax import lax
from jax.experimental import pallas as pl
from jax.experimental.pallas import tpu as pltpu
from jax.sharding import PartitionSpec as P

HQ = 32
KVH = 4
HD = 128
SLOTS = 8
QBLK = 256
ZS = 4
PARTS = 4
PCOLS = 2 * KVH * HD // PARTS
LOW = jnp.bfloat16
FULL = jnp.float32
MESH = pl.DeviceIdType.MESH
NT = (((1,), (1,)), ((), ()))


def each(first, last, step):
    def body(i, carry):
        step(i)
        return carry

    lax.fori_loop(first, last, body, 0)


def layer_kernel(
    group_size,
    replica_count,
    lengths,
    groups,
    offsets,
    hidden,
    queries,
    out_grad,
    key_weight,
    value_weight,
    grad_query,
    grad_hidden,
    grad_key,
    grad_value,
    hid_v,
    kw_v,
    vw_v,
    q_r,
    do_r,
    kv_s,
    kv_r,
    kt_v,
    hid_s,
    hid_t,
    s_v,
    pg_v,
    wl_v,
    ds_v,
    acc,
    dq_s,
    dq_g,
    dl_s,
    dl_r,
    dg_s,
    dg_r,
    dkv_all,
    prod,
    prod_s,
    rs_r,
    gh_v,
    begin_v,
    load_sem,
    own_sem,
    q_send,
    q_recv,
    do_send,
    do_recv,
    kv_send,
    kv_recv,
    hid_send,
    hid_recv,
    dq_send,
    dq_recv,
    dq_own,
    dl_send,
    dl_recv,
    dg_send,
    dg_recv,
    ya_send,
    ya_recv,
    yf_send,
    yf_recv,
    yc_send,
    yc_recv,
    rs_send,
    rs_recv,
    gh_sem,
):
    me = lax.axis_index("grp")
    rep = lax.axis_index("dp")
    x_lo, z = me // ZS, lax.rem(me, ZS)
    y, x_hi, core = rep // 4, lax.rem(rep // 2, 2), lax.rem(rep, 2)
    ys = replica_count // 4
    column = 2 * ys
    summed_over = 2 * group_size
    rows = hidden.shape[0]
    width = hidden.shape[1]
    total = rows * group_size
    heads = HQ // group_size
    wide = heads * HD
    kvw = KVH * HD
    piece = width // (group_size * replica_count)
    inv_root = 1.0 / math.sqrt(HD)
    exp_scale = inv_root / math.log(2.0)
    blocks = total // QBLK
    per_block = QBLK // rows

    def peer(o):
        return lax.rem(x_lo + o // ZS, 2) * ZS + lax.rem(z + o, ZS)

    def origin(o):
        return lax.rem(x_lo + o // ZS, 2) * ZS + lax.rem(z - o + 2 * ZS, ZS)

    def place(at_y, at_x_hi, at_core):
        return (at_y * 2 + at_x_hi) * 2 + at_core

    def first_col(device):
        return lax.rem(device, KVH) * (2 * wide) + (device // KVH) * wide

    def rows_of(block):
        return pl.ds(pl.multiple_of(block * rows, rows), rows)

    def cols(at, n):
        return pl.ds(pl.multiple_of(at, n), n)

    load_hid = pltpu.make_async_copy(hidden, hid_v, load_sem.at[0])
    load_kw = pltpu.make_async_copy(key_weight, kw_v, load_sem.at[1])
    load_vw = pltpu.make_async_copy(value_weight, vw_v, load_sem.at[2])
    load_hid.start()
    load_kw.start()
    load_vw.start()

    barrier = pltpu.get_barrier_semaphore()

    def column_peer(o):
        return place(lax.rem(y + o // 2, ys), x_hi, lax.rem(core + o, 2))

    def column_origin(o):
        return lax.rem(y - o // 2 + ys, ys), lax.rem(core + o, 2)

    def sum_peer(o):
        return {
            "grp": peer(lax.rem(o, group_size)),
            "dp": place(y, lax.rem(x_hi + o // group_size, 2), core),
        }

    each(
        1,
        column,
        lambda o: pl.semaphore_signal(
            barrier, inc=1, device_id={"dp": column_peer(o)}, device_id_type=MESH
        ),
    )
    each(
        1,
        summed_over,
        lambda o: pl.semaphore_signal(
            barrier, inc=1, device_id=sum_peer(o), device_id_type=MESH
        ),
    )

    def q_copy(h, o, to):
        dest = peer(o)
        at = rows_of(me if to else origin(o))
        return pltpu.make_async_remote_copy(
            src_ref=queries.at[:, cols(first_col(dest) + h * HD, HD)],
            dst_ref=q_r.at[h, at, :],
            send_sem=q_send.at[h, o],
            recv_sem=q_recv.at[h, o],
            device_id={"grp": dest},
            device_id_type=MESH,
        )

    def do_copy(h, o, to):
        dest = peer(o)
        at = rows_of(me if to else origin(o))
        return pltpu.make_async_remote_copy(
            src_ref=out_grad.at[:, cols(first_col(dest) + h * HD, HD)],
            dst_ref=do_r.at[h, at, :],
            send_sem=do_send.at[h, o],
            recv_sem=do_recv.at[h, o],
            device_id={"grp": dest},
            device_id_type=MESH,
        )

    def kv_copy(o, to):
        dest = peer(o)
        at = rows_of(me if to else origin(o))
        return pltpu.make_async_remote_copy(
            src_ref=kv_s.at[lax.rem(dest, KVH)],
            dst_ref=kv_r.at[:, at, :],
            send_sem=kv_send.at[o],
            recv_sem=kv_recv.at[o],
            device_id={"grp": dest},
            device_id_type=MESH,
        )

    def hid_copy(o, to):
        dest_y, dest_core = lax.rem(y + o // 2, ys), lax.rem(core + o, 2)
        from_y, from_core = (y, core) if to else column_origin(o)
        return pltpu.make_async_remote_copy(
            src_ref=hid_s.at[dest_y * 2 + dest_core],
            dst_ref=hid_t.at[from_y, :, cols(from_core * rows, rows)],
            send_sem=hid_send.at[o],
            recv_sem=hid_recv.at[o],
            device_id={"dp": column_peer(o)},
            device_id_type=MESH,
        )

    def dq_copy(h, o, to):
        dest = peer(o)
        at = first_col(me if to else origin(o)) + h * HD
        return pltpu.make_async_remote_copy(
            src_ref=dq_g.at[h, rows_of(dest), :],
            dst_ref=grad_query.at[:, cols(at, HD)],
            send_sem=dq_send.at[h, o],
            recv_sem=dq_recv.at[h, o],
            device_id={"grp": dest},
            device_id_type=MESH,
        )

    def dq_stay(h):
        return pltpu.make_async_copy(
            dq_g.at[h, rows_of(me), :],
            grad_query.at[:, cols(first_col(me) + h * HD, HD)],
            dq_own.at[h],
        )

    def dl_copy(dest, source):
        return pltpu.make_async_remote_copy(
            src_ref=dl_s.at[dest],
            dst_ref=dl_r.at[source],
            send_sem=dl_send.at[dest],
            recv_sem=dl_recv.at[source],
            device_id={"grp": dest},
            device_id_type=MESH,
        )

    def dg_copy(o, to):
        dest = peer(o)
        return pltpu.make_async_remote_copy(
            src_ref=dg_s.at[dest],
            dst_ref=dg_r.at[me if to else origin(o)],
            send_sem=dg_send.at[o],
            recv_sem=dg_recv.at[o],
            device_id={"grp": dest},
            device_id_type=MESH,
        )

    def ya_copy(part, k, to):
        step = ys - 1 if k else 1
        at = (y if to else lax.rem(y + ys - step, ys)) * 2 + core
        return pltpu.make_async_remote_copy(
            src_ref=dkv_all.at[y * 2 + core, part],
            dst_ref=dkv_all.at[at, part],
            send_sem=ya_send.at[part, k],
            recv_sem=ya_recv.at[part, k],
            device_id={"dp": place(lax.rem(y + step, ys), x_hi, core)},
            device_id_type=MESH,
        )

    def yf_copy(part, k, to):
        step = ys - 1 if k else 1
        come = lax.rem(y + ys - step, ys) * 2 + core
        far = lax.rem(y + 2, ys) * 2 + core
        half = pl.ds(k * (rows // 2), rows // 2)
        return pltpu.make_async_remote_copy(
            src_ref=dkv_all.at[come, part, half],
            dst_ref=dkv_all.at[come if to else far, part, half],
            send_sem=yf_send.at[part, k],
            recv_sem=yf_recv.at[part, k],
            device_id={"dp": place(lax.rem(y + step, ys), x_hi, core)},
            device_id_type=MESH,
        )

    def yc_copy(part, k, to):
        from_y = lax.rem(y + k, ys)
        return pltpu.make_async_remote_copy(
            src_ref=dkv_all.at[from_y * 2 + core, part],
            dst_ref=dkv_all.at[from_y * 2 + (core if to else 1 - core), part],
            send_sem=yc_send.at[part, k],
            recv_sem=yc_recv.at[part, k],
            device_id={"dp": place(y, x_hi, 1 - core)},
            device_id_type=MESH,
        )

    def rs_copy(part, o):
        dest = sum_peer(o)
        at = dest["grp"] * 2 + lax.rem(x_hi + o // group_size, 2)
        return pltpu.make_async_remote_copy(
            src_ref=prod_s.at[part, pl.ds(pl.multiple_of(at * piece, piece), piece), :],
            dst_ref=rs_r.at[part, o],
            send_sem=rs_send.at[part, o],
            recv_sem=rs_recv.at[part, o],
            device_id=dest,
            device_id_type=MESH,
        )

    def own_q(h):
        return pltpu.make_async_copy(
            queries.at[:, cols(first_col(me) + h * HD, HD)],
            q_r.at[h, rows_of(me), :],
            own_sem.at[0, h],
        )

    def own_do(h):
        return pltpu.make_async_copy(
            out_grad.at[:, cols(first_col(me) + h * HD, HD)],
            do_r.at[h, rows_of(me), :],
            own_sem.at[1, h],
        )

    def send_heads(first, last):
        def one(i):
            h = i // (group_size - 1)
            o = lax.rem(i, group_size - 1) + 1
            q_copy(h, o, True).start()
            do_copy(h, o, True).start()

        each(first * (group_size - 1), last * (group_size - 1), one)

    load_hid.wait()
    load_kw.wait()
    hid_rows = hid_v[...]

    def project(weight, which):
        for g in range(0, KVH, 2):
            both = jnp.dot(
                hid_rows, weight[:, g * HD : (g + 2) * HD], preferred_element_type=FULL
            ).astype(LOW)
            kv_s[g, which] = both[:, :HD]
            kv_s[g + 1, which] = both[:, HD:]

    project(kw_v, 0)
    load_vw.wait()
    project(vw_v, 1)

    pl.semaphore_wait(barrier, column - 1 + summed_over - 1)

    each(1, group_size, lambda o: kv_copy(o, True).start())
    send_heads(0, heads)
    for h in range(heads):
        own_q(h).start()
        own_do(h).start()
    kv_r[:, rows_of(me), :] = kv_s[lax.rem(me, KVH)]

    lanes = 4 * piece

    def turn(t):
        turned = hid_v[:, cols(t * lanes, lanes)].T
        g = t // ys
        to_y = lax.rem(t, ys)
        for xh in range(2):
            at = pl.ds(pl.multiple_of((g * 2 + xh) * piece, piece), piece)
            for c in range(2):
                hid_s[to_y * 2 + c, at, :] = turned[(xh * 2 + c) * piece :][:piece]

    each(0, width // lanes, turn)
    each(1, column, lambda o: hid_copy(o, True).start())
    hid_t[y, :, cols(core * rows, rows)] = hid_s[y * 2 + core]

    row_ids = lax.broadcasted_iota(jnp.int32, (1, total), 1)
    begin = jnp.zeros((1, total), jnp.int32)
    for s in range(SLOTS):
        at, size = offsets[0, s], lengths[0, s]
        begin = jnp.where((row_ids >= at) & (row_ids < at + size), at, begin)
    begin_v[...] = begin
    starts = []
    for s in range(SLOTS):
        start = jnp.int32(0)
        for t in range(SLOTS):
            if t < s:
                before = groups[0, t] <= groups[0, s]
            else:
                before = groups[0, t] < groups[0, s]
            if t != s:
                start = start + jnp.where(before, lengths[0, t], 0)
        starts.append(start)

    def source_block(row):
        found = jnp.int32(0)
        for s in range(SLOTS):
            inside = (row >= starts[s]) & (row < starts[s] + lengths[0, s])
            found = found + jnp.where(inside, offsets[0, s] + row - starts[s], 0)
        return found // rows

    sources = [source_block(b * rows) for b in range(group_size)]

    acc[...] = jnp.zeros_like(acc)
    each(1, group_size, lambda o: kv_copy(o, False).wait_recv())
    kt_v[...] = kv_r[0].T

    key_ids = lax.broadcasted_iota(jnp.int32, (HD, QBLK), 0)
    lane_ids = lax.broadcasted_iota(jnp.int32, (HD, QBLK), 1)

    def fold(tile):
        return tile.reshape(HD // 8, 8, QBLK)

    def attend(h, b):
        r0 = b * QBLK
        keys = r0 + QBLK
        tiles = keys // HD
        q_blk = q_r[h, r0 : r0 + QBLK, :]
        do_blk = do_r[h, r0 : r0 + QBLK, :]
        begin_row = begin_v[:, r0 : r0 + QBLK]
        s_v[0:keys, :] = lax.dot_general(
            kv_r[0, 0:keys, :], q_blk, NT, preferred_element_type=FULL
        )
        pg_v[0:keys, :] = lax.dot_general(
            kv_r[1, 0:keys, :], do_blk, NT, preferred_element_type=FULL
        )
        top = jnp.full((8, QBLK), -1e30, FULL)
        for j in range(tiles):
            at = slice(j * HD, (j + 1) * HD)
            seen = key_ids + j * HD >= begin_row
            if j * HD >= r0:
                seen = seen & (key_ids + (j * HD - r0) <= lane_ids)
            tile = jnp.where(seen, s_v[at, :], -1e30)
            s_v[at, :] = tile
            top = jnp.maximum(top, jnp.max(fold(tile), axis=0))
        top = jnp.max(top, axis=0, keepdims=True)
        mass = jnp.zeros((8, QBLK), FULL)
        for j in range(tiles):
            at = slice(j * HD, (j + 1) * HD)
            tile = jnp.exp2((s_v[at, :] - top) * exp_scale)
            s_v[at, :] = tile
            mass = mass + jnp.sum(fold(tile), axis=0)
        inverse = 1.0 / jnp.sum(mass, axis=0, keepdims=True)
        delta = jnp.zeros((8, QBLK), FULL)
        for j in range(tiles):
            at = slice(j * HD, (j + 1) * HD)
            weights = s_v[at, :] * inverse
            low = weights.astype(LOW)
            s_v[at, :] = weights
            wl_v[at, :] = low
            delta = delta + jnp.sum(fold(low.astype(FULL) * pg_v[at, :]), axis=0)
        delta = jnp.sum(delta, axis=0, keepdims=True)
        for j in range(tiles):
            at = slice(j * HD, (j + 1) * HD)
            ds_v[at, :] = (s_v[at, :] * (pg_v[at, :] - delta)).astype(LOW)
        acc[1, 0:keys, :] += jnp.dot(wl_v[0:keys, :], do_blk, preferred_element_type=FULL)
        acc[0, 0:keys, :] += jnp.dot(ds_v[0:keys, :], q_blk, preferred_element_type=FULL)
        grad_t = jnp.dot(kt_v[:, 0:keys], ds_v[0:keys, :], preferred_element_type=FULL)
        grad_rows = (grad_t * inv_root).T.astype(LOW)
        for j in range(per_block):
            dq_s[r0 // rows + j] = grad_rows[j * rows : (j + 1) * rows, :]

    def send_dq(h):
        each(1, group_size, lambda o: dq_copy(h, o, True).start())
        dq_stay(h).start()

    def one_head(h):
        own_q(h).wait()
        own_do(h).wait()

        def arrive(o):
            q_copy(h, o, False).wait_recv()
            do_copy(h, o, False).wait_recv()

        each(1, group_size, arrive)

        for b in reversed(range(blocks)):
            attend(h, b)

            @pl.when(h == heads - 1)
            def _():
                for j in range(b * per_block, (b + 1) * per_block):
                    at = slice(j * rows, (j + 1) * rows)
                    dl_s[j, 0] = (acc[0, at, :] * inv_root).astype(LOW)
                    dl_s[j, 1] = acc[1, at, :].astype(LOW)

                    @pl.when(me != j)
                    def _():
                        dl_copy(j, me).start()

        for b in range(group_size):
            dq_g[h, b * rows : (b + 1) * rows, :] = dq_s[sources[b]]

    each(0, heads, one_head)

    for b in range(group_size):
        dg_s[b] = dl_s[sources[b]]
    each(1, group_size, lambda o: dg_copy(o, True).start())
    each(0, heads, send_dq)

    dl_r[me] = dl_s[me]
    for s in range(group_size):

        @pl.when(me != s)
        def _():
            dl_copy(s, s).wait_recv()

    def merge(received, part, g):
        return (
            received[g, part].astype(FULL) + received[KVH + g, part].astype(FULL)
        ).astype(LOW)

    for part in range(PARTS):
        for i in range(PCOLS // HD):
            dkv_all[y * 2 + core, part, :, i * HD : (i + 1) * HD] = merge(
                dl_r, part * PCOLS // kvw, (part * PCOLS % kvw) // HD + i
            )
        for k in range(2):
            ya_copy(part, k, True).start()
        yc_copy(part, 0, True).start()

    def close_early(o):
        kv_copy(o, True).wait_send()
        for h in range(heads):
            q_copy(h, o, True).wait_send()
            do_copy(h, o, True).wait_send()

    each(1, group_size, close_early)

    each(1, column, lambda o: hid_copy(o, False).wait_recv())
    def pass_on(part):
        for k in range(2):
            ya_copy(part, k, False).wait_recv()
            yf_copy(part, k, True).start()
            yc_copy(part, 1 if k else ys - 1, True).start()

    def hand_far(part):
        for k in range(2):
            yf_copy(part, k, False).wait_recv()
        yc_copy(part, 2, True).start()

    def multiply(part):
        for k in (0, 1, ys - 1, 2):
            yc_copy(part, k, False).wait_recv()
            from_y = lax.rem(y + k, ys)
            grads = dkv_all[pl.ds(from_y * 2, 2), part].reshape(2 * rows, PCOLS)
            term = jnp.dot(hid_t[from_y], grads, preferred_element_type=FULL)
            if k > 0:
                term = prod[part] + term
            prod[part] = term
            if k == 2:
                prod_s[part] = term.astype(LOW)
        each(1, summed_over, lambda o: rs_copy(part, o).start())

    pass_on(0)
    for part in range(PARTS):
        if part + 1 < PARTS:
            pass_on(part + 1)
        hand_far(part)
        multiply(part)

    dg_r[me] = dg_s[me]
    each(1, group_size, lambda o: dg_copy(o, False).wait_recv())
    dk_rows = jnp.concatenate([merge(dg_r, 0, g) for g in range(KVH)], axis=1)
    dv_rows = jnp.concatenate([merge(dg_r, 1, g) for g in range(KVH)], axis=1)

    def hidden_tile(t):
        at = pl.ds(pl.multiple_of(t * 512, 512), 512)
        tile = lax.dot_general(
            dk_rows, kw_v[at, :], NT, preferred_element_type=FULL
        ) + lax.dot_general(dv_rows, vw_v[at, :], NT, preferred_element_type=FULL)
        gh_v[:, at] = tile.astype(LOW)

    each(0, width // 512, hidden_tile)
    gh_out = pltpu.make_async_copy(gh_v, grad_hidden, gh_sem)
    gh_out.start()

    def close(o):
        dg_copy(o, True).wait_send()
        for h in range(heads):
            dq_copy(h, o, True).wait_send()
            dq_copy(h, o, False).wait_recv()

    each(1, group_size, close)
    each(1, column, lambda o: hid_copy(o, True).wait_send())
    for s in range(group_size):

        @pl.when(me != s)
        def _():
            dl_copy(s, me).wait_send()

    for h in range(heads):
        dq_stay(h).wait()
    for part in range(PARTS):
        for k in range(2):
            ya_copy(part, k, True).wait_send()
            yf_copy(part, k, True).wait_send()
        for k in range(ys):
            yc_copy(part, k, True).wait_send()

    norm = 1.0 / math.sqrt(total * replica_count)
    own = pl.ds(pl.multiple_of((me * 2 + x_hi) * piece, piece), piece)
    for part in range(PARTS):
        each(1, summed_over, lambda o: rs_copy(part, o).wait_recv())
        summed = prod[part, own, :]
        for o in range(1, summed_over):
            summed = summed + rs_r[part, o].astype(FULL)
        result = grad_value if part * PCOLS >= kvw else grad_key
        at = part * PCOLS % kvw
        result[:, at : at + PCOLS] = (summed * norm).astype(LOW)

    gh_out.wait()
    for part in range(PARTS):
        each(1, summed_over, lambda o: rs_copy(part, o).wait_send())


def hand_over(*refs):
    sources, results = refs[0:4], refs[4:8]
    held, sems = refs[8:12], refs[12]
    steps = []
    for i, (source, result, slot) in enumerate(zip(sources, results, held)):
        parts = 4 if i < 2 else 1
        size = source.shape[0] // parts
        for j in range(parts):
            at = pl.ds(j * size, size)
            steps.append(
                (
                    pltpu.make_async_copy(source.at[at], slot.at[at], sems.at[0, i, j]),
                    pltpu.make_async_copy(slot.at[at], result.at[at], sems.at[1, i, j]),
                )
            )
    for load, _ in steps:
        load.start()
    for load, store in steps:
        load.wait()
        store.start()
    for _, store in steps:
        store.wait()


def on_device(
    hidden, queries, out_grad, key_weight, value_weight, seq_lengths, seq_group, loader_offsets
):
    group_size = lax.axis_size("grp")
    replica_count = lax.axis_size("dp")
    rows, width = hidden.shape[1:]
    total = rows * group_size
    heads = HQ // group_size
    kvw = KVH * HD
    piece = width // (group_size * replica_count)
    blocks = total // QBLK
    ys = replica_count // 4
    column = 2 * ys
    chunk = width // column
    dma = pltpu.SemaphoreType.DMA
    scratch = [
        pltpu.VMEM((rows, width), LOW),
        pltpu.VMEM((width, kvw), LOW),
        pltpu.VMEM((width, kvw), LOW),
        pltpu.VMEM((heads, total, HD), LOW),
        pltpu.VMEM((heads, total, HD), LOW),
        pltpu.VMEM((KVH, 2, rows, HD), LOW),
        pltpu.VMEM((2, total, HD), LOW),
        pltpu.VMEM((HD, total), LOW),
        pltpu.VMEM((column, chunk, rows), LOW),
        pltpu.VMEM((ys, chunk, 2 * rows), LOW),
        pltpu.VMEM((total, QBLK), FULL),
        pltpu.VMEM((total, QBLK), FULL),
        pltpu.VMEM((total, QBLK), LOW),
        pltpu.VMEM((total, QBLK), LOW),
        pltpu.VMEM((2, total, HD), FULL),
        pltpu.VMEM((group_size, rows, HD), LOW),
        pltpu.VMEM((heads, total, HD), LOW),
        pltpu.VMEM((group_size, 2, rows, HD), LOW),
        pltpu.VMEM((group_size, 2, rows, HD), LOW),
        pltpu.VMEM((group_size, 2, rows, HD), LOW),
        pltpu.VMEM((group_size, 2, rows, HD), LOW),
        pltpu.VMEM((column, PARTS, rows, PCOLS), LOW),
        pltpu.VMEM((PARTS, chunk, PCOLS), FULL),
        pltpu.VMEM((PARTS, chunk, PCOLS), LOW),
        pltpu.VMEM((PARTS, 2 * group_size, piece, PCOLS), LOW),
        pltpu.VMEM((rows, width), LOW),
        pltpu.VMEM((1, total), jnp.int32),
        dma((3,)),
        dma((2, heads)),
        dma((heads, group_size)),
        dma((heads, group_size)),
        dma((heads, group_size)),
        dma((heads, group_size)),
        dma((group_size,)),
        dma((group_size,)),
        dma((column,)),
        dma((column,)),
        dma((heads, group_size)),
        dma((heads, group_size)),
        dma((heads,)),
        dma((group_size,)),
        dma((group_size,)),
        dma((group_size,)),
        dma((group_size,)),
        dma((PARTS, 2)),
        dma((PARTS, 2)),
        dma((PARTS, 2)),
        dma((PARTS, 2)),
        dma((PARTS, ys)),
        dma((PARTS, ys)),
        dma((PARTS, 2 * group_size)),
        dma((PARTS, 2 * group_size)),
        dma,
    ]
    smem = pl.BlockSpec(memory_space=pltpu.SMEM)
    vmem = pl.BlockSpec(memory_space=pltpu.VMEM)
    anywhere = pl.BlockSpec(memory_space=pl.ANY)

    def kernel(*refs):
        layer_kernel(group_size, replica_count, *refs)

    out_shape = (
        jax.ShapeDtypeStruct((rows, HQ * HD), LOW),
        jax.ShapeDtypeStruct((rows, width), LOW),
        jax.ShapeDtypeStruct((piece, kvw), LOW),
        jax.ShapeDtypeStruct((piece, kvw), LOW),
    )
    results = pl.pallas_call(
        kernel,
        out_shape=out_shape,
        in_specs=[smem, smem, smem] + [anywhere] * 5,
        out_specs=(anywhere, anywhere, vmem, vmem),
        scratch_shapes=scratch,
        compiler_params=pltpu.CompilerParams(
            collective_id=0, has_side_effects=True, vmem_limit_bytes=56 * 1024 * 1024
        ),
        name="layer",
    )(
        seq_lengths,
        seq_group,
        loader_offsets,
        hidden[0],
        queries[0],
        out_grad[0],
        key_weight,
        value_weight,
    )
    grad_query, grad_hidden, grad_key, grad_value = pl.pallas_call(
        hand_over,
        out_shape=out_shape,
        in_specs=[anywhere] * 4,
        out_specs=[anywhere] * 4,
        scratch_shapes=[pltpu.VMEM(shape.shape, LOW) for shape in out_shape] + [dma((2, 4, 4))],
        name="hand_over",
    )(*results)
    return (grad_query[None], grad_hidden[None], grad_key, grad_value)


def solution(mesh):
    placed = (
        P("dp", "grp", None),
        P("dp", "grp", None),
        P("dp", "grp", None),
        P(),
        P(),
        P("dp", None),
        P("dp", None),
        P("dp", None),
    )
    return jax.shard_map(
        on_device,
        mesh=mesh,
        in_specs=placed,
        out_specs=(
            P("dp", "grp", None),
            P("dp", "grp", None),
            P(("grp", "dp"), None),
            P(("grp", "dp"), None),
        ),
        check_vma=False,
    )
```

```python
import math

import jax
import jax.numpy as jnp
from jax import lax
from jax.experimental import pallas as pl
from jax.experimental.pallas import tpu as pltpu
from jax.sharding import PartitionSpec as P

HQ = 32
KVH = 4
HD = 128
SLOTS = 8
QBLK = 256
ZS = 4
PARTS = 4
PCOLS = 2 * KVH * HD // PARTS
LOW = jnp.bfloat16
FULL = jnp.float32
MESH = pl.DeviceIdType.MESH
NT = (((1,), (1,)), ((), ()))


def each(first, last, step):
    def body(i, carry):
        step(i)
        return carry

    lax.fori_loop(first, last, body, 0)


def layer_kernel(
    group_size,
    replica_count,
    lengths,
    groups,
    offsets,
    hidden,
    queries,
    out_grad,
    key_weight,
    value_weight,
    grad_query,
    grad_hidden,
    grad_key,
    grad_value,
    hid_v,
    kw_v,
    vw_v,
    qd_r,
    kv_s,
    kv_r,
    kt_v,
    hid_s,
    hid_t,
    s_v,
    pg_v,
    wl_v,
    ds_v,
    acc,
    dq_s,
    dq_g,
    dl_s,
    dl_r,
    dg_s,
    dg_r,
    dkv_all,
    prod,
    prod_s,
    rs_r,
    gh_v,
    begin_v,
    load_sem,
    in_send,
    in_recv,
    kv_send,
    kv_recv,
    hid_send,
    hid_recv,
    dq_send,
    dq_recv,
    dq_own,
    dl_send,
    dl_recv,
    dg_send,
    dg_recv,
    ya_send,
    ya_recv,
    yf_send,
    yf_recv,
    yc_send,
    yc_recv,
    rs_send,
    rs_recv,
    gh_sem,
):
    me = lax.axis_index("grp")
    rep = lax.axis_index("dp")
    x_lo, z = me // ZS, lax.rem(me, ZS)
    y, x_hi, core = rep // 4, lax.rem(rep // 2, 2), lax.rem(rep, 2)
    ys = replica_count // 4
    column = 2 * ys
    summed_over = 2 * group_size
    rows = hidden.shape[0]
    width = hidden.shape[1]
    total = rows * group_size
    heads = HQ // group_size
    wide = heads * HD
    kvw = KVH * HD
    piece = width // (group_size * replica_count)
    inv_root = 1.0 / math.sqrt(HD)
    exp_scale = inv_root / math.log(2.0)
    blocks = total // QBLK
    per_block = QBLK // rows

    def peer(o):
        return lax.rem(x_lo + o // ZS, 2) * ZS + lax.rem(z + o, ZS)

    def origin(o):
        return lax.rem(x_lo + o // ZS, 2) * ZS + lax.rem(z - o + 2 * ZS, ZS)

    def place(at_y, at_x_hi, at_core):
        return (at_y * 2 + at_x_hi) * 2 + at_core

    def first_col(device):
        return lax.rem(device, KVH) * (2 * wide) + (device // KVH) * wide

    def rows_of(block):
        return pl.ds(pl.multiple_of(block * rows, rows), rows)

    def cols(at, n):
        return pl.ds(pl.multiple_of(at, n), n)

    load_hid = pltpu.make_async_copy(hidden, hid_v, load_sem.at[0])
    load_kw = pltpu.make_async_copy(key_weight, kw_v, load_sem.at[1])
    load_vw = pltpu.make_async_copy(value_weight, vw_v, load_sem.at[2])
    load_hid.start()
    load_kw.start()
    load_vw.start()

    barrier = pltpu.get_barrier_semaphore()

    def column_peer(o):
        return place(lax.rem(y + o // 2, ys), x_hi, lax.rem(core + o, 2))

    def column_origin(o):
        return lax.rem(y - o // 2 + ys, ys), lax.rem(core + o, 2)

    def sum_peer(o):
        return {
            "grp": peer(lax.rem(o, group_size)),
            "dp": place(y, lax.rem(x_hi + o // group_size, 2), core),
        }

    each(
        1,
        column,
        lambda o: pl.semaphore_signal(
            barrier, inc=1, device_id={"dp": column_peer(o)}, device_id_type=MESH
        ),
    )
    each(
        1,
        summed_over,
        lambda o: pl.semaphore_signal(
            barrier, inc=1, device_id=sum_peer(o), device_id_type=MESH
        ),
    )

    def q_copy(h, o, to):
        dest = peer(o)
        at = rows_of(me if to else origin(o))
        return pltpu.make_async_remote_copy(
            src_ref=queries.at[:, cols(first_col(dest) + h * HD, HD)],
            dst_ref=qd_r.at[h, 0, at, :],
            send_sem=in_send,
            recv_sem=in_recv.at[h],
            device_id={"grp": dest},
            device_id_type=MESH,
        )

    def do_copy(h, o, to):
        dest = peer(o)
        at = rows_of(me if to else origin(o))
        return pltpu.make_async_remote_copy(
            src_ref=out_grad.at[:, cols(first_col(dest) + h * HD, HD)],
            dst_ref=qd_r.at[h, 1, at, :],
            send_sem=in_send,
            recv_sem=in_recv.at[h],
            device_id={"grp": dest},
            device_id_type=MESH,
        )

    def kv_copy(o, to):
        dest = peer(o)
        at = rows_of(me if to else origin(o))
        return pltpu.make_async_remote_copy(
            src_ref=kv_s.at[lax.rem(dest, KVH)],
            dst_ref=kv_r.at[:, at, :],
            send_sem=kv_send,
            recv_sem=kv_recv,
            device_id={"grp": dest},
            device_id_type=MESH,
        )

    def hid_copy(o, to):
        dest_y, dest_core = lax.rem(y + o // 2, ys), lax.rem(core + o, 2)
        from_y, from_core = (y, core) if to else column_origin(o)
        return pltpu.make_async_remote_copy(
            src_ref=hid_s.at[dest_y * 2 + dest_core],
            dst_ref=hid_t.at[from_y, :, cols(from_core * rows, rows)],
            send_sem=hid_send,
            recv_sem=hid_recv,
            device_id={"dp": column_peer(o)},
            device_id_type=MESH,
        )

    def dq_copy(h, o, to):
        dest = peer(o)
        at = first_col(me if to else origin(o)) + h * HD
        return pltpu.make_async_remote_copy(
            src_ref=dq_g.at[h, rows_of(dest), :],
            dst_ref=grad_query.at[:, cols(at, HD)],
            send_sem=dq_send,
            recv_sem=dq_recv,
            device_id={"grp": dest},
            device_id_type=MESH,
        )

    def dq_stay(h):
        return pltpu.make_async_copy(
            dq_g.at[h, rows_of(me), :],
            grad_query.at[:, cols(first_col(me) + h * HD, HD)],
            dq_own,
        )

    def dl_copy(dest, source):
        return pltpu.make_async_remote_copy(
            src_ref=dl_s.at[dest],
            dst_ref=dl_r.at[source],
            send_sem=dl_send,
            recv_sem=dl_recv,
            device_id={"grp": dest},
            device_id_type=MESH,
        )

    def dg_copy(o, to):
        dest = peer(o)
        return pltpu.make_async_remote_copy(
            src_ref=dg_s.at[dest],
            dst_ref=dg_r.at[me if to else origin(o)],
            send_sem=dg_send,
            recv_sem=dg_recv,
            device_id={"grp": dest},
            device_id_type=MESH,
        )

    def ya_copy(part, k, to):
        step = ys - 1 if k else 1
        at = (y if to else lax.rem(y + ys - step, ys)) * 2 + core
        return pltpu.make_async_remote_copy(
            src_ref=dkv_all.at[y * 2 + core, part],
            dst_ref=dkv_all.at[at, part],
            send_sem=ya_send,
            recv_sem=ya_recv.at[part, k],
            device_id={"dp": place(lax.rem(y + step, ys), x_hi, core)},
            device_id_type=MESH,
        )

    def yf_copy(part, k, to):
        step = ys - 1 if k else 1
        come = lax.rem(y + ys - step, ys) * 2 + core
        far = lax.rem(y + 2, ys) * 2 + core
        half = pl.ds(k * (rows // 2), rows // 2)
        return pltpu.make_async_remote_copy(
            src_ref=dkv_all.at[come, part, half],
            dst_ref=dkv_all.at[come if to else far, part, half],
            send_sem=yf_send,
            recv_sem=yf_recv.at[part],
            device_id={"dp": place(lax.rem(y + step, ys), x_hi, core)},
            device_id_type=MESH,
        )

    def yc_copy(part, k, to):
        from_y = lax.rem(y + k, ys)
        return pltpu.make_async_remote_copy(
            src_ref=dkv_all.at[from_y * 2 + core, part],
            dst_ref=dkv_all.at[from_y * 2 + (core if to else 1 - core), part],
            send_sem=yc_send,
            recv_sem=yc_recv.at[part, k],
            device_id={"dp": place(y, x_hi, 1 - core)},
            device_id_type=MESH,
        )

    def rs_copy(part, o):
        dest = sum_peer(o)
        at = dest["grp"] * 2 + lax.rem(x_hi + o // group_size, 2)
        return pltpu.make_async_remote_copy(
            src_ref=prod_s.at[part, pl.ds(pl.multiple_of(at * piece, piece), piece), :],
            dst_ref=rs_r.at[part, o],
            send_sem=rs_send,
            recv_sem=rs_recv.at[part],
            device_id=dest,
            device_id_type=MESH,
        )

    def settle(ref, sem):
        pltpu.make_async_copy(ref, ref, sem).wait()

    others = total - rows
    seven = pl.ds(0, group_size - 1)

    def own_q(h):
        return pltpu.make_async_copy(
            queries.at[:, cols(first_col(me) + h * HD, HD)],
            qd_r.at[h, 0, rows_of(me), :],
            in_recv.at[h],
        )

    def own_do(h):
        return pltpu.make_async_copy(
            out_grad.at[:, cols(first_col(me) + h * HD, HD)],
            qd_r.at[h, 1, rows_of(me), :],
            in_recv.at[h],
        )

    def send_heads(first, last):
        def one(i):
            h = i // (group_size - 1)
            o = lax.rem(i, group_size - 1) + 1
            q_copy(h, o, True).start()
            do_copy(h, o, True).start()

        each(first * (group_size - 1), last * (group_size - 1), one)

    load_hid.wait()
    load_kw.wait()
    hid_rows = hid_v[...]

    def project(weight, which):
        for g in range(0, KVH, 2):
            both = jnp.dot(
                hid_rows, weight[:, g * HD : (g + 2) * HD], preferred_element_type=FULL
            ).astype(LOW)
            kv_s[g, which] = both[:, :HD]
            kv_s[g + 1, which] = both[:, HD:]

    project(kw_v, 0)
    load_vw.wait()
    project(vw_v, 1)

    pl.semaphore_wait(barrier, column - 1 + summed_over - 1)

    each(1, group_size, lambda o: kv_copy(o, True).start())
    send_heads(0, heads)
    for h in range(heads):
        own_q(h).start()
        own_do(h).start()
    kv_r[:, rows_of(me), :] = kv_s[lax.rem(me, KVH)]

    lanes = 4 * piece

    def turn(t):
        turned = hid_v[:, cols(t * lanes, lanes)].T
        g = t // ys
        to_y = lax.rem(t, ys)
        for xh in range(2):
            at = pl.ds(pl.multiple_of((g * 2 + xh) * piece, piece), piece)
            for c in range(2):
                hid_s[to_y * 2 + c, at, :] = turned[(xh * 2 + c) * piece :][:piece]

    each(0, width // lanes, turn)
    each(1, column, lambda o: hid_copy(o, True).start())
    hid_t[y, :, cols(core * rows, rows)] = hid_s[y * 2 + core]

    row_ids = lax.broadcasted_iota(jnp.int32, (1, total), 1)
    begin = jnp.zeros((1, total), jnp.int32)
    for s in range(SLOTS):
        at, size = offsets[0, s], lengths[0, s]
        begin = jnp.where((row_ids >= at) & (row_ids < at + size), at, begin)
    begin_v[...] = begin
    starts = []
    for s in range(SLOTS):
        start = jnp.int32(0)
        for t in range(SLOTS):
            if t < s:
                before = groups[0, t] <= groups[0, s]
            else:
                before = groups[0, t] < groups[0, s]
            if t != s:
                start = start + jnp.where(before, lengths[0, t], 0)
        starts.append(start)

    def source_block(row):
        found = jnp.int32(0)
        for s in range(SLOTS):
            inside = (row >= starts[s]) & (row < starts[s] + lengths[0, s])
            found = found + jnp.where(inside, offsets[0, s] + row - starts[s], 0)
        return found // rows

    sources = [source_block(b * rows) for b in range(group_size)]

    acc[...] = jnp.zeros_like(acc)
    settle(kv_r.at[:, pl.ds(0, others), :], kv_recv)
    kt_v[...] = kv_r[0].T

    key_ids = lax.broadcasted_iota(jnp.int32, (HD, QBLK), 0)
    lane_ids = lax.broadcasted_iota(jnp.int32, (HD, QBLK), 1)

    def fold(tile):
        return tile.reshape(HD // 8, 8, QBLK)

    def attend(h, b):
        r0 = b * QBLK
        keys = r0 + QBLK
        tiles = keys // HD
        q_blk = qd_r[h, 0, r0 : r0 + QBLK, :]
        do_blk = qd_r[h, 1, r0 : r0 + QBLK, :]
        begin_row = begin_v[:, r0 : r0 + QBLK]
        s_v[0:keys, :] = lax.dot_general(
            kv_r[0, 0:keys, :], q_blk, NT, preferred_element_type=FULL
        )
        pg_v[0:keys, :] = lax.dot_general(
            kv_r[1, 0:keys, :], do_blk, NT, preferred_element_type=FULL
        )
        top = jnp.full((8, QBLK), -1e30, FULL)
        for j in range(tiles):
            at = slice(j * HD, (j + 1) * HD)
            seen = key_ids + j * HD >= begin_row
            if j * HD >= r0:
                seen = seen & (key_ids + (j * HD - r0) <= lane_ids)
            tile = jnp.where(seen, s_v[at, :], -1e30)
            s_v[at, :] = tile
            top = jnp.maximum(top, jnp.max(fold(tile), axis=0))
        top = jnp.max(top, axis=0, keepdims=True)
        mass = jnp.zeros((8, QBLK), FULL)
        for j in range(tiles):
            at = slice(j * HD, (j + 1) * HD)
            tile = jnp.exp2((s_v[at, :] - top) * exp_scale)
            s_v[at, :] = tile
            mass = mass + jnp.sum(fold(tile), axis=0)
        inverse = 1.0 / jnp.sum(mass, axis=0, keepdims=True)
        delta = jnp.zeros((8, QBLK), FULL)
        for j in range(tiles):
            at = slice(j * HD, (j + 1) * HD)
            weights = s_v[at, :] * inverse
            low = weights.astype(LOW)
            s_v[at, :] = weights
            wl_v[at, :] = low
            delta = delta + jnp.sum(fold(low.astype(FULL) * pg_v[at, :]), axis=0)
        delta = jnp.sum(delta, axis=0, keepdims=True)
        for j in range(tiles):
            at = slice(j * HD, (j + 1) * HD)
            ds_v[at, :] = (s_v[at, :] * (pg_v[at, :] - delta)).astype(LOW)
        acc[1, 0:keys, :] += jnp.dot(wl_v[0:keys, :], do_blk, preferred_element_type=FULL)
        acc[0, 0:keys, :] += jnp.dot(ds_v[0:keys, :], q_blk, preferred_element_type=FULL)
        grad_t = jnp.dot(kt_v[:, 0:keys], ds_v[0:keys, :], preferred_element_type=FULL)
        grad_rows = (grad_t * inv_root).T.astype(LOW)
        for j in range(per_block):
            dq_s[r0 // rows + j] = grad_rows[j * rows : (j + 1) * rows, :]

    def send_dq(h):
        each(1, group_size, lambda o: dq_copy(h, o, True).start())
        dq_stay(h).start()

    def one_head(h):
        settle(qd_r.at[h], in_recv.at[h])

        for b in reversed(range(blocks)):
            attend(h, b)

            @pl.when(h == heads - 1)
            def _():
                for j in range(b * per_block, (b + 1) * per_block):
                    at = slice(j * rows, (j + 1) * rows)
                    dl_s[j, 0] = (acc[0, at, :] * inv_root).astype(LOW)
                    dl_s[j, 1] = acc[1, at, :].astype(LOW)

                    @pl.when(me != j)
                    def _():
                        dl_copy(j, me).start()

        for b in range(group_size):
            dq_g[h, b * rows : (b + 1) * rows, :] = dq_s[sources[b]]

    each(0, heads, one_head)

    for b in range(group_size):
        dg_s[b] = dl_s[sources[b]]
    each(1, group_size, lambda o: dg_copy(o, True).start())
    each(0, heads, send_dq)

    dl_r[me] = dl_s[me]
    settle(dl_r.at[seven], dl_recv)

    def merge(received, part, g):
        return (
            received[g, part].astype(FULL) + received[KVH + g, part].astype(FULL)
        ).astype(LOW)

    for part in range(PARTS):
        for i in range(PCOLS // HD):
            dkv_all[y * 2 + core, part, :, i * HD : (i + 1) * HD] = merge(
                dl_r, part * PCOLS // kvw, (part * PCOLS % kvw) // HD + i
            )
        for k in range(2):
            ya_copy(part, k, True).start()
        yc_copy(part, 0, True).start()

    settle(kv_r.at[:, pl.ds(0, others), :], kv_send)
    settle(qd_r.at[:, :, pl.ds(0, others), :], in_send)
    settle(hid_s.at[pl.ds(0, column - 1)], hid_send)

    settle(hid_s.at[pl.ds(0, column - 1)], hid_recv)
    def pass_on(part):
        for k in range(2):
            ya_copy(part, k, False).wait_recv()
            yf_copy(part, k, True).start()
            yc_copy(part, 1 if k else ys - 1, True).start()

    def hand_far(part):
        settle(dkv_all.at[0, part], yf_recv.at[part])
        yc_copy(part, 2, True).start()

    def multiply(part):
        for k in (0, 1, ys - 1, 2):
            yc_copy(part, k, False).wait_recv()
            from_y = lax.rem(y + k, ys)
            grads = dkv_all[pl.ds(from_y * 2, 2), part].reshape(2 * rows, PCOLS)
            term = jnp.dot(hid_t[from_y], grads, preferred_element_type=FULL)
            if k > 0:
                term = prod[part] + term
            prod[part] = term
            if k == 2:
                prod_s[part] = term.astype(LOW)
        each(1, summed_over, lambda o: rs_copy(part, o).start())

    pass_on(0)
    for part in range(PARTS):
        if part + 1 < PARTS:
            pass_on(part + 1)
        hand_far(part)
        multiply(part)

    dg_r[me] = dg_s[me]
    settle(dg_r.at[seven], dg_recv)
    dk_rows = jnp.concatenate([merge(dg_r, 0, g) for g in range(KVH)], axis=1)
    dv_rows = jnp.concatenate([merge(dg_r, 1, g) for g in range(KVH)], axis=1)

    def hidden_tile(t):
        at = pl.ds(pl.multiple_of(t * 512, 512), 512)
        tile = lax.dot_general(
            dk_rows, kw_v[at, :], NT, preferred_element_type=FULL
        ) + lax.dot_general(dv_rows, vw_v[at, :], NT, preferred_element_type=FULL)
        gh_v[:, at] = tile.astype(LOW)

    each(0, width // 512, hidden_tile)
    gh_out = pltpu.make_async_copy(gh_v, grad_hidden, gh_sem)
    gh_out.start()

    settle(dg_s.at[seven], dg_send)
    settle(dl_s.at[seven], dl_send)
    settle(dq_g.at[:, pl.ds(0, others), :], dq_send)
    settle(dq_g.at[:, pl.ds(0, others), :], dq_recv)
    settle(dq_g.at[:, pl.ds(0, rows), :], dq_own)
    settle(dkv_all.at[pl.ds(0, 2)], ya_send)
    settle(dkv_all.at[0], yf_send)
    settle(dkv_all.at[pl.ds(0, ys)], yc_send)

    norm = 1.0 / math.sqrt(total * replica_count)
    own = pl.ds(pl.multiple_of((me * 2 + x_hi) * piece, piece), piece)
    for part in range(PARTS):
        settle(rs_r.at[part, pl.ds(0, summed_over - 1)], rs_recv.at[part])
        summed = prod[part, own, :]
        for o in range(1, summed_over):
            summed = summed + rs_r[part, o].astype(FULL)
        result = grad_value if part * PCOLS >= kvw else grad_key
        at = part * PCOLS % kvw
        result[:, at : at + PCOLS] = (summed * norm).astype(LOW)

    gh_out.wait()
    settle(rs_r.at[:, pl.ds(0, summed_over - 1)], rs_send)


def hand_over(*refs):
    sources, results = refs[0:4], refs[4:8]
    held, sems = refs[8:12], refs[12]
    steps = []
    for i, (source, result, slot) in enumerate(zip(sources, results, held)):
        parts = 4 if i < 2 else 1
        size = source.shape[0] // parts
        for j in range(parts):
            at = pl.ds(j * size, size)
            steps.append(
                (
                    pltpu.make_async_copy(source.at[at], slot.at[at], sems.at[0, i, j]),
                    pltpu.make_async_copy(slot.at[at], result.at[at], sems.at[1, i, j]),
                )
            )
    for load, _ in steps:
        load.start()
    for load, store in steps:
        load.wait()
        store.start()
    for _, store in steps:
        store.wait()


def on_device(
    hidden, queries, out_grad, key_weight, value_weight, seq_lengths, seq_group, loader_offsets
):
    group_size = lax.axis_size("grp")
    replica_count = lax.axis_size("dp")
    rows, width = hidden.shape[1:]
    total = rows * group_size
    heads = HQ // group_size
    kvw = KVH * HD
    piece = width // (group_size * replica_count)
    blocks = total // QBLK
    ys = replica_count // 4
    column = 2 * ys
    chunk = width // column
    dma = pltpu.SemaphoreType.DMA
    scratch = [
        pltpu.VMEM((rows, width), LOW),
        pltpu.VMEM((width, kvw), LOW),
        pltpu.VMEM((width, kvw), LOW),
        pltpu.VMEM((heads, 2, total, HD), LOW),
        pltpu.VMEM((KVH, 2, rows, HD), LOW),
        pltpu.VMEM((2, total, HD), LOW),
        pltpu.VMEM((HD, total), LOW),
        pltpu.VMEM((column, chunk, rows), LOW),
        pltpu.VMEM((ys, chunk, 2 * rows), LOW),
        pltpu.VMEM((total, QBLK), FULL),
        pltpu.VMEM((total, QBLK), FULL),
        pltpu.VMEM((total, QBLK), LOW),
        pltpu.VMEM((total, QBLK), LOW),
        pltpu.VMEM((2, total, HD), FULL),
        pltpu.VMEM((group_size, rows, HD), LOW),
        pltpu.VMEM((heads, total, HD), LOW),
        pltpu.VMEM((group_size, 2, rows, HD), LOW),
        pltpu.VMEM((group_size, 2, rows, HD), LOW),
        pltpu.VMEM((group_size, 2, rows, HD), LOW),
        pltpu.VMEM((group_size, 2, rows, HD), LOW),
        pltpu.VMEM((column, PARTS, rows, PCOLS), LOW),
        pltpu.VMEM((PARTS, chunk, PCOLS), FULL),
        pltpu.VMEM((PARTS, chunk, PCOLS), LOW),
        pltpu.VMEM((PARTS, 2 * group_size, piece, PCOLS), LOW),
        pltpu.VMEM((rows, width), LOW),
        pltpu.VMEM((1, total), jnp.int32),
        dma((3,)),
        dma,
        dma((heads,)),
        dma,
        dma,
        dma,
        dma,
        dma,
        dma,
        dma,
        dma,
        dma,
        dma,
        dma,
        dma,
        dma((PARTS, 2)),
        dma,
        dma((PARTS,)),
        dma,
        dma((PARTS, ys)),
        dma,
        dma((PARTS,)),
        dma,
    ]
    smem = pl.BlockSpec(memory_space=pltpu.SMEM)
    vmem = pl.BlockSpec(memory_space=pltpu.VMEM)
    anywhere = pl.BlockSpec(memory_space=pl.ANY)

    def kernel(*refs):
        layer_kernel(group_size, replica_count, *refs)

    out_shape = (
        jax.ShapeDtypeStruct((rows, HQ * HD), LOW),
        jax.ShapeDtypeStruct((rows, width), LOW),
        jax.ShapeDtypeStruct((piece, kvw), LOW),
        jax.ShapeDtypeStruct((piece, kvw), LOW),
    )
    results = pl.pallas_call(
        kernel,
        out_shape=out_shape,
        in_specs=[smem, smem, smem] + [anywhere] * 5,
        out_specs=(anywhere, anywhere, vmem, vmem),
        scratch_shapes=scratch,
        compiler_params=pltpu.CompilerParams(
            collective_id=0, has_side_effects=True, vmem_limit_bytes=56 * 1024 * 1024
        ),
        name="layer",
    )(
        seq_lengths,
        seq_group,
        loader_offsets,
        hidden[0],
        queries[0],
        out_grad[0],
        key_weight,
        value_weight,
    )
    grad_query, grad_hidden, grad_key, grad_value = pl.pallas_call(
        hand_over,
        out_shape=out_shape,
        in_specs=[anywhere] * 4,
        out_specs=[anywhere] * 4,
        scratch_shapes=[pltpu.VMEM(shape.shape, LOW) for shape in out_shape] + [dma((2, 4, 4))],
        name="hand_over",
    )(*results)
    return (grad_query[None], grad_hidden[None], grad_key, grad_value)


def solution(mesh):
    placed = (
        P("dp", "grp", None),
        P("dp", "grp", None),
        P("dp", "grp", None),
        P(),
        P(),
        P("dp", None),
        P("dp", None),
        P("dp", None),
    )
    return jax.shard_map(
        on_device,
        mesh=mesh,
        in_specs=placed,
        out_specs=(
            P("dp", "grp", None),
            P("dp", "grp", None),
            P(("grp", "dp"), None),
            P(("grp", "dp"), None),
        ),
        check_vma=False,
    )
```

```python
import math

import jax
import jax.numpy as jnp
from jax import lax
from jax.experimental import pallas as pl
from jax.experimental.pallas import tpu as pltpu
from jax.sharding import PartitionSpec as P

HQ = 32
KVH = 4
HD = 128
SLOTS = 8
QBLK = 256
ZS = 4
PARTS = 4
PCOLS = 2 * KVH * HD // PARTS
LOW = jnp.bfloat16
FULL = jnp.float32
MESH = pl.DeviceIdType.MESH
NT = (((1,), (1,)), ((), ()))


def each(first, last, step):
    def body(i, carry):
        step(i)
        return carry

    lax.fori_loop(first, last, body, 0)


def layer_kernel(
    group_size,
    replica_count,
    lengths,
    groups,
    offsets,
    hidden,
    queries,
    out_grad,
    key_weight,
    value_weight,
    grad_query,
    grad_hidden,
    grad_key,
    grad_value,
    hid_v,
    kw_v,
    vw_v,
    qd_r,
    kv_s,
    kv_r,
    kt_v,
    hid_s,
    hid_t,
    s_v,
    pg_v,
    wl_v,
    ds_v,
    acc,
    dq_s,
    dq_g,
    dl_s,
    dl_r,
    dg_s,
    dg_r,
    dkv_all,
    prod,
    prod_s,
    rs_r,
    gh_v,
    begin_v,
    load_sem,
    in_send,
    in_recv,
    kv_send,
    kv_recv,
    hid_send,
    hid_recv,
    dq_send,
    dq_recv,
    dq_own,
    dl_send,
    dl_recv,
    dg_send,
    dg_recv,
    ya_send,
    ya_recv,
    yf_send,
    yf_recv,
    yc_send,
    yc_recv,
    rs_send,
    rs_recv,
    gh_sem,
):
    me = lax.axis_index("grp")
    rep = lax.axis_index("dp")
    x_lo, z = me // ZS, lax.rem(me, ZS)
    y, x_hi, core = rep // 4, lax.rem(rep // 2, 2), lax.rem(rep, 2)
    ys = replica_count // 4
    column = 2 * ys
    summed_over = 2 * group_size
    rows = hidden.shape[0]
    width = hidden.shape[1]
    total = rows * group_size
    heads = HQ // group_size
    wide = heads * HD
    kvw = KVH * HD
    piece = width // (group_size * replica_count)
    inv_root = 1.0 / math.sqrt(HD)
    exp_scale = inv_root / math.log(2.0)
    blocks = total // QBLK
    per_block = QBLK // rows

    def peer(o):
        return lax.rem(x_lo + o // ZS, 2) * ZS + lax.rem(z + o, ZS)

    def origin(o):
        return lax.rem(x_lo + o // ZS, 2) * ZS + lax.rem(z - o + 2 * ZS, ZS)

    def place(at_y, at_x_hi, at_core):
        return (at_y * 2 + at_x_hi) * 2 + at_core

    def first_col(device):
        return lax.rem(device, KVH) * (2 * wide) + (device // KVH) * wide

    def rows_of(block):
        return pl.ds(pl.multiple_of(block * rows, rows), rows)

    def cols(at, n):
        return pl.ds(pl.multiple_of(at, n), n)

    load_hid = pltpu.make_async_copy(hidden, hid_v, load_sem.at[0])
    load_kw = pltpu.make_async_copy(key_weight, kw_v, load_sem.at[1])
    load_vw = pltpu.make_async_copy(value_weight, vw_v, load_sem.at[2])
    load_hid.start()
    load_kw.start()
    load_vw.start()

    barrier = pltpu.get_barrier_semaphore()

    def column_peer(o):
        return place(lax.rem(y + o // 2, ys), x_hi, lax.rem(core + o, 2))

    def column_origin(o):
        return lax.rem(y - o // 2 + ys, ys), lax.rem(core + o, 2)

    def sum_peer(o):
        return {
            "grp": peer(lax.rem(o, group_size)),
            "dp": place(y, lax.rem(x_hi + o // group_size, 2), core),
        }

    each(
        1,
        column,
        lambda o: pl.semaphore_signal(
            barrier, inc=1, device_id={"dp": column_peer(o)}, device_id_type=MESH
        ),
    )
    each(
        1,
        summed_over,
        lambda o: pl.semaphore_signal(
            barrier, inc=1, device_id=sum_peer(o), device_id_type=MESH
        ),
    )

    def q_copy(h, o, to):
        dest = peer(o)
        at = rows_of(me if to else origin(o))
        return pltpu.make_async_remote_copy(
            src_ref=queries.at[:, cols(first_col(dest) + h * HD, HD)],
            dst_ref=qd_r.at[h, 0, at, :],
            send_sem=in_send,
            recv_sem=in_recv.at[h, 0],
            device_id={"grp": dest},
            device_id_type=MESH,
        )

    def do_copy(h, o, to):
        dest = peer(o)
        at = rows_of(me if to else origin(o))
        return pltpu.make_async_remote_copy(
            src_ref=out_grad.at[:, cols(first_col(dest) + h * HD, HD)],
            dst_ref=qd_r.at[h, 1, at, :],
            send_sem=in_send,
            recv_sem=in_recv.at[h, 1],
            device_id={"grp": dest},
            device_id_type=MESH,
        )

    def kv_copy(o, to):
        dest = peer(o)
        at = rows_of(me if to else origin(o))
        return pltpu.make_async_remote_copy(
            src_ref=kv_s.at[lax.rem(dest, KVH)],
            dst_ref=kv_r.at[:, at, :],
            send_sem=kv_send,
            recv_sem=kv_recv,
            device_id={"grp": dest},
            device_id_type=MESH,
        )

    def hid_copy(o, to):
        dest_y, dest_core = lax.rem(y + o // 2, ys), lax.rem(core + o, 2)
        from_y, from_core = (y, core) if to else column_origin(o)
        return pltpu.make_async_remote_copy(
            src_ref=hid_s.at[dest_y * 2 + dest_core],
            dst_ref=hid_t.at[from_y, :, cols(from_core * rows, rows)],
            send_sem=hid_send,
            recv_sem=hid_recv,
            device_id={"dp": column_peer(o)},
            device_id_type=MESH,
        )

    def dq_copy(h, o, to):
        dest = peer(o)
        at = first_col(me if to else origin(o)) + h * HD
        return pltpu.make_async_remote_copy(
            src_ref=dq_g.at[h, rows_of(dest), :],
            dst_ref=grad_query.at[:, cols(at, HD)],
            send_sem=dq_send,
            recv_sem=dq_recv,
            device_id={"grp": dest},
            device_id_type=MESH,
        )

    def dq_stay(h):
        return pltpu.make_async_copy(
            dq_g.at[h, rows_of(me), :],
            grad_query.at[:, cols(first_col(me) + h * HD, HD)],
            dq_own,
        )

    def dl_copy(part, dest):
        return pltpu.make_async_remote_copy(
            src_ref=dl_s.at[dest, part],
            dst_ref=dl_r.at[me, part],
            send_sem=dl_send,
            recv_sem=dl_recv.at[part],
            device_id={"grp": dest},
            device_id_type=MESH,
        )

    def dg_copy(o, to):
        dest = peer(o)
        return pltpu.make_async_remote_copy(
            src_ref=dg_s.at[dest],
            dst_ref=dg_r.at[me if to else origin(o)],
            send_sem=dg_send,
            recv_sem=dg_recv,
            device_id={"grp": dest},
            device_id_type=MESH,
        )

    def ya_copy(part, k, to):
        step = (1, ys - 1, 2)[k]
        at = (y if to else lax.rem(y + ys - step, ys)) * 2 + core
        return pltpu.make_async_remote_copy(
            src_ref=dkv_all.at[y * 2 + core, part],
            dst_ref=dkv_all.at[at, part],
            send_sem=ya_send,
            recv_sem=ya_recv.at[part, k],
            device_id={"dp": place(lax.rem(y + step, ys), x_hi, core)},
            device_id_type=MESH,
        )

    def yf_copy(part, k, to):
        step = ys - 1 if k else 1
        come = lax.rem(y + ys - step, ys) * 2 + core
        far = lax.rem(y + 2, ys) * 2 + core
        half = pl.ds(k * (rows // 2), rows // 2)
        return pltpu.make_async_remote_copy(
            src_ref=dkv_all.at[come, part, half],
            dst_ref=dkv_all.at[come if to else far, part, half],
            send_sem=yf_send,
            recv_sem=yf_recv.at[part],
            device_id={"dp": place(lax.rem(y + step, ys), x_hi, core)},
            device_id_type=MESH,
        )

    def yc_copy(part, k, to):
        from_y = lax.rem(y + k, ys)
        return pltpu.make_async_remote_copy(
            src_ref=dkv_all.at[from_y * 2 + core, part],
            dst_ref=dkv_all.at[from_y * 2 + (core if to else 1 - core), part],
            send_sem=yc_send,
            recv_sem=yc_recv.at[part, k],
            device_id={"dp": place(y, x_hi, 1 - core)},
            device_id_type=MESH,
        )

    def rs_copy(part, o):
        dest = sum_peer(o)
        at = dest["grp"] * 2 + lax.rem(x_hi + o // group_size, 2)
        return pltpu.make_async_remote_copy(
            src_ref=prod_s.at[part, pl.ds(pl.multiple_of(at * piece, piece), piece), :],
            dst_ref=rs_r.at[part, o],
            send_sem=rs_send,
            recv_sem=rs_recv.at[part],
            device_id=dest,
            device_id_type=MESH,
        )

    def settle(ref, sem):
        pltpu.make_async_copy(ref, ref, sem).wait()

    others = total - rows
    seven = pl.ds(0, group_size - 1)

    def own_q(h):
        return pltpu.make_async_copy(
            queries.at[:, cols(first_col(me) + h * HD, HD)],
            qd_r.at[h, 0, rows_of(me), :],
            in_recv.at[h, 0],
        )

    def own_do(h):
        return pltpu.make_async_copy(
            out_grad.at[:, cols(first_col(me) + h * HD, HD)],
            qd_r.at[h, 1, rows_of(me), :],
            in_recv.at[h, 1],
        )

    def send_head(h):
        each(1, group_size, lambda o: q_copy(h, o, True).start())
        each(1, group_size, lambda o: do_copy(h, o, True).start())

    load_hid.wait()
    load_kw.wait()
    hid_rows = hid_v[...]

    def project(weight, which):
        for g in range(0, KVH, 2):
            both = jnp.dot(
                hid_rows, weight[:, g * HD : (g + 2) * HD], preferred_element_type=FULL
            ).astype(LOW)
            kv_s[g, which] = both[:, :HD]
            kv_s[g + 1, which] = both[:, HD:]

    project(kw_v, 0)
    load_vw.wait()
    project(vw_v, 1)

    pl.semaphore_wait(barrier, column - 1 + summed_over - 1)

    each(1, group_size, lambda o: kv_copy(o, True).start())
    each(0, heads, send_head)
    for h in range(heads):
        own_q(h).start()
        own_do(h).start()
    kv_r[:, rows_of(me), :] = kv_s[lax.rem(me, KVH)]

    lanes = 4 * piece

    def turn(t):
        turned = hid_v[:, cols(t * lanes, lanes)].T
        g = t // ys
        to_y = lax.rem(t, ys)
        for xh in range(2):
            at = pl.ds(pl.multiple_of((g * 2 + xh) * piece, piece), piece)
            for c in range(2):
                hid_s[to_y * 2 + c, at, :] = turned[(xh * 2 + c) * piece :][:piece]

    each(0, width // lanes, turn)
    each(1, column, lambda o: hid_copy(o, True).start())
    hid_t[y, :, cols(core * rows, rows)] = hid_s[y * 2 + core]

    row_ids = lax.broadcasted_iota(jnp.int32, (1, total), 1)
    begin = jnp.zeros((1, total), jnp.int32)
    for s in range(SLOTS):
        at, size = offsets[0, s], lengths[0, s]
        begin = jnp.where((row_ids >= at) & (row_ids < at + size), at, begin)
    begin_v[...] = begin
    starts = []
    for s in range(SLOTS):
        start = jnp.int32(0)
        for t in range(SLOTS):
            if t < s:
                before = groups[0, t] <= groups[0, s]
            else:
                before = groups[0, t] < groups[0, s]
            if t != s:
                start = start + jnp.where(before, lengths[0, t], 0)
        starts.append(start)

    def source_block(row):
        found = jnp.int32(0)
        for s in range(SLOTS):
            inside = (row >= starts[s]) & (row < starts[s] + lengths[0, s])
            found = found + jnp.where(inside, offsets[0, s] + row - starts[s], 0)
        return found // rows

    sources = [source_block(b * rows) for b in range(group_size)]

    acc[...] = jnp.zeros_like(acc)
    settle(kv_r.at[:, pl.ds(0, others), :], kv_recv)
    kt_v[...] = kv_r[0].T

    key_ids = lax.broadcasted_iota(jnp.int32, (HD, QBLK), 0)
    lane_ids = lax.broadcasted_iota(jnp.int32, (HD, QBLK), 1)

    def fold(tile):
        return tile.reshape(HD // 8, 8, QBLK)

    def span(b):
        first = sum((i + 1) * QBLK for i in range(b))
        return first, (b + 1) * QBLK

    def weigh(h, b):
        r0 = b * QBLK
        first, keys = span(b)
        q_blk = qd_r[h, 0, r0 : r0 + QBLK, :]
        begin_row = begin_v[:, r0 : r0 + QBLK]
        s_v[first : first + keys, :] = lax.dot_general(
            kv_r[0, 0:keys, :], q_blk, NT, preferred_element_type=FULL
        )
        top = jnp.full((8, QBLK), -1e30, FULL)
        for j in range(keys // HD):
            at = slice(first + j * HD, first + (j + 1) * HD)
            seen = key_ids + j * HD >= begin_row
            if j * HD >= r0:
                seen = seen & (key_ids + (j * HD - r0) <= lane_ids)
            tile = jnp.where(seen, s_v[at, :], -1e30)
            s_v[at, :] = tile
            top = jnp.maximum(top, jnp.max(fold(tile), axis=0))
        top = jnp.max(top, axis=0, keepdims=True)
        mass = jnp.zeros((8, QBLK), FULL)
        for j in range(keys // HD):
            at = slice(first + j * HD, first + (j + 1) * HD)
            tile = jnp.exp2((s_v[at, :] - top) * exp_scale)
            s_v[at, :] = tile
            mass = mass + jnp.sum(fold(tile), axis=0)
        inverse = 1.0 / jnp.sum(mass, axis=0, keepdims=True)
        for j in range(keys // HD):
            at = slice(first + j * HD, first + (j + 1) * HD)
            weights = s_v[at, :] * inverse
            s_v[at, :] = weights
            wl_v[at, :] = weights.astype(LOW)

    def attend(h, b):
        r0 = b * QBLK
        first, keys = span(b)
        q_blk = qd_r[h, 0, r0 : r0 + QBLK, :]
        do_blk = qd_r[h, 1, r0 : r0 + QBLK, :]
        pg_v[first : first + keys, :] = lax.dot_general(
            kv_r[1, 0:keys, :], do_blk, NT, preferred_element_type=FULL
        )
        delta = jnp.zeros((8, QBLK), FULL)
        for j in range(keys // HD):
            at = slice(first + j * HD, first + (j + 1) * HD)
            delta = delta + jnp.sum(fold(wl_v[at, :].astype(FULL) * pg_v[at, :]), axis=0)
        delta = jnp.sum(delta, axis=0, keepdims=True)
        for j in range(keys // HD):
            at = slice(first + j * HD, first + (j + 1) * HD)
            ds_v[at, :] = (s_v[at, :] * (pg_v[at, :] - delta)).astype(LOW)
        all_keys = slice(first, first + keys)
        acc[1, 0:keys, :] += jnp.dot(wl_v[all_keys, :], do_blk, preferred_element_type=FULL)
        acc[0, 0:keys, :] += jnp.dot(ds_v[all_keys, :], q_blk, preferred_element_type=FULL)
        grad_t = jnp.dot(kt_v[:, 0:keys], ds_v[all_keys, :], preferred_element_type=FULL)
        grad_rows = (grad_t * inv_root).T.astype(LOW)
        for j in range(per_block):
            dq_s[r0 // rows + j] = grad_rows[j * rows : (j + 1) * rows, :]

    def send_dq(h):
        each(1, group_size, lambda o: dq_copy(h, o, True).start())
        dq_stay(h).start()

    def one_head(h):
        settle(qd_r.at[h, 0], in_recv.at[h, 0])
        for b in reversed(range(blocks)):
            weigh(h, b)
        settle(qd_r.at[h, 1], in_recv.at[h, 1])

        @pl.when(h == heads - 1)
        def _():
            send_dq(0)

        for b in reversed(range(blocks)):
            attend(h, b)

            @pl.when(h == heads - 1)
            def _():
                for part in range(2):
                    for j in range(b * per_block, (b + 1) * per_block):
                        at = slice(j * rows, (j + 1) * rows)
                        term = acc[part, at, :]
                        if part == 0:
                            term = term * inv_root
                        dl_s[j, part] = term.astype(LOW)

                        @pl.when(me != j)
                        def _():
                            dl_copy(part, j).start()

        for b in range(group_size):
            dq_g[h, b * rows : (b + 1) * rows, :] = dq_s[sources[b]]

    each(0, heads, one_head)

    send_dq(1)
    dl_r[me] = dl_s[me]
    for b in range(group_size):
        dg_s[b] = dl_s[sources[b]]

    def merge(received, part, g):
        return (
            received[g, part].astype(FULL) + received[KVH + g, part].astype(FULL)
        ).astype(LOW)

    for part in range(PARTS):
        which = part * PCOLS // kvw
        if part * PCOLS % kvw == 0:
            settle(dl_r.at[seven, which], dl_recv.at[which])
        for i in range(PCOLS // HD):
            dkv_all[y * 2 + core, part, :, i * HD : (i + 1) * HD] = merge(
                dl_r, which, (part * PCOLS % kvw) // HD + i
            )
        for k in range(3 if part == PARTS - 1 else 2):
            ya_copy(part, k, True).start()
        yc_copy(part, 0, True).start()

    each(1, group_size, lambda o: dg_copy(o, True).start())
    each(2, heads, send_dq)
    settle(kv_r.at[:, pl.ds(0, others), :], kv_send)
    settle(qd_r.at[:, :, pl.ds(0, others), :], in_send)
    settle(hid_s.at[pl.ds(0, column - 1)], hid_send)

    settle(hid_s.at[pl.ds(0, column - 1)], hid_recv)
    def pass_on(part):
        for k in range(2):
            ya_copy(part, k, False).wait_recv()
            if part < PARTS - 1:
                yf_copy(part, k, True).start()
            yc_copy(part, 1 if k else ys - 1, True).start()

    def hand_far(part):
        if part < PARTS - 1:
            settle(dkv_all.at[0, part], yf_recv.at[part])
        else:
            ya_copy(part, 2, False).wait_recv()
        yc_copy(part, 2, True).start()

    def multiply(part):
        for k in (0, 1, ys - 1, 2):
            yc_copy(part, k, False).wait_recv()
            from_y = lax.rem(y + k, ys)
            grads = dkv_all[pl.ds(from_y * 2, 2), part].reshape(2 * rows, PCOLS)
            term = jnp.dot(hid_t[from_y], grads, preferred_element_type=FULL)
            if k > 0:
                term = prod[part] + term
            prod[part] = term
            if k == 2:
                prod_s[part] = term.astype(LOW)
        each(1, summed_over, lambda o: rs_copy(part, o).start())

    pass_on(0)
    for part in range(PARTS):
        if part + 1 < PARTS:
            pass_on(part + 1)
        hand_far(part)
        multiply(part)

    dg_r[me] = dg_s[me]
    settle(dg_r.at[seven], dg_recv)
    dk_rows = jnp.concatenate([merge(dg_r, 0, g) for g in range(KVH)], axis=1)
    dv_rows = jnp.concatenate([merge(dg_r, 1, g) for g in range(KVH)], axis=1)

    def hidden_tile(t):
        at = pl.ds(pl.multiple_of(t * 512, 512), 512)
        tile = lax.dot_general(
            dk_rows, kw_v[at, :], NT, preferred_element_type=FULL
        ) + lax.dot_general(dv_rows, vw_v[at, :], NT, preferred_element_type=FULL)
        gh_v[:, at] = tile.astype(LOW)

    each(0, width // 512, hidden_tile)
    gh_out = pltpu.make_async_copy(gh_v, grad_hidden, gh_sem)
    gh_out.start()

    settle(dg_s.at[seven], dg_send)
    settle(dl_s.at[seven], dl_send)
    settle(dq_g.at[:, pl.ds(0, others), :], dq_send)
    settle(dq_g.at[:, pl.ds(0, others), :], dq_recv)
    settle(dq_g.at[:, pl.ds(0, rows), :], dq_own)
    settle(dkv_all.at[pl.ds(0, 2)], ya_send)
    settle(dkv_all.at[0, 0], ya_send)
    settle(dkv_all.at[0, pl.ds(0, PARTS - 1)], yf_send)
    settle(dkv_all.at[pl.ds(0, ys)], yc_send)

    norm = 1.0 / math.sqrt(total * replica_count)
    own = pl.ds(pl.multiple_of((me * 2 + x_hi) * piece, piece), piece)
    for part in range(PARTS):
        settle(rs_r.at[part, pl.ds(0, summed_over - 1)], rs_recv.at[part])
        summed = prod[part, own, :]
        for o in range(1, summed_over):
            summed = summed + rs_r[part, o].astype(FULL)
        result = grad_value if part * PCOLS >= kvw else grad_key
        at = part * PCOLS % kvw
        result[:, at : at + PCOLS] = (summed * norm).astype(LOW)

    gh_out.wait()
    settle(rs_r.at[:, pl.ds(0, summed_over - 1)], rs_send)


def hand_over(*refs):
    sources, results = refs[0:4], refs[4:8]
    held, sems = refs[8:12], refs[12]
    steps = []
    for i, (source, result, slot) in enumerate(zip(sources, results, held)):
        parts = 4 if i < 2 else 1
        size = source.shape[0] // parts
        for j in range(parts):
            at = pl.ds(j * size, size)
            steps.append(
                (
                    pltpu.make_async_copy(source.at[at], slot.at[at], sems.at[0, i, j]),
                    pltpu.make_async_copy(slot.at[at], result.at[at], sems.at[1, i, j]),
                )
            )
    for load, _ in steps:
        load.start()
    for load, store in steps:
        load.wait()
        store.start()
    for _, store in steps:
        store.wait()


def on_device(
    hidden, queries, out_grad, key_weight, value_weight, seq_lengths, seq_group, loader_offsets
):
    group_size = lax.axis_size("grp")
    replica_count = lax.axis_size("dp")
    rows, width = hidden.shape[1:]
    total = rows * group_size
    heads = HQ // group_size
    kvw = KVH * HD
    piece = width // (group_size * replica_count)
    blocks = total // QBLK
    ys = replica_count // 4
    column = 2 * ys
    chunk = width // column
    tall = sum((b + 1) * QBLK for b in range(blocks))
    dma = pltpu.SemaphoreType.DMA
    scratch = [
        pltpu.VMEM((rows, width), LOW),
        pltpu.VMEM((width, kvw), LOW),
        pltpu.VMEM((width, kvw), LOW),
        pltpu.VMEM((heads, 2, total, HD), LOW),
        pltpu.VMEM((KVH, 2, rows, HD), LOW),
        pltpu.VMEM((2, total, HD), LOW),
        pltpu.VMEM((HD, total), LOW),
        pltpu.VMEM((column, chunk, rows), LOW),
        pltpu.VMEM((ys, chunk, 2 * rows), LOW),
        pltpu.VMEM((tall, QBLK), FULL),
        pltpu.VMEM((tall, QBLK), FULL),
        pltpu.VMEM((tall, QBLK), LOW),
        pltpu.VMEM((tall, QBLK), LOW),
        pltpu.VMEM((2, total, HD), FULL),
        pltpu.VMEM((group_size, rows, HD), LOW),
        pltpu.VMEM((heads, total, HD), LOW),
        pltpu.VMEM((group_size, 2, rows, HD), LOW),
        pltpu.VMEM((group_size, 2, rows, HD), LOW),
        pltpu.VMEM((group_size, 2, rows, HD), LOW),
        pltpu.VMEM((group_size, 2, rows, HD), LOW),
        pltpu.VMEM((column, PARTS, rows, PCOLS), LOW),
        pltpu.VMEM((PARTS, chunk, PCOLS), FULL),
        pltpu.VMEM((PARTS, chunk, PCOLS), LOW),
        pltpu.VMEM((PARTS, 2 * group_size, piece, PCOLS), LOW),
        pltpu.VMEM((rows, width), LOW),
        pltpu.VMEM((1, total), jnp.int32),
        dma((3,)),
        dma,
        dma((heads, 2)),
        dma,
        dma,
        dma,
        dma,
        dma,
        dma,
        dma,
        dma,
        dma((2,)),
        dma,
        dma,
        dma,
        dma((PARTS, 3)),
        dma,
        dma((PARTS - 1,)),
        dma,
        dma((PARTS, ys)),
        dma,
        dma((PARTS,)),
        dma,
    ]
    smem = pl.BlockSpec(memory_space=pltpu.SMEM)
    vmem = pl.BlockSpec(memory_space=pltpu.VMEM)
    anywhere = pl.BlockSpec(memory_space=pl.ANY)

    def kernel(*refs):
        layer_kernel(group_size, replica_count, *refs)

    out_shape = (
        jax.ShapeDtypeStruct((rows, HQ * HD), LOW),
        jax.ShapeDtypeStruct((rows, width), LOW),
        jax.ShapeDtypeStruct((piece, kvw), LOW),
        jax.ShapeDtypeStruct((piece, kvw), LOW),
    )
    results = pl.pallas_call(
        kernel,
        out_shape=out_shape,
        in_specs=[smem, smem, smem] + [anywhere] * 5,
        out_specs=(anywhere, anywhere, vmem, vmem),
        scratch_shapes=scratch,
        compiler_params=pltpu.CompilerParams(
            collective_id=0, has_side_effects=True, vmem_limit_bytes=56 * 1024 * 1024
        ),
        name="layer",
    )(
        seq_lengths,
        seq_group,
        loader_offsets,
        hidden[0],
        queries[0],
        out_grad[0],
        key_weight,
        value_weight,
    )
    grad_query, grad_hidden, grad_key, grad_value = pl.pallas_call(
        hand_over,
        out_shape=out_shape,
        in_specs=[anywhere] * 4,
        out_specs=[anywhere] * 4,
        scratch_shapes=[pltpu.VMEM(shape.shape, LOW) for shape in out_shape] + [dma((2, 4, 4))],
        name="hand_over",
    )(*results)
    return (grad_query[None], grad_hidden[None], grad_key, grad_value)


def solution(mesh):
    placed = (
        P("dp", "grp", None),
        P("dp", "grp", None),
        P("dp", "grp", None),
        P(),
        P(),
        P("dp", None),
        P("dp", None),
        P("dp", None),
    )
    return jax.shard_map(
        on_device,
        mesh=mesh,
        in_specs=placed,
        out_specs=(
            P("dp", "grp", None),
            P("dp", "grp", None),
            P(("grp", "dp"), None),
            P(("grp", "dp"), None),
        ),
        check_vma=False,
    )
```

```python
import math

import jax
import jax.numpy as jnp
from jax import lax
from jax.experimental import pallas as pl
from jax.experimental.pallas import tpu as pltpu
from jax.sharding import PartitionSpec as P

HQ = 32
KVH = 4
HD = 128
SLOTS = 8
QBLK = 256
ZS = 4
PARTS = 4
PCOLS = 2 * KVH * HD // PARTS
LOW = jnp.bfloat16
FULL = jnp.float32
MESH = pl.DeviceIdType.MESH
NT = (((1,), (1,)), ((), ()))


def each(first, last, step):
    def body(i, carry):
        step(i)
        return carry

    lax.fori_loop(first, last, body, 0)


def layer_kernel(
    group_size,
    replica_count,
    lengths,
    groups,
    offsets,
    hidden,
    queries,
    out_grad,
    key_weight,
    value_weight,
    grad_query,
    grad_hidden,
    grad_key,
    grad_value,
    hid_v,
    kw_v,
    vw_v,
    qd_r,
    kv_s,
    kv_r,
    kt_v,
    hid_s,
    hid_t,
    s_v,
    pg_v,
    wl_v,
    ds_v,
    acc,
    dq_s,
    dq_g,
    dl_s,
    dl_r,
    dg_s,
    dg_r,
    dkv_all,
    prod,
    rx_s,
    rx_r,
    rs_s,
    rs_r,
    gh_v,
    begin_v,
    load_sem,
    in_send,
    in_recv,
    kv_send,
    kv_recv,
    hid_send,
    hid_recv,
    dq_send,
    dq_recv,
    dq_own,
    dl_send,
    dl_recv,
    dg_send,
    dg_recv,
    ya_send,
    ya_recv,
    yf_send,
    yf_recv,
    yc_send,
    yc_recv,
    rx_send,
    rx_recv,
    rs_send,
    rs_recv,
    gh_sem,
):
    me = lax.axis_index("grp")
    rep = lax.axis_index("dp")
    x_lo, z = me // ZS, lax.rem(me, ZS)
    y, x_hi, core = rep // 4, lax.rem(rep // 2, 2), lax.rem(rep, 2)
    ys = replica_count // 4
    column = 2 * ys
    rows = hidden.shape[0]
    width = hidden.shape[1]
    total = rows * group_size
    heads = HQ // group_size
    wide = heads * HD
    kvw = KVH * HD
    piece = width // (group_size * replica_count)
    half_rows = group_size * piece
    inv_root = 1.0 / math.sqrt(HD)
    exp_scale = inv_root / math.log(2.0)
    blocks = total // QBLK
    per_block = QBLK // rows

    def peer(o):
        return lax.rem(x_lo + o // ZS, 2) * ZS + lax.rem(z + o, ZS)

    def origin(o):
        return lax.rem(x_lo + o // ZS, 2) * ZS + lax.rem(z - o + 2 * ZS, ZS)

    def place(at_y, at_x_hi, at_core):
        return (at_y * 2 + at_x_hi) * 2 + at_core

    def first_col(device):
        return lax.rem(device, KVH) * (2 * wide) + (device // KVH) * wide

    def rows_of(block):
        return pl.ds(pl.multiple_of(block * rows, rows), rows)

    def cols(at, n):
        return pl.ds(pl.multiple_of(at, n), n)

    load_hid = pltpu.make_async_copy(hidden, hid_v, load_sem.at[0])
    load_kw = pltpu.make_async_copy(key_weight, kw_v, load_sem.at[1])
    load_vw = pltpu.make_async_copy(value_weight, vw_v, load_sem.at[2])
    load_hid.start()
    load_kw.start()
    load_vw.start()

    barrier = pltpu.get_barrier_semaphore()

    def column_peer(o):
        return place(lax.rem(y + o // 2, ys), x_hi, lax.rem(core + o, 2))

    def column_origin(o):
        return lax.rem(y - o // 2 + ys, ys), lax.rem(core + o, 2)

    across = {"grp": lax.rem(me + ZS, group_size), "dp": place(y, 1 - x_hi, core)}

    each(
        1,
        column,
        lambda o: pl.semaphore_signal(
            barrier, inc=1, device_id={"dp": column_peer(o)}, device_id_type=MESH
        ),
    )
    each(
        1,
        group_size,
        lambda o: pl.semaphore_signal(
            barrier, inc=1, device_id={"grp": peer(o)}, device_id_type=MESH
        ),
    )
    pl.semaphore_signal(barrier, inc=1, device_id=across, device_id_type=MESH)

    def q_copy(h, o, to):
        dest = peer(o)
        at = rows_of(me if to else origin(o))
        return pltpu.make_async_remote_copy(
            src_ref=queries.at[:, cols(first_col(dest) + h * HD, HD)],
            dst_ref=qd_r.at[h, 0, at, :],
            send_sem=in_send,
            recv_sem=in_recv.at[h, 0],
            device_id={"grp": dest},
            device_id_type=MESH,
        )

    def do_copy(h, o, to):
        dest = peer(o)
        at = rows_of(me if to else origin(o))
        return pltpu.make_async_remote_copy(
            src_ref=out_grad.at[:, cols(first_col(dest) + h * HD, HD)],
            dst_ref=qd_r.at[h, 1, at, :],
            send_sem=in_send,
            recv_sem=in_recv.at[h, 1],
            device_id={"grp": dest},
            device_id_type=MESH,
        )

    def kv_copy(o, to):
        dest = peer(o)
        at = rows_of(me if to else origin(o))
        return pltpu.make_async_remote_copy(
            src_ref=kv_s.at[lax.rem(dest, KVH)],
            dst_ref=kv_r.at[:, at, :],
            send_sem=kv_send,
            recv_sem=kv_recv,
            device_id={"grp": dest},
            device_id_type=MESH,
        )

    def hid_copy(o, to):
        dest_y, dest_core = lax.rem(y + o // 2, ys), lax.rem(core + o, 2)
        from_y, from_core = (y, core) if to else column_origin(o)
        return pltpu.make_async_remote_copy(
            src_ref=hid_s.at[dest_y * 2 + dest_core],
            dst_ref=hid_t.at[from_y, :, cols(from_core * rows, rows)],
            send_sem=hid_send,
            recv_sem=hid_recv,
            device_id={"dp": column_peer(o)},
            device_id_type=MESH,
        )

    def dq_copy(h, o, to):
        dest = peer(o)
        at = first_col(me if to else origin(o)) + h * HD
        return pltpu.make_async_remote_copy(
            src_ref=dq_g.at[h, rows_of(dest), :],
            dst_ref=grad_query.at[:, cols(at, HD)],
            send_sem=dq_send,
            recv_sem=dq_recv,
            device_id={"grp": dest},
            device_id_type=MESH,
        )

    def dq_stay(h):
        return pltpu.make_async_copy(
            dq_g.at[h, rows_of(me), :],
            grad_query.at[:, cols(first_col(me) + h * HD, HD)],
            dq_own,
        )

    def dl_copy(part, dest):
        return pltpu.make_async_remote_copy(
            src_ref=dl_s.at[dest, part],
            dst_ref=dl_r.at[me, part],
            send_sem=dl_send,
            recv_sem=dl_recv.at[part],
            device_id={"grp": dest},
            device_id_type=MESH,
        )

    def dg_copy(o, to):
        dest = peer(o)
        return pltpu.make_async_remote_copy(
            src_ref=dg_s.at[dest],
            dst_ref=dg_r.at[me if to else origin(o)],
            send_sem=dg_send,
            recv_sem=dg_recv,
            device_id={"grp": dest},
            device_id_type=MESH,
        )

    def ya_copy(part, k, to):
        step = (1, ys - 1, 2)[k]
        at = (y if to else lax.rem(y + ys - step, ys)) * 2 + core
        return pltpu.make_async_remote_copy(
            src_ref=dkv_all.at[y * 2 + core, part],
            dst_ref=dkv_all.at[at, part],
            send_sem=ya_send,
            recv_sem=ya_recv.at[part, k],
            device_id={"dp": place(lax.rem(y + step, ys), x_hi, core)},
            device_id_type=MESH,
        )

    def yf_copy(part, k, to):
        step = ys - 1 if k else 1
        come = lax.rem(y + ys - step, ys) * 2 + core
        far = lax.rem(y + 2, ys) * 2 + core
        half = pl.ds(k * (rows // 2), rows // 2)
        return pltpu.make_async_remote_copy(
            src_ref=dkv_all.at[come, part, half],
            dst_ref=dkv_all.at[come if to else far, part, half],
            send_sem=yf_send,
            recv_sem=yf_recv.at[part],
            device_id={"dp": place(lax.rem(y + step, ys), x_hi, core)},
            device_id_type=MESH,
        )

    def yc_copy(part, k, to):
        from_y = lax.rem(y + k, ys)
        return pltpu.make_async_remote_copy(
            src_ref=dkv_all.at[from_y * 2 + core, part],
            dst_ref=dkv_all.at[from_y * 2 + (core if to else 1 - core), part],
            send_sem=yc_send,
            recv_sem=yc_recv.at[part, k],
            device_id={"dp": place(y, x_hi, 1 - core)},
            device_id_type=MESH,
        )

    def rx_copy(part):
        return pltpu.make_async_remote_copy(
            src_ref=rx_s.at[part],
            dst_ref=rx_r.at[part],
            send_sem=rx_send,
            recv_sem=rx_recv.at[part],
            device_id=across,
            device_id_type=MESH,
        )

    def rs_copy(part, o):
        dest = peer(o)
        return pltpu.make_async_remote_copy(
            src_ref=rs_s.at[part, pl.ds(pl.multiple_of(dest * piece, piece), piece), :],
            dst_ref=rs_r.at[part, o],
            send_sem=rs_send,
            recv_sem=rs_recv.at[part],
            device_id={"grp": dest},
            device_id_type=MESH,
        )

    def settle(ref, sem):
        pltpu.make_async_copy(ref, ref, sem).wait()

    others = total - rows
    seven = pl.ds(0, group_size - 1)

    def own_q(h):
        return pltpu.make_async_copy(
            queries.at[:, cols(first_col(me) + h * HD, HD)],
            qd_r.at[h, 0, rows_of(me), :],
            in_recv.at[h, 0],
        )

    def own_do(h):
        return pltpu.make_async_copy(
            out_grad.at[:, cols(first_col(me) + h * HD, HD)],
            qd_r.at[h, 1, rows_of(me), :],
            in_recv.at[h, 1],
        )

    def send_head(h):
        each(1, group_size, lambda o: q_copy(h, o, True).start())
        each(1, group_size, lambda o: do_copy(h, o, True).start())

    load_hid.wait()
    load_kw.wait()
    hid_rows = hid_v[...]

    def project(weight, which):
        for g in range(0, KVH, 2):
            both = jnp.dot(
                hid_rows, weight[:, g * HD : (g + 2) * HD], preferred_element_type=FULL
            ).astype(LOW)
            kv_s[g, which] = both[:, :HD]
            kv_s[g + 1, which] = both[:, HD:]

    project(kw_v, 0)
    load_vw.wait()
    project(vw_v, 1)

    pl.semaphore_wait(barrier, column - 1 + group_size - 1 + 1)

    each(1, group_size, lambda o: kv_copy(o, True).start())
    each(0, heads, send_head)
    for h in range(heads):
        own_q(h).start()
        own_do(h).start()
    kv_r[:, rows_of(me), :] = kv_s[lax.rem(me, KVH)]

    lanes = 4 * piece

    def turn(t):
        turned = hid_v[:, cols(t * lanes, lanes)].T
        g = t // ys
        to_y = lax.rem(t, ys)
        for xh in range(2):
            at = pl.ds(pl.multiple_of((xh * group_size + g) * piece, piece), piece)
            for c in range(2):
                hid_s[to_y * 2 + c, at, :] = turned[(xh * 2 + c) * piece :][:piece]

    each(0, width // lanes, turn)
    each(1, column, lambda o: hid_copy(o, True).start())
    hid_t[y, :, cols(core * rows, rows)] = hid_s[y * 2 + core]

    row_ids = lax.broadcasted_iota(jnp.int32, (1, total), 1)
    begin = jnp.zeros((1, total), jnp.int32)
    for s in range(SLOTS):
        at, size = offsets[0, s], lengths[0, s]
        begin = jnp.where((row_ids >= at) & (row_ids < at + size), at, begin)
    begin_v[...] = begin
    starts = []
    for s in range(SLOTS):
        start = jnp.int32(0)
        for t in range(SLOTS):
            if t < s:
                before = groups[0, t] <= groups[0, s]
            else:
                before = groups[0, t] < groups[0, s]
            if t != s:
                start = start + jnp.where(before, lengths[0, t], 0)
        starts.append(start)

    def source_block(row):
        found = jnp.int32(0)
        for s in range(SLOTS):
            inside = (row >= starts[s]) & (row < starts[s] + lengths[0, s])
            found = found + jnp.where(inside, offsets[0, s] + row - starts[s], 0)
        return found // rows

    sources = [source_block(b * rows) for b in range(group_size)]

    acc[...] = jnp.zeros_like(acc)
    settle(kv_r.at[:, pl.ds(0, others), :], kv_recv)
    kt_v[...] = kv_r[0].T

    key_ids = lax.broadcasted_iota(jnp.int32, (HD, QBLK), 0)
    lane_ids = lax.broadcasted_iota(jnp.int32, (HD, QBLK), 1)

    def fold(tile):
        return tile.reshape(HD // 8, 8, QBLK)

    def span(b):
        first = sum((i + 1) * QBLK for i in range(b))
        return first, (b + 1) * QBLK

    def weigh(h, b):
        r0 = b * QBLK
        first, keys = span(b)
        q_blk = qd_r[h, 0, r0 : r0 + QBLK, :]
        begin_row = begin_v[:, r0 : r0 + QBLK]
        s_v[first : first + keys, :] = lax.dot_general(
            kv_r[0, 0:keys, :], q_blk, NT, preferred_element_type=FULL
        )
        top = jnp.full((8, QBLK), -1e30, FULL)
        for j in range(keys // HD):
            at = slice(first + j * HD, first + (j + 1) * HD)
            seen = key_ids + j * HD >= begin_row
            if j * HD >= r0:
                seen = seen & (key_ids + (j * HD - r0) <= lane_ids)
            tile = jnp.where(seen, s_v[at, :], -1e30)
            s_v[at, :] = tile
            top = jnp.maximum(top, jnp.max(fold(tile), axis=0))
        top = jnp.max(top, axis=0, keepdims=True)
        mass = jnp.zeros((8, QBLK), FULL)
        for j in range(keys // HD):
            at = slice(first + j * HD, first + (j + 1) * HD)
            tile = jnp.exp2((s_v[at, :] - top) * exp_scale)
            s_v[at, :] = tile
            mass = mass + jnp.sum(fold(tile), axis=0)
        inverse = 1.0 / jnp.sum(mass, axis=0, keepdims=True)
        for j in range(keys // HD):
            at = slice(first + j * HD, first + (j + 1) * HD)
            weights = s_v[at, :] * inverse
            s_v[at, :] = weights
            wl_v[at, :] = weights.astype(LOW)

    def attend(h, b):
        r0 = b * QBLK
        first, keys = span(b)
        q_blk = qd_r[h, 0, r0 : r0 + QBLK, :]
        do_blk = qd_r[h, 1, r0 : r0 + QBLK, :]
        pg_v[first : first + keys, :] = lax.dot_general(
            kv_r[1, 0:keys, :], do_blk, NT, preferred_element_type=FULL
        )
        delta = jnp.zeros((8, QBLK), FULL)
        for j in range(keys // HD):
            at = slice(first + j * HD, first + (j + 1) * HD)
            delta = delta + jnp.sum(fold(wl_v[at, :].astype(FULL) * pg_v[at, :]), axis=0)
        delta = jnp.sum(delta, axis=0, keepdims=True)
        for j in range(keys // HD):
            at = slice(first + j * HD, first + (j + 1) * HD)
            ds_v[at, :] = (s_v[at, :] * (pg_v[at, :] - delta)).astype(LOW)
        all_keys = slice(first, first + keys)
        acc[1, 0:keys, :] += jnp.dot(wl_v[all_keys, :], do_blk, preferred_element_type=FULL)
        acc[0, 0:keys, :] += jnp.dot(ds_v[all_keys, :], q_blk, preferred_element_type=FULL)
        grad_t = jnp.dot(kt_v[:, 0:keys], ds_v[all_keys, :], preferred_element_type=FULL)
        grad_rows = (grad_t * inv_root).T.astype(LOW)
        for j in range(per_block):
            dq_s[r0 // rows + j] = grad_rows[j * rows : (j + 1) * rows, :]

    def send_dq(h):
        each(1, group_size, lambda o: dq_copy(h, o, True).start())
        dq_stay(h).start()

    def one_head(h):
        settle(qd_r.at[h, 0], in_recv.at[h, 0])
        for b in reversed(range(blocks)):
            weigh(h, b)
        settle(qd_r.at[h, 1], in_recv.at[h, 1])

        @pl.when(h == heads - 1)
        def _():
            send_dq(0)

        for b in reversed(range(blocks)):
            attend(h, b)

            @pl.when(h == heads - 1)
            def _():
                for part in range(2):
                    for j in range(b * per_block, (b + 1) * per_block):
                        at = slice(j * rows, (j + 1) * rows)
                        term = acc[part, at, :]
                        if part == 0:
                            term = term * inv_root
                        dl_s[j, part] = term.astype(LOW)

                        @pl.when(me != j)
                        def _():
                            dl_copy(part, j).start()

        for b in range(group_size):
            dq_g[h, b * rows : (b + 1) * rows, :] = dq_s[sources[b]]

    each(0, heads, one_head)

    send_dq(1)
    dl_r[me] = dl_s[me]
    for b in range(group_size):
        dg_s[b] = dl_s[sources[b]]

    def merge(received, part, g):
        return (
            received[g, part].astype(FULL) + received[KVH + g, part].astype(FULL)
        ).astype(LOW)

    for part in range(PARTS):
        which = part * PCOLS // kvw
        if part * PCOLS % kvw == 0:
            settle(dl_r.at[seven, which], dl_recv.at[which])
        for i in range(PCOLS // HD):
            dkv_all[y * 2 + core, part, :, i * HD : (i + 1) * HD] = merge(
                dl_r, which, (part * PCOLS % kvw) // HD + i
            )
        for k in range(3 if part == PARTS - 1 else 2):
            ya_copy(part, k, True).start()
        yc_copy(part, 0, True).start()

    each(1, group_size, lambda o: dg_copy(o, True).start())
    each(2, heads, send_dq)
    settle(kv_r.at[:, pl.ds(0, others), :], kv_send)
    settle(qd_r.at[:, :, pl.ds(0, others), :], in_send)
    settle(hid_s.at[pl.ds(0, column - 1)], hid_send)

    settle(hid_s.at[pl.ds(0, column - 1)], hid_recv)
    def pass_on(part):
        for k in range(2):
            ya_copy(part, k, False).wait_recv()
            if part < PARTS - 1:
                yf_copy(part, k, True).start()
            yc_copy(part, 1 if k else ys - 1, True).start()

    def hand_far(part):
        if part < PARTS - 1:
            settle(dkv_all.at[0, part], yf_recv.at[part])
        else:
            ya_copy(part, 2, False).wait_recv()
        yc_copy(part, 2, True).start()

    def multiply(part):
        for k in (0, 1, ys - 1, 2):
            yc_copy(part, k, False).wait_recv()
            from_y = lax.rem(y + k, ys)
            grads = dkv_all[pl.ds(from_y * 2, 2), part].reshape(2 * rows, PCOLS)
            term = jnp.dot(hid_t[from_y], grads, preferred_element_type=FULL)
            if k > 0:
                term = prod[part] + term
            prod[part] = term
        rx_s[part] = prod[part, pl.ds((1 - x_hi) * half_rows, half_rows), :].astype(LOW)
        rx_copy(part).start()

    def combine(part):
        settle(rx_r.at[part], rx_recv.at[part])
        at = pl.ds(x_hi * half_rows, half_rows)
        both = prod[part, at, :] + rx_r[part].astype(FULL)
        prod[part, at, :] = both
        rs_s[part] = both.astype(LOW)
        each(1, group_size, lambda o: rs_copy(part, o).start())

    pass_on(0)
    for part in range(PARTS):
        if part + 1 < PARTS:
            pass_on(part + 1)
        hand_far(part)
        multiply(part)
        if part > 0:
            combine(part - 1)
    combine(PARTS - 1)

    dg_r[me] = dg_s[me]
    settle(dg_r.at[seven], dg_recv)
    dk_rows = jnp.concatenate([merge(dg_r, 0, g) for g in range(KVH)], axis=1)
    dv_rows = jnp.concatenate([merge(dg_r, 1, g) for g in range(KVH)], axis=1)

    def hidden_tile(t):
        at = pl.ds(pl.multiple_of(t * 512, 512), 512)
        tile = lax.dot_general(
            dk_rows, kw_v[at, :], NT, preferred_element_type=FULL
        ) + lax.dot_general(dv_rows, vw_v[at, :], NT, preferred_element_type=FULL)
        gh_v[:, at] = tile.astype(LOW)

    each(0, width // 512, hidden_tile)
    gh_out = pltpu.make_async_copy(gh_v, grad_hidden, gh_sem)
    gh_out.start()

    settle(dg_s.at[seven], dg_send)
    settle(dl_s.at[seven], dl_send)
    settle(dq_g.at[:, pl.ds(0, others), :], dq_send)
    settle(dq_g.at[:, pl.ds(0, others), :], dq_recv)
    settle(dq_g.at[:, pl.ds(0, rows), :], dq_own)
    settle(dkv_all.at[pl.ds(0, 2)], ya_send)
    settle(dkv_all.at[0, 0], ya_send)
    settle(dkv_all.at[0, pl.ds(0, PARTS - 1)], yf_send)
    settle(dkv_all.at[pl.ds(0, ys)], yc_send)

    norm = 1.0 / math.sqrt(total * replica_count)
    own = pl.ds(pl.multiple_of((x_hi * group_size + me) * piece, piece), piece)
    for part in range(PARTS):
        settle(rs_r.at[part, seven], rs_recv.at[part])
        summed = prod[part, own, :]
        for o in range(1, group_size):
            summed = summed + rs_r[part, o].astype(FULL)
        result = grad_value if part * PCOLS >= kvw else grad_key
        at = part * PCOLS % kvw
        result[:, at : at + PCOLS] = (summed * norm).astype(LOW)

    gh_out.wait()
    settle(rx_r, rx_send)
    settle(rs_r.at[:, seven], rs_send)


def hand_over(*refs):
    sources, results = refs[0:4], refs[4:8]
    held, sems = refs[8:12], refs[12]
    steps = []
    for i, (source, result, slot) in enumerate(zip(sources, results, held)):
        parts = 4 if i < 2 else 1
        size = source.shape[0] // parts
        for j in range(parts):
            at = pl.ds(j * size, size)
            steps.append(
                (
                    pltpu.make_async_copy(source.at[at], slot.at[at], sems.at[0, i, j]),
                    pltpu.make_async_copy(slot.at[at], result.at[at], sems.at[1, i, j]),
                )
            )
    for load, _ in steps:
        load.start()
    for load, store in steps:
        load.wait()
        store.start()
    for _, store in steps:
        store.wait()


def on_device(
    hidden, queries, out_grad, key_weight, value_weight, seq_lengths, seq_group, loader_offsets
):
    group_size = lax.axis_size("grp")
    replica_count = lax.axis_size("dp")
    rows, width = hidden.shape[1:]
    total = rows * group_size
    heads = HQ // group_size
    kvw = KVH * HD
    piece = width // (group_size * replica_count)
    blocks = total // QBLK
    ys = replica_count // 4
    column = 2 * ys
    chunk = width // column
    tall = sum((b + 1) * QBLK for b in range(blocks))
    dma = pltpu.SemaphoreType.DMA
    scratch = [
        pltpu.VMEM((rows, width), LOW),
        pltpu.VMEM((width, kvw), LOW),
        pltpu.VMEM((width, kvw), LOW),
        pltpu.VMEM((heads, 2, total, HD), LOW),
        pltpu.VMEM((KVH, 2, rows, HD), LOW),
        pltpu.VMEM((2, total, HD), LOW),
        pltpu.VMEM((HD, total), LOW),
        pltpu.VMEM((column, chunk, rows), LOW),
        pltpu.VMEM((ys, chunk, 2 * rows), LOW),
        pltpu.VMEM((tall, QBLK), FULL),
        pltpu.VMEM((tall, QBLK), FULL),
        pltpu.VMEM((tall, QBLK), LOW),
        pltpu.VMEM((tall, QBLK), LOW),
        pltpu.VMEM((2, total, HD), FULL),
        pltpu.VMEM((group_size, rows, HD), LOW),
        pltpu.VMEM((heads, total, HD), LOW),
        pltpu.VMEM((group_size, 2, rows, HD), LOW),
        pltpu.VMEM((group_size, 2, rows, HD), LOW),
        pltpu.VMEM((group_size, 2, rows, HD), LOW),
        pltpu.VMEM((group_size, 2, rows, HD), LOW),
        pltpu.VMEM((column, PARTS, rows, PCOLS), LOW),
        pltpu.VMEM((PARTS, chunk, PCOLS), FULL),
        pltpu.VMEM((PARTS, chunk // 2, PCOLS), LOW),
        pltpu.VMEM((PARTS, chunk // 2, PCOLS), LOW),
        pltpu.VMEM((PARTS, chunk // 2, PCOLS), LOW),
        pltpu.VMEM((PARTS, group_size, piece, PCOLS), LOW),
        pltpu.VMEM((rows, width), LOW),
        pltpu.VMEM((1, total), jnp.int32),
        dma((3,)),
        dma,
        dma((heads, 2)),
        dma,
        dma,
        dma,
        dma,
        dma,
        dma,
        dma,
        dma,
        dma((2,)),
        dma,
        dma,
        dma,
        dma((PARTS, 3)),
        dma,
        dma((PARTS - 1,)),
        dma,
        dma((PARTS, ys)),
        dma,
        dma((PARTS,)),
        dma,
        dma((PARTS,)),
        dma,
    ]
    smem = pl.BlockSpec(memory_space=pltpu.SMEM)
    vmem = pl.BlockSpec(memory_space=pltpu.VMEM)
    anywhere = pl.BlockSpec(memory_space=pl.ANY)

    def kernel(*refs):
        layer_kernel(group_size, replica_count, *refs)

    out_shape = (
        jax.ShapeDtypeStruct((rows, HQ * HD), LOW),
        jax.ShapeDtypeStruct((rows, width), LOW),
        jax.ShapeDtypeStruct((piece, kvw), LOW),
        jax.ShapeDtypeStruct((piece, kvw), LOW),
    )
    results = pl.pallas_call(
        kernel,
        out_shape=out_shape,
        in_specs=[smem, smem, smem] + [anywhere] * 5,
        out_specs=(anywhere, anywhere, vmem, vmem),
        scratch_shapes=scratch,
        compiler_params=pltpu.CompilerParams(
            collective_id=0, has_side_effects=True, vmem_limit_bytes=56 * 1024 * 1024
        ),
        name="layer",
    )(
        seq_lengths,
        seq_group,
        loader_offsets,
        hidden[0],
        queries[0],
        out_grad[0],
        key_weight,
        value_weight,
    )
    grad_query, grad_hidden, grad_key, grad_value = pl.pallas_call(
        hand_over,
        out_shape=out_shape,
        in_specs=[anywhere] * 4,
        out_specs=[anywhere] * 4,
        scratch_shapes=[pltpu.VMEM(shape.shape, LOW) for shape in out_shape] + [dma((2, 4, 4))],
        name="hand_over",
    )(*results)
    return (grad_query[None], grad_hidden[None], grad_key, grad_value)


def solution(mesh):
    placed = (
        P("dp", "grp", None),
        P("dp", "grp", None),
        P("dp", "grp", None),
        P(),
        P(),
        P("dp", None),
        P("dp", None),
        P("dp", None),
    )
    return jax.shard_map(
        on_device,
        mesh=mesh,
        in_specs=placed,
        out_specs=(
            P("dp", "grp", None),
            P("dp", "grp", None),
            P(("grp", "dp"), None),
            P(("grp", "dp"), None),
        ),
        check_vma=False,
    )
```

```python
import math

import jax
import jax.numpy as jnp
from jax import lax
from jax.experimental import pallas as pl
from jax.experimental.pallas import tpu as pltpu
from jax.sharding import PartitionSpec as P

HQ = 32
KVH = 4
HD = 128
SLOTS = 8
QBLK = 256
ZS = 4
PARTS = 4
PCOLS = 2 * KVH * HD // PARTS
LOW = jnp.bfloat16
FULL = jnp.float32
MESH = pl.DeviceIdType.MESH
NT = (((1,), (1,)), ((), ()))


def each(first, last, step):
    def body(i, carry):
        step(i)
        return carry

    lax.fori_loop(first, last, body, 0)


def layer_kernel(
    group_size,
    replica_count,
    lengths,
    groups,
    offsets,
    hidden,
    queries,
    out_grad,
    key_weight,
    value_weight,
    grad_query,
    grad_hidden,
    grad_key,
    grad_value,
    hid_v,
    kw_v,
    vw_v,
    qd_r,
    kv_s,
    kv_r,
    kt_v,
    hid_s,
    hid_t,
    s_v,
    pg_v,
    wl_v,
    ds_v,
    acc,
    dq_s,
    dq_g,
    dl_s,
    dl_r,
    dg_s,
    dg_r,
    dkv_all,
    prod,
    prod_s,
    rs_r,
    gh_v,
    begin_v,
    inv_v,
    load_sem,
    in_send,
    in_recv,
    kv_send,
    kv_recv,
    hid_send,
    hid_recv,
    dq_send,
    dq_recv,
    dq_own,
    dl_send,
    dl_recv,
    dg_send,
    dg_recv,
    ya_send,
    ya_recv,
    yf_send,
    yf_recv,
    yc_send,
    yc_recv,
    rs_send,
    rs_recv,
    gh_sem,
):
    me = lax.axis_index("grp")
    rep = lax.axis_index("dp")
    x_lo, z = me // ZS, lax.rem(me, ZS)
    y, x_hi, core = rep // 4, lax.rem(rep // 2, 2), lax.rem(rep, 2)
    ys = replica_count // 4
    column = 2 * ys
    summed_over = 2 * group_size
    rows = hidden.shape[0]
    width = hidden.shape[1]
    total = rows * group_size
    heads = HQ // group_size
    wide = heads * HD
    kvw = KVH * HD
    piece = width // (group_size * replica_count)
    inv_root = 1.0 / math.sqrt(HD)
    exp_scale = inv_root / math.log(2.0)
    blocks = total // QBLK
    per_block = QBLK // rows

    def peer(o):
        return lax.rem(x_lo + o // ZS, 2) * ZS + lax.rem(z + o, ZS)

    def origin(o):
        return lax.rem(x_lo + o // ZS, 2) * ZS + lax.rem(z - o + 2 * ZS, ZS)

    def place(at_y, at_x_hi, at_core):
        return (at_y * 2 + at_x_hi) * 2 + at_core

    def first_col(device):
        return lax.rem(device, KVH) * (2 * wide) + (device // KVH) * wide

    def rows_of(block):
        return pl.ds(pl.multiple_of(block * rows, rows), rows)

    def cols(at, n):
        return pl.ds(pl.multiple_of(at, n), n)

    load_hid = pltpu.make_async_copy(hidden, hid_v, load_sem.at[0])
    load_kw = pltpu.make_async_copy(key_weight, kw_v, load_sem.at[1])
    load_vw = pltpu.make_async_copy(value_weight, vw_v, load_sem.at[2])
    load_hid.start()
    load_kw.start()
    load_vw.start()

    barrier = pltpu.get_barrier_semaphore()

    def column_peer(o):
        return place(lax.rem(y + o // 2, ys), x_hi, lax.rem(core + o, 2))

    def column_origin(o):
        return lax.rem(y - o // 2 + ys, ys), lax.rem(core + o, 2)

    def sum_peer(o):
        return {
            "grp": peer(lax.rem(o, group_size)),
            "dp": place(y, lax.rem(x_hi + o // group_size, 2), core),
        }

    each(
        1,
        column,
        lambda o: pl.semaphore_signal(
            barrier, inc=1, device_id={"dp": column_peer(o)}, device_id_type=MESH
        ),
    )
    each(
        1,
        summed_over,
        lambda o: pl.semaphore_signal(
            barrier, inc=1, device_id=sum_peer(o), device_id_type=MESH
        ),
    )

    def q_copy(h, o, to):
        dest = peer(o)
        at = rows_of(me if to else origin(o))
        return pltpu.make_async_remote_copy(
            src_ref=queries.at[:, cols(first_col(dest) + h * HD, HD)],
            dst_ref=qd_r.at[h, 0, at, :],
            send_sem=in_send,
            recv_sem=in_recv.at[h, 0],
            device_id={"grp": dest},
            device_id_type=MESH,
        )

    def do_copy(h, o, to):
        dest = peer(o)
        at = rows_of(me if to else origin(o))
        return pltpu.make_async_remote_copy(
            src_ref=out_grad.at[:, cols(first_col(dest) + h * HD, HD)],
            dst_ref=qd_r.at[h, 1, at, :],
            send_sem=in_send,
            recv_sem=in_recv.at[h, 1],
            device_id={"grp": dest},
            device_id_type=MESH,
        )

    def kv_copy(o, to):
        dest = peer(o)
        at = rows_of(me if to else origin(o))
        return pltpu.make_async_remote_copy(
            src_ref=kv_s.at[lax.rem(dest, KVH)],
            dst_ref=kv_r.at[:, at, :],
            send_sem=kv_send,
            recv_sem=kv_recv,
            device_id={"grp": dest},
            device_id_type=MESH,
        )

    def hid_copy(o, to):
        dest_y, dest_core = lax.rem(y + o // 2, ys), lax.rem(core + o, 2)
        from_y, from_core = (y, core) if to else column_origin(o)
        return pltpu.make_async_remote_copy(
            src_ref=hid_s.at[dest_y * 2 + dest_core],
            dst_ref=hid_t.at[from_y, :, cols(from_core * rows, rows)],
            send_sem=hid_send,
            recv_sem=hid_recv,
            device_id={"dp": column_peer(o)},
            device_id_type=MESH,
        )

    def dq_copy(h, o, to):
        dest = peer(o)
        at = first_col(me if to else origin(o)) + h * HD
        return pltpu.make_async_remote_copy(
            src_ref=dq_g.at[h, rows_of(dest), :],
            dst_ref=grad_query.at[:, cols(at, HD)],
            send_sem=dq_send,
            recv_sem=dq_recv,
            device_id={"grp": dest},
            device_id_type=MESH,
        )

    def dq_stay(h):
        return pltpu.make_async_copy(
            dq_g.at[h, rows_of(me), :],
            grad_query.at[:, cols(first_col(me) + h * HD, HD)],
            dq_own,
        )

    def dl_copy(part, dest):
        return pltpu.make_async_remote_copy(
            src_ref=dl_s.at[dest, part],
            dst_ref=dl_r.at[me, part],
            send_sem=dl_send,
            recv_sem=dl_recv.at[part],
            device_id={"grp": dest},
            device_id_type=MESH,
        )

    def dg_copy(o, to):
        dest = peer(o)
        return pltpu.make_async_remote_copy(
            src_ref=dg_s.at[dest],
            dst_ref=dg_r.at[me if to else origin(o)],
            send_sem=dg_send,
            recv_sem=dg_recv,
            device_id={"grp": dest},
            device_id_type=MESH,
        )

    def ya_copy(part, k, to):
        step = (1, ys - 1, 2)[k]
        at = (y if to else lax.rem(y + ys - step, ys)) * 2 + core
        return pltpu.make_async_remote_copy(
            src_ref=dkv_all.at[y * 2 + core, part],
            dst_ref=dkv_all.at[at, part],
            send_sem=ya_send,
            recv_sem=ya_recv.at[part, k],
            device_id={"dp": place(lax.rem(y + step, ys), x_hi, core)},
            device_id_type=MESH,
        )

    def yf_copy(part, k, to):
        step = ys - 1 if k else 1
        come = lax.rem(y + ys - step, ys) * 2 + core
        far = lax.rem(y + 2, ys) * 2 + core
        half = pl.ds(k * (rows // 2), rows // 2)
        return pltpu.make_async_remote_copy(
            src_ref=dkv_all.at[come, part, half],
            dst_ref=dkv_all.at[come if to else far, part, half],
            send_sem=yf_send,
            recv_sem=yf_recv.at[part],
            device_id={"dp": place(lax.rem(y + step, ys), x_hi, core)},
            device_id_type=MESH,
        )

    def yc_copy(part, k, to):
        from_y = lax.rem(y + k, ys)
        return pltpu.make_async_remote_copy(
            src_ref=dkv_all.at[from_y * 2 + core, part],
            dst_ref=dkv_all.at[from_y * 2 + (core if to else 1 - core), part],
            send_sem=yc_send,
            recv_sem=yc_recv.at[part, k],
            device_id={"dp": place(y, x_hi, 1 - core)},
            device_id_type=MESH,
        )

    def rs_copy(part, o):
        dest = sum_peer(o)
        at = dest["grp"] * 2 + lax.rem(x_hi + o // group_size, 2)
        return pltpu.make_async_remote_copy(
            src_ref=prod_s.at[part, pl.ds(pl.multiple_of(at * piece, piece), piece), :],
            dst_ref=rs_r.at[part, o],
            send_sem=rs_send,
            recv_sem=rs_recv.at[part],
            device_id=dest,
            device_id_type=MESH,
        )

    def settle(ref, sem):
        pltpu.make_async_copy(ref, ref, sem).wait()

    others = total - rows
    seven = pl.ds(0, group_size - 1)

    def own_q(h):
        return pltpu.make_async_copy(
            queries.at[:, cols(first_col(me) + h * HD, HD)],
            qd_r.at[h, 0, rows_of(me), :],
            in_recv.at[h, 0],
        )

    def own_do(h):
        return pltpu.make_async_copy(
            out_grad.at[:, cols(first_col(me) + h * HD, HD)],
            qd_r.at[h, 1, rows_of(me), :],
            in_recv.at[h, 1],
        )

    def send_head(h):
        each(1, group_size, lambda o: q_copy(h, o, True).start())
        each(1, group_size, lambda o: do_copy(h, o, True).start())

    pl.semaphore_wait(barrier, column - 1 + summed_over - 1)
    send_head(0)

    load_hid.wait()
    load_kw.wait()
    hid_rows = hid_v[...]

    def project(weight, which):
        for g in range(0, KVH, 2):
            both = jnp.dot(
                hid_rows, weight[:, g * HD : (g + 2) * HD], preferred_element_type=FULL
            ).astype(LOW)
            kv_s[g, which] = both[:, :HD]
            kv_s[g + 1, which] = both[:, HD:]

    project(kw_v, 0)
    load_vw.wait()
    project(vw_v, 1)

    each(1, group_size, lambda o: kv_copy(o, True).start())
    each(1, heads, send_head)
    for h in range(heads):
        own_q(h).start()
        own_do(h).start()
    kv_r[:, rows_of(me), :] = kv_s[lax.rem(me, KVH)]

    lanes = 4 * piece

    def turn(t):
        turned = hid_v[:, cols(t * lanes, lanes)].T
        g = t // ys
        to_y = lax.rem(t, ys)
        for xh in range(2):
            at = pl.ds(pl.multiple_of((g * 2 + xh) * piece, piece), piece)
            for c in range(2):
                hid_s[to_y * 2 + c, at, :] = turned[(xh * 2 + c) * piece :][:piece]

    each(0, width // lanes, turn)
    each(1, column, lambda o: hid_copy(o, True).start())
    hid_t[y, :, cols(core * rows, rows)] = hid_s[y * 2 + core]

    row_ids = lax.broadcasted_iota(jnp.int32, (1, total), 1)
    begin = jnp.zeros((1, total), jnp.int32)
    for s in range(SLOTS):
        at, size = offsets[0, s], lengths[0, s]
        begin = jnp.where((row_ids >= at) & (row_ids < at + size), at, begin)
    begin_v[...] = begin
    starts = []
    for s in range(SLOTS):
        start = jnp.int32(0)
        for t in range(SLOTS):
            if t < s:
                before = groups[0, t] <= groups[0, s]
            else:
                before = groups[0, t] < groups[0, s]
            if t != s:
                start = start + jnp.where(before, lengths[0, t], 0)
        starts.append(start)

    def source_block(row):
        found = jnp.int32(0)
        for s in range(SLOTS):
            inside = (row >= starts[s]) & (row < starts[s] + lengths[0, s])
            found = found + jnp.where(inside, offsets[0, s] + row - starts[s], 0)
        return found // rows

    sources = [source_block(b * rows) for b in range(group_size)]

    acc[...] = jnp.zeros_like(acc)
    settle(kv_r.at[:, pl.ds(0, others), :], kv_recv)
    kt_v[...] = kv_r[0].T

    key_ids = lax.broadcasted_iota(jnp.int32, (HD, QBLK), 0)
    lane_ids = lax.broadcasted_iota(jnp.int32, (HD, QBLK), 1)

    def fold(tile):
        return tile.reshape(HD // 8, 8, QBLK)

    def span(b):
        first = sum((i + 1) * QBLK for i in range(b))
        return first, (b + 1) * QBLK

    def weigh(h, b):
        r0 = b * QBLK
        first, keys = span(b)
        q_blk = qd_r[h, 0, r0 : r0 + QBLK, :]
        begin_row = begin_v[:, r0 : r0 + QBLK]
        top = jnp.full((8, QBLK), -1e30, FULL)
        for j in range(0, keys, QBLK):
            block = lax.dot_general(
                kv_r[0, j : j + QBLK, :], q_blk, NT, preferred_element_type=FULL
            )
            for i in range(j, j + QBLK, HD):
                seen = key_ids + i >= begin_row
                if j >= r0:
                    seen = seen & (key_ids + (i - r0) <= lane_ids)
                tile = jnp.where(seen, block[i - j : i - j + HD], -1e30)
                s_v[first + i : first + i + HD, :] = tile
                top = jnp.maximum(top, jnp.max(fold(tile), axis=0))
        top = jnp.max(top, axis=0, keepdims=True)
        mass = jnp.zeros((8, QBLK), FULL)
        for j in range(keys // HD):
            at = slice(first + j * HD, first + (j + 1) * HD)
            tile = jnp.exp2((s_v[at, :] - top) * exp_scale)
            s_v[at, :] = tile
            mass = mass + jnp.sum(fold(tile), axis=0)
        inverse = 1.0 / jnp.sum(mass, axis=0, keepdims=True)
        inv_v[b : b + 1, :] = inverse
        for j in range(keys // HD):
            at = slice(first + j * HD, first + (j + 1) * HD)
            wl_v[at, :] = (s_v[at, :] * inverse).astype(LOW)

    def attend(h, b):
        r0 = b * QBLK
        first, keys = span(b)
        q_blk = qd_r[h, 0, r0 : r0 + QBLK, :]
        do_blk = qd_r[h, 1, r0 : r0 + QBLK, :]
        delta = jnp.zeros((8, QBLK), FULL)
        for j in range(0, keys, QBLK):
            at = slice(first + j, first + j + QBLK)
            block = lax.dot_general(
                kv_r[1, j : j + QBLK, :], do_blk, NT, preferred_element_type=FULL
            )
            pg_v[at, :] = block
            terms = wl_v[at, :].astype(FULL) * block
            delta = delta + jnp.sum(terms.reshape(QBLK // 8, 8, QBLK), axis=0)
        delta = jnp.sum(delta, axis=0, keepdims=True)
        inverse = inv_v[b : b + 1, :]
        for j in range(keys // HD):
            at = slice(first + j * HD, first + (j + 1) * HD)
            ds_v[at, :] = (s_v[at, :] * inverse * (pg_v[at, :] - delta)).astype(LOW)
        all_keys = slice(first, first + keys)
        acc[1, 0:keys, :] += jnp.dot(wl_v[all_keys, :], do_blk, preferred_element_type=FULL)
        acc[0, 0:keys, :] += jnp.dot(ds_v[all_keys, :], q_blk, preferred_element_type=FULL)

    def query_grad(b):
        r0 = b * QBLK
        first, keys = span(b)
        grad_t = jnp.dot(
            kt_v[:, 0:keys], ds_v[first : first + keys, :], preferred_element_type=FULL
        )
        grad_rows = (grad_t * inv_root).T.astype(LOW)
        for j in range(per_block):
            dq_s[r0 // rows + j] = grad_rows[j * rows : (j + 1) * rows, :]

    def send_dq(h):
        each(1, group_size, lambda o: dq_copy(h, o, True).start())
        dq_stay(h).start()

    def one_head(h):
        settle(qd_r.at[h, 0], in_recv.at[h, 0])
        for b in reversed(range(blocks)):
            weigh(h, b)
        settle(qd_r.at[h, 1], in_recv.at[h, 1])

        @pl.when(h == heads - 1)
        def _():
            send_dq(0)

        for b in reversed(range(blocks)):
            attend(h, b)

            @pl.when(h == heads - 1)
            def _():
                for part in range(2):
                    for j in range(b * per_block, (b + 1) * per_block):
                        at = slice(j * rows, (j + 1) * rows)
                        term = acc[part, at, :]
                        if part == 0:
                            term = term * inv_root
                        dl_s[j, part] = term.astype(LOW)

                        @pl.when(me != j)
                        def _():
                            dl_copy(part, j).start()

        for b in range(blocks):
            query_grad(b)
        for b in range(group_size):
            dq_g[h, b * rows : (b + 1) * rows, :] = dq_s[sources[b]]

    each(0, heads, one_head)

    dl_r[me] = dl_s[me]
    for b in range(group_size):
        dg_s[b] = dl_s[sources[b]]

    def merge(received, part, g):
        return (
            received[g, part].astype(FULL) + received[KVH + g, part].astype(FULL)
        ).astype(LOW)

    for part in range(PARTS):
        which = part * PCOLS // kvw
        if part * PCOLS % kvw == 0:
            settle(dl_r.at[seven, which], dl_recv.at[which])
        for i in range(PCOLS // HD):
            dkv_all[y * 2 + core, part, :, i * HD : (i + 1) * HD] = merge(
                dl_r, which, (part * PCOLS % kvw) // HD + i
            )
        for k in range(3 if part == PARTS - 1 else 2):
            ya_copy(part, k, True).start()
        yc_copy(part, 0, True).start()

    each(1, group_size, lambda o: dg_copy(o, True).start())
    each(1, heads, send_dq)
    settle(kv_r.at[:, pl.ds(0, others), :], kv_send)
    settle(qd_r.at[:, :, pl.ds(0, others), :], in_send)
    settle(hid_s.at[pl.ds(0, column - 1)], hid_send)

    settle(hid_s.at[pl.ds(0, column - 1)], hid_recv)
    def pass_on(part):
        for k in range(2):
            ya_copy(part, k, False).wait_recv()
            if part < PARTS - 1:
                yf_copy(part, k, True).start()
            yc_copy(part, 1 if k else ys - 1, True).start()

    def hand_far(part):
        if part < PARTS - 1:
            settle(dkv_all.at[0, part], yf_recv.at[part])
        else:
            ya_copy(part, 2, False).wait_recv()
        yc_copy(part, 2, True).start()

    def multiply(part):
        for k in (0, 1, ys - 1, 2):
            yc_copy(part, k, False).wait_recv()
            from_y = lax.rem(y + k, ys)
            grads = dkv_all[pl.ds(from_y * 2, 2), part].reshape(2 * rows, PCOLS)
            term = jnp.dot(hid_t[from_y], grads, preferred_element_type=FULL)
            if k > 0:
                term = prod[part] + term
            prod[part] = term
            if k == 2:
                prod_s[part] = term.astype(LOW)
        each(1, summed_over, lambda o: rs_copy(part, o).start())

    pass_on(0)
    for part in range(PARTS):
        if part + 1 < PARTS:
            pass_on(part + 1)
        hand_far(part)
        multiply(part)

    dg_r[me] = dg_s[me]
    settle(dg_r.at[seven], dg_recv)
    dk_rows = jnp.concatenate([merge(dg_r, 0, g) for g in range(KVH)], axis=1)
    dv_rows = jnp.concatenate([merge(dg_r, 1, g) for g in range(KVH)], axis=1)

    def hidden_tile(t):
        at = pl.ds(pl.multiple_of(t * 512, 512), 512)
        tile = lax.dot_general(
            dk_rows, kw_v[at, :], NT, preferred_element_type=FULL
        ) + lax.dot_general(dv_rows, vw_v[at, :], NT, preferred_element_type=FULL)
        gh_v[:, at] = tile.astype(LOW)

    each(0, width // 512, hidden_tile)
    gh_out = pltpu.make_async_copy(gh_v, grad_hidden, gh_sem)
    gh_out.start()

    settle(dg_s.at[seven], dg_send)
    settle(dl_s.at[seven], dl_send)
    settle(dq_g.at[:, pl.ds(0, others), :], dq_send)
    settle(dq_g.at[:, pl.ds(0, others), :], dq_recv)
    settle(dq_g.at[:, pl.ds(0, rows), :], dq_own)
    settle(dkv_all.at[pl.ds(0, 2)], ya_send)
    settle(dkv_all.at[0, 0], ya_send)
    settle(dkv_all.at[0, pl.ds(0, PARTS - 1)], yf_send)
    settle(dkv_all.at[pl.ds(0, ys)], yc_send)

    norm = 1.0 / math.sqrt(total * replica_count)
    own = pl.ds(pl.multiple_of((me * 2 + x_hi) * piece, piece), piece)
    for part in range(PARTS):
        settle(rs_r.at[part, pl.ds(0, summed_over - 1)], rs_recv.at[part])
        summed = prod[part, own, :]
        for o in range(1, summed_over):
            summed = summed + rs_r[part, o].astype(FULL)
        result = grad_value if part * PCOLS >= kvw else grad_key
        at = part * PCOLS % kvw
        result[:, at : at + PCOLS] = (summed * norm).astype(LOW)

    gh_out.wait()
    settle(rs_r.at[:, pl.ds(0, summed_over - 1)], rs_send)


def hand_over(*refs):
    sources, results = refs[0:4], refs[4:8]
    held, sems = refs[8:12], refs[12]
    steps = []
    for i, (source, result, slot) in enumerate(zip(sources, results, held)):
        parts = 4 if i < 2 else 1
        size = source.shape[0] // parts
        for j in range(parts):
            at = pl.ds(j * size, size)
            steps.append(
                (
                    pltpu.make_async_copy(source.at[at], slot.at[at], sems.at[0, i, j]),
                    pltpu.make_async_copy(slot.at[at], result.at[at], sems.at[1, i, j]),
                )
            )
    for load, _ in steps:
        load.start()
    for load, store in steps:
        load.wait()
        store.start()
    for _, store in steps:
        store.wait()


def on_device(
    hidden, queries, out_grad, key_weight, value_weight, seq_lengths, seq_group, loader_offsets
):
    group_size = lax.axis_size("grp")
    replica_count = lax.axis_size("dp")
    rows, width = hidden.shape[1:]
    total = rows * group_size
    heads = HQ // group_size
    kvw = KVH * HD
    piece = width // (group_size * replica_count)
    blocks = total // QBLK
    ys = replica_count // 4
    column = 2 * ys
    chunk = width // column
    tall = sum((b + 1) * QBLK for b in range(blocks))
    dma = pltpu.SemaphoreType.DMA
    scratch = [
        pltpu.VMEM((rows, width), LOW),
        pltpu.VMEM((width, kvw), LOW),
        pltpu.VMEM((width, kvw), LOW),
        pltpu.VMEM((heads, 2, total, HD), LOW),
        pltpu.VMEM((KVH, 2, rows, HD), LOW),
        pltpu.VMEM((2, total, HD), LOW),
        pltpu.VMEM((HD, total), LOW),
        pltpu.VMEM((column, chunk, rows), LOW),
        pltpu.VMEM((ys, chunk, 2 * rows), LOW),
        pltpu.VMEM((tall, QBLK), FULL),
        pltpu.VMEM((tall, QBLK), FULL),
        pltpu.VMEM((tall, QBLK), LOW),
        pltpu.VMEM((tall, QBLK), LOW),
        pltpu.VMEM((2, total, HD), FULL),
        pltpu.VMEM((group_size, rows, HD), LOW),
        pltpu.VMEM((heads, total, HD), LOW),
        pltpu.VMEM((group_size, 2, rows, HD), LOW),
        pltpu.VMEM((group_size, 2, rows, HD), LOW),
        pltpu.VMEM((group_size, 2, rows, HD), LOW),
        pltpu.VMEM((group_size, 2, rows, HD), LOW),
        pltpu.VMEM((column, PARTS, rows, PCOLS), LOW),
        pltpu.VMEM((PARTS, chunk, PCOLS), FULL),
        pltpu.VMEM((PARTS, chunk, PCOLS), LOW),
        pltpu.VMEM((PARTS, 2 * group_size, piece, PCOLS), LOW),
        pltpu.VMEM((rows, width), LOW),
        pltpu.VMEM((1, total), jnp.int32),
        pltpu.VMEM((8, QBLK), FULL),
        dma((3,)),
        dma,
        dma((heads, 2)),
        dma,
        dma,
        dma,
        dma,
        dma,
        dma,
        dma,
        dma,
        dma((2,)),
        dma,
        dma,
        dma,
        dma((PARTS, 3)),
        dma,
        dma((PARTS - 1,)),
        dma,
        dma((PARTS, ys)),
        dma,
        dma((PARTS,)),
        dma,
    ]
    smem = pl.BlockSpec(memory_space=pltpu.SMEM)
    vmem = pl.BlockSpec(memory_space=pltpu.VMEM)
    anywhere = pl.BlockSpec(memory_space=pl.ANY)

    def kernel(*refs):
        layer_kernel(group_size, replica_count, *refs)

    out_shape = (
        jax.ShapeDtypeStruct((rows, HQ * HD), LOW),
        jax.ShapeDtypeStruct((rows, width), LOW),
        jax.ShapeDtypeStruct((piece, kvw), LOW),
        jax.ShapeDtypeStruct((piece, kvw), LOW),
    )
    results = pl.pallas_call(
        kernel,
        out_shape=out_shape,
        in_specs=[smem, smem, smem] + [anywhere] * 5,
        out_specs=(anywhere, anywhere, vmem, vmem),
        scratch_shapes=scratch,
        compiler_params=pltpu.CompilerParams(
            collective_id=0, has_side_effects=True, vmem_limit_bytes=56 * 1024 * 1024
        ),
        name="layer",
    )(
        seq_lengths,
        seq_group,
        loader_offsets,
        hidden[0],
        queries[0],
        out_grad[0],
        key_weight,
        value_weight,
    )
    grad_query, grad_hidden, grad_key, grad_value = pl.pallas_call(
        hand_over,
        out_shape=out_shape,
        in_specs=[anywhere] * 4,
        out_specs=[anywhere] * 4,
        scratch_shapes=[pltpu.VMEM(shape.shape, LOW) for shape in out_shape] + [dma((2, 4, 4))],
        name="hand_over",
    )(*results)
    return (grad_query[None], grad_hidden[None], grad_key, grad_value)


def solution(mesh):
    placed = (
        P("dp", "grp", None),
        P("dp", "grp", None),
        P("dp", "grp", None),
        P(),
        P(),
        P("dp", None),
        P("dp", None),
        P("dp", None),
    )
    return jax.shard_map(
        on_device,
        mesh=mesh,
        in_specs=placed,
        out_specs=(
            P("dp", "grp", None),
            P("dp", "grp", None),
            P(("grp", "dp"), None),
            P(("grp", "dp"), None),
        ),
        check_vma=False,
    )
```

```python
import math

import jax
import jax.numpy as jnp
from jax import lax
from jax.experimental import pallas as pl
from jax.experimental.pallas import tpu as pltpu
from jax.sharding import PartitionSpec as P

HQ = 32
KVH = 4
HD = 128
SLOTS = 8
QBLK = 256
ZS = 4
PARTS = 4
PCOLS = 2 * KVH * HD // PARTS
ORDER = (2, 3, 0, 1)
LOW = jnp.bfloat16
FULL = jnp.float32
MESH = pl.DeviceIdType.MESH
NT = (((1,), (1,)), ((), ()))


def each(first, last, step):
    def body(i, carry):
        step(i)
        return carry

    lax.fori_loop(first, last, body, 0)


def layer_kernel(
    group_size,
    replica_count,
    lengths,
    groups,
    offsets,
    hidden,
    queries,
    out_grad,
    key_weight,
    value_weight,
    grad_query,
    grad_hidden,
    grad_key,
    grad_value,
    hid_v,
    kw_v,
    vw_v,
    qd_r,
    kv_s,
    kv_r,
    kt_v,
    hid_s,
    hid_t,
    s_v,
    pg_v,
    wl_v,
    ds_v,
    acc,
    dq_s,
    dq_g,
    dl_s,
    dl_r,
    dg_s,
    dg_r,
    dkv_all,
    prod,
    prod_s,
    rs_r,
    gh_v,
    begin_v,
    inv_v,
    load_sem,
    in_send,
    in_recv,
    kv_send,
    kv_recv,
    hid_send,
    hid_recv,
    dq_send,
    dq_recv,
    dq_own,
    dl_send,
    dl_recv,
    dg_send,
    dg_recv,
    ya_send,
    ya_recv,
    yf_send,
    yf_recv,
    yc_send,
    yc_recv,
    rs_send,
    rs_recv,
    gh_sem,
):
    me = lax.axis_index("grp")
    rep = lax.axis_index("dp")
    x_lo, z = me // ZS, lax.rem(me, ZS)
    y, x_hi, core = rep // 4, lax.rem(rep // 2, 2), lax.rem(rep, 2)
    ys = replica_count // 4
    column = 2 * ys
    summed_over = 2 * group_size
    rows = hidden.shape[0]
    width = hidden.shape[1]
    total = rows * group_size
    heads = HQ // group_size
    wide = heads * HD
    kvw = KVH * HD
    piece = width // (group_size * replica_count)
    inv_root = 1.0 / math.sqrt(HD)
    exp_scale = inv_root / math.log(2.0)
    blocks = total // QBLK
    per_block = QBLK // rows

    def peer(o):
        return lax.rem(x_lo + o // ZS, 2) * ZS + lax.rem(z + o, ZS)

    def origin(o):
        return lax.rem(x_lo + o // ZS, 2) * ZS + lax.rem(z - o + 2 * ZS, ZS)

    def place(at_y, at_x_hi, at_core):
        return (at_y * 2 + at_x_hi) * 2 + at_core

    def first_col(device):
        return lax.rem(device, KVH) * (2 * wide) + (device // KVH) * wide

    def rows_of(block):
        return pl.ds(pl.multiple_of(block * rows, rows), rows)

    def cols(at, n):
        return pl.ds(pl.multiple_of(at, n), n)

    load_hid = pltpu.make_async_copy(hidden, hid_v, load_sem.at[0])
    load_kw = pltpu.make_async_copy(key_weight, kw_v, load_sem.at[1])
    load_vw = pltpu.make_async_copy(value_weight, vw_v, load_sem.at[2])
    load_hid.start()
    load_kw.start()
    load_vw.start()

    barrier = pltpu.get_barrier_semaphore()

    def column_peer(o):
        return place(lax.rem(y + o // 2, ys), x_hi, lax.rem(core + o, 2))

    def column_origin(o):
        return lax.rem(y - o // 2 + ys, ys), lax.rem(core + o, 2)

    def sum_peer(o):
        return {
            "grp": peer(lax.rem(o, group_size)),
            "dp": place(y, lax.rem(x_hi + o // group_size, 2), core),
        }

    each(
        1,
        column,
        lambda o: pl.semaphore_signal(
            barrier, inc=1, device_id={"dp": column_peer(o)}, device_id_type=MESH
        ),
    )
    each(
        1,
        summed_over,
        lambda o: pl.semaphore_signal(
            barrier, inc=1, device_id=sum_peer(o), device_id_type=MESH
        ),
    )

    def q_copy(h, o, to):
        dest = peer(o)
        at = rows_of(me if to else origin(o))
        return pltpu.make_async_remote_copy(
            src_ref=queries.at[:, cols(first_col(dest) + h * HD, HD)],
            dst_ref=qd_r.at[h, 0, at, :],
            send_sem=in_send,
            recv_sem=in_recv.at[h, 0],
            device_id={"grp": dest},
            device_id_type=MESH,
        )

    def do_copy(h, o, to):
        dest = peer(o)
        at = rows_of(me if to else origin(o))
        return pltpu.make_async_remote_copy(
            src_ref=out_grad.at[:, cols(first_col(dest) + h * HD, HD)],
            dst_ref=qd_r.at[h, 1, at, :],
            send_sem=in_send,
            recv_sem=in_recv.at[h, 1],
            device_id={"grp": dest},
            device_id_type=MESH,
        )

    def kv_copy(o, to):
        dest = peer(o)
        at = rows_of(me if to else origin(o))
        return pltpu.make_async_remote_copy(
            src_ref=kv_s.at[lax.rem(dest, KVH)],
            dst_ref=kv_r.at[:, at, :],
            send_sem=kv_send,
            recv_sem=kv_recv,
            device_id={"grp": dest},
            device_id_type=MESH,
        )

    def hid_copy(o, to):
        dest_y, dest_core = lax.rem(y + o // 2, ys), lax.rem(core + o, 2)
        from_y, from_core = (y, core) if to else column_origin(o)
        return pltpu.make_async_remote_copy(
            src_ref=hid_s.at[dest_y * 2 + dest_core],
            dst_ref=hid_t.at[from_y, :, cols(from_core * rows, rows)],
            send_sem=hid_send,
            recv_sem=hid_recv,
            device_id={"dp": column_peer(o)},
            device_id_type=MESH,
        )

    def dq_copy(h, o, to):
        dest = peer(o)
        at = first_col(me if to else origin(o)) + h * HD
        return pltpu.make_async_remote_copy(
            src_ref=dq_g.at[h, rows_of(dest), :],
            dst_ref=grad_query.at[:, cols(at, HD)],
            send_sem=dq_send,
            recv_sem=dq_recv,
            device_id={"grp": dest},
            device_id_type=MESH,
        )

    def dq_stay(h):
        return pltpu.make_async_copy(
            dq_g.at[h, rows_of(me), :],
            grad_query.at[:, cols(first_col(me) + h * HD, HD)],
            dq_own,
        )

    def dl_copy(part, dest):
        return pltpu.make_async_remote_copy(
            src_ref=dl_s.at[dest, part],
            dst_ref=dl_r.at[me, part],
            send_sem=dl_send,
            recv_sem=dl_recv.at[part],
            device_id={"grp": dest},
            device_id_type=MESH,
        )

    def dg_copy(o, to):
        dest = peer(o)
        return pltpu.make_async_remote_copy(
            src_ref=dg_s.at[dest],
            dst_ref=dg_r.at[me if to else origin(o)],
            send_sem=dg_send,
            recv_sem=dg_recv,
            device_id={"grp": dest},
            device_id_type=MESH,
        )

    def ya_copy(part, k, to):
        step = (1, ys - 1, 2)[k]
        at = (y if to else lax.rem(y + ys - step, ys)) * 2 + core
        return pltpu.make_async_remote_copy(
            src_ref=dkv_all.at[y * 2 + core, part],
            dst_ref=dkv_all.at[at, part],
            send_sem=ya_send,
            recv_sem=ya_recv.at[part, k],
            device_id={"dp": place(lax.rem(y + step, ys), x_hi, core)},
            device_id_type=MESH,
        )

    def yf_copy(part, k, to):
        step = ys - 1 if k else 1
        come = lax.rem(y + ys - step, ys) * 2 + core
        far = lax.rem(y + 2, ys) * 2 + core
        half = pl.ds(k * (rows // 2), rows // 2)
        return pltpu.make_async_remote_copy(
            src_ref=dkv_all.at[come, part, half],
            dst_ref=dkv_all.at[come if to else far, part, half],
            send_sem=yf_send,
            recv_sem=yf_recv.at[part],
            device_id={"dp": place(lax.rem(y + step, ys), x_hi, core)},
            device_id_type=MESH,
        )

    def yc_copy(part, k, to):
        from_y = lax.rem(y + k, ys)
        return pltpu.make_async_remote_copy(
            src_ref=dkv_all.at[from_y * 2 + core, part],
            dst_ref=dkv_all.at[from_y * 2 + (core if to else 1 - core), part],
            send_sem=yc_send,
            recv_sem=yc_recv.at[part, k],
            device_id={"dp": place(y, x_hi, 1 - core)},
            device_id_type=MESH,
        )

    def rs_copy(part, o):
        dest = sum_peer(o)
        at = dest["grp"] * 2 + lax.rem(x_hi + o // group_size, 2)
        return pltpu.make_async_remote_copy(
            src_ref=prod_s.at[part, pl.ds(pl.multiple_of(at * piece, piece), piece), :],
            dst_ref=rs_r.at[part, o],
            send_sem=rs_send,
            recv_sem=rs_recv.at[part],
            device_id=dest,
            device_id_type=MESH,
        )

    def settle(ref, sem):
        pltpu.make_async_copy(ref, ref, sem).wait()

    others = total - rows
    seven = pl.ds(0, group_size - 1)

    def own_q(h):
        return pltpu.make_async_copy(
            queries.at[:, cols(first_col(me) + h * HD, HD)],
            qd_r.at[h, 0, rows_of(me), :],
            in_recv.at[h, 0],
        )

    def own_do(h):
        return pltpu.make_async_copy(
            out_grad.at[:, cols(first_col(me) + h * HD, HD)],
            qd_r.at[h, 1, rows_of(me), :],
            in_recv.at[h, 1],
        )

    def send_head(h):
        each(1, group_size, lambda o: q_copy(h, o, True).start())
        each(1, group_size, lambda o: do_copy(h, o, True).start())

    pl.semaphore_wait(barrier, column - 1 + summed_over - 1)
    send_head(0)

    load_hid.wait()
    load_kw.wait()
    hid_rows = hid_v[...]

    def project(weight, which):
        for g in range(0, KVH, 2):
            both = jnp.dot(
                hid_rows, weight[:, g * HD : (g + 2) * HD], preferred_element_type=FULL
            ).astype(LOW)
            kv_s[g, which] = both[:, :HD]
            kv_s[g + 1, which] = both[:, HD:]

    project(kw_v, 0)
    load_vw.wait()
    project(vw_v, 1)

    each(1, group_size, lambda o: kv_copy(o, True).start())
    each(1, heads, send_head)
    for h in range(heads):
        own_q(h).start()
        own_do(h).start()
    kv_r[:, rows_of(me), :] = kv_s[lax.rem(me, KVH)]

    lanes = 4 * piece

    def turn(t):
        turned = hid_v[:, cols(t * lanes, lanes)].T
        g = t // ys
        to_y = lax.rem(t, ys)
        for xh in range(2):
            at = pl.ds(pl.multiple_of((g * 2 + xh) * piece, piece), piece)
            for c in range(2):
                hid_s[to_y * 2 + c, at, :] = turned[(xh * 2 + c) * piece :][:piece]

    each(0, width // lanes, turn)
    each(1, column, lambda o: hid_copy(o, True).start())
    hid_t[y, :, cols(core * rows, rows)] = hid_s[y * 2 + core]

    row_ids = lax.broadcasted_iota(jnp.int32, (1, total), 1)
    begin = jnp.zeros((1, total), jnp.int32)
    for s in range(SLOTS):
        at, size = offsets[0, s], lengths[0, s]
        begin = jnp.where((row_ids >= at) & (row_ids < at + size), at, begin)
    begin_v[...] = begin
    starts = []
    for s in range(SLOTS):
        start = jnp.int32(0)
        for t in range(SLOTS):
            if t < s:
                before = groups[0, t] <= groups[0, s]
            else:
                before = groups[0, t] < groups[0, s]
            if t != s:
                start = start + jnp.where(before, lengths[0, t], 0)
        starts.append(start)

    def source_block(row):
        found = jnp.int32(0)
        for s in range(SLOTS):
            inside = (row >= starts[s]) & (row < starts[s] + lengths[0, s])
            found = found + jnp.where(inside, offsets[0, s] + row - starts[s], 0)
        return found // rows

    sources = [source_block(b * rows) for b in range(group_size)]

    acc[...] = jnp.zeros_like(acc)
    settle(kv_r.at[:, pl.ds(0, others), :], kv_recv)
    kt_v[...] = kv_r[0].T

    key_ids = lax.broadcasted_iota(jnp.int32, (HD, QBLK), 0)
    lane_ids = lax.broadcasted_iota(jnp.int32, (HD, QBLK), 1)

    def fold(tile):
        return tile.reshape(HD // 8, 8, QBLK)

    def span(b):
        first = sum((i + 1) * QBLK for i in range(b))
        return first, (b + 1) * QBLK

    def weigh(h, b):
        r0 = b * QBLK
        first, keys = span(b)
        q_blk = qd_r[h, 0, r0 : r0 + QBLK, :]
        begin_row = begin_v[:, r0 : r0 + QBLK]
        top = jnp.full((8, QBLK), -1e30, FULL)
        for j in range(0, keys, QBLK):
            block = lax.dot_general(
                kv_r[0, j : j + QBLK, :], q_blk, NT, preferred_element_type=FULL
            )
            for i in range(j, j + QBLK, HD):
                seen = key_ids + i >= begin_row
                if j >= r0:
                    seen = seen & (key_ids + (i - r0) <= lane_ids)
                tile = jnp.where(seen, block[i - j : i - j + HD], -1e30)
                s_v[first + i : first + i + HD, :] = tile
                top = jnp.maximum(top, jnp.max(fold(tile), axis=0))
        top = jnp.max(top, axis=0, keepdims=True)
        mass = jnp.zeros((8, QBLK), FULL)
        for j in range(keys // HD):
            at = slice(first + j * HD, first + (j + 1) * HD)
            tile = jnp.exp2((s_v[at, :] - top) * exp_scale)
            s_v[at, :] = tile
            mass = mass + jnp.sum(fold(tile), axis=0)
        inverse = 1.0 / jnp.sum(mass, axis=0, keepdims=True)
        inv_v[b : b + 1, :] = inverse
        for j in range(keys // HD):
            at = slice(first + j * HD, first + (j + 1) * HD)
            wl_v[at, :] = (s_v[at, :] * inverse).astype(LOW)

    def value_grad(h, b):
        r0 = b * QBLK
        first, keys = span(b)
        acc[1, 0:keys, :] += jnp.dot(
            wl_v[first : first + keys, :],
            qd_r[h, 1, r0 : r0 + QBLK, :],
            preferred_element_type=FULL,
        )

    def send_terms(part, first_block, last_block):
        for j in range(first_block, last_block):
            term = acc[part, j * rows : (j + 1) * rows, :]
            if part == 0:
                term = term * inv_root
            dl_s[j, part] = term.astype(LOW)

            @pl.when(me != j)
            def _():
                dl_copy(part, j).start()

    def attend(h, b):
        r0 = b * QBLK
        first, keys = span(b)
        q_blk = qd_r[h, 0, r0 : r0 + QBLK, :]
        do_blk = qd_r[h, 1, r0 : r0 + QBLK, :]
        delta = jnp.zeros((8, QBLK), FULL)
        for j in range(0, keys, QBLK):
            at = slice(first + j, first + j + QBLK)
            block = lax.dot_general(
                kv_r[1, j : j + QBLK, :], do_blk, NT, preferred_element_type=FULL
            )
            pg_v[at, :] = block
            terms = wl_v[at, :].astype(FULL) * block
            delta = delta + jnp.sum(terms.reshape(QBLK // 8, 8, QBLK), axis=0)
        delta = jnp.sum(delta, axis=0, keepdims=True)
        inverse = inv_v[b : b + 1, :]
        for j in range(keys // HD):
            at = slice(first + j * HD, first + (j + 1) * HD)
            ds_v[at, :] = (s_v[at, :] * inverse * (pg_v[at, :] - delta)).astype(LOW)
        all_keys = slice(first, first + keys)
        acc[0, 0:keys, :] += jnp.dot(ds_v[all_keys, :], q_blk, preferred_element_type=FULL)

    def query_grad(b):
        r0 = b * QBLK
        first, keys = span(b)
        grad_t = jnp.dot(
            kt_v[:, 0:keys], ds_v[first : first + keys, :], preferred_element_type=FULL
        )
        grad_rows = (grad_t * inv_root).T.astype(LOW)
        for j in range(per_block):
            dq_s[r0 // rows + j] = grad_rows[j * rows : (j + 1) * rows, :]

    def send_dq(h):
        each(1, group_size, lambda o: dq_copy(h, o, True).start())
        dq_stay(h).start()

    def one_head(h):
        settle(qd_r.at[h, 0], in_recv.at[h, 0])
        for b in reversed(range(blocks)):
            weigh(h, b)
        settle(qd_r.at[h, 1], in_recv.at[h, 1])

        for b in reversed(range(blocks)):
            value_grad(h, b)

        @pl.when(h == heads - 1)
        def _():
            send_terms(1, 0, group_size)
            send_dq(0)

        for b in reversed(range(blocks)):
            attend(h, b)

            @pl.when(h == heads - 1)
            def _():
                send_terms(0, b * per_block, (b + 1) * per_block)

        for b in range(blocks):
            query_grad(b)
        for b in range(group_size):
            dq_g[h, b * rows : (b + 1) * rows, :] = dq_s[sources[b]]

    each(0, heads, one_head)

    dl_r[me] = dl_s[me]

    def merge(received, part, g):
        return (
            received[g, part].astype(FULL) + received[KVH + g, part].astype(FULL)
        ).astype(LOW)

    last = ORDER[-1]

    def gather(part):
        which = part * PCOLS // kvw
        for i in range(PCOLS // HD):
            dkv_all[y * 2 + core, part, :, i * HD : (i + 1) * HD] = merge(
                dl_r, which, (part * PCOLS % kvw) // HD + i
            )
        for k in range(3 if part == last else 2):
            ya_copy(part, k, True).start()
        yc_copy(part, 0, True).start()

    settle(dl_r.at[seven, 1], dl_recv.at[1])
    for part in ORDER[: PARTS // 2]:
        gather(part)
    send_dq(1)
    for b in range(group_size):
        dg_s[b] = dl_s[sources[b]]
    settle(dl_r.at[seven, 0], dl_recv.at[0])
    for part in ORDER[PARTS // 2 :]:
        gather(part)

    each(1, group_size, lambda o: dg_copy(o, True).start())
    settle(kv_r.at[:, pl.ds(0, others), :], kv_send)
    settle(qd_r.at[:, :, pl.ds(0, others), :], in_send)
    settle(hid_s.at[pl.ds(0, column - 1)], hid_send)

    settle(hid_s.at[pl.ds(0, column - 1)], hid_recv)
    def pass_on(part):
        for k in range(2):
            ya_copy(part, k, False).wait_recv()
            if part != last:
                yf_copy(part, k, True).start()
            yc_copy(part, 1 if k else ys - 1, True).start()

    def hand_far(part):
        if part != last:
            settle(dkv_all.at[0, part], yf_recv.at[part])
        else:
            ya_copy(part, 2, False).wait_recv()
        yc_copy(part, 2, True).start()

    def multiply(part):
        for k in (0, 1, ys - 1, 2):
            yc_copy(part, k, False).wait_recv()
            from_y = lax.rem(y + k, ys)
            grads = dkv_all[pl.ds(from_y * 2, 2), part].reshape(2 * rows, PCOLS)
            term = jnp.dot(hid_t[from_y], grads, preferred_element_type=FULL)
            if k > 0:
                term = prod[part] + term
            prod[part] = term
            if k == 2:
                prod_s[part] = term.astype(LOW)
        each(1, summed_over, lambda o: rs_copy(part, o).start())

    pass_on(ORDER[0])
    for i, part in enumerate(ORDER):
        if i + 1 < PARTS:
            pass_on(ORDER[i + 1])
        hand_far(part)
        multiply(part)
        if i + 2 < heads:
            send_dq(i + 2)

    dg_r[me] = dg_s[me]
    settle(dg_r.at[seven], dg_recv)
    dk_rows = jnp.concatenate([merge(dg_r, 0, g) for g in range(KVH)], axis=1)
    dv_rows = jnp.concatenate([merge(dg_r, 1, g) for g in range(KVH)], axis=1)

    def hidden_tile(t):
        at = pl.ds(pl.multiple_of(t * 512, 512), 512)
        tile = lax.dot_general(
            dk_rows, kw_v[at, :], NT, preferred_element_type=FULL
        ) + lax.dot_general(dv_rows, vw_v[at, :], NT, preferred_element_type=FULL)
        gh_v[:, at] = tile.astype(LOW)

    each(0, width // 512, hidden_tile)
    gh_out = pltpu.make_async_copy(gh_v, grad_hidden, gh_sem)
    gh_out.start()

    settle(dg_s.at[seven], dg_send)
    settle(dl_s.at[seven], dl_send)
    settle(dq_g.at[:, pl.ds(0, others), :], dq_send)
    settle(dq_g.at[:, pl.ds(0, others), :], dq_recv)
    settle(dq_g.at[:, pl.ds(0, rows), :], dq_own)
    settle(dkv_all.at[pl.ds(0, 2)], ya_send)
    settle(dkv_all.at[0, 0], ya_send)
    settle(dkv_all.at[0, pl.ds(0, PARTS - 1)], yf_send)
    settle(dkv_all.at[pl.ds(0, ys)], yc_send)

    norm = 1.0 / math.sqrt(total * replica_count)
    own = pl.ds(pl.multiple_of((me * 2 + x_hi) * piece, piece), piece)
    for part in ORDER:
        settle(rs_r.at[part, pl.ds(0, summed_over - 1)], rs_recv.at[part])
        summed = prod[part, own, :]
        for o in range(1, summed_over):
            summed = summed + rs_r[part, o].astype(FULL)
        result = grad_value if part * PCOLS >= kvw else grad_key
        at = part * PCOLS % kvw
        result[:, at : at + PCOLS] = (summed * norm).astype(LOW)

    gh_out.wait()
    settle(rs_r.at[:, pl.ds(0, summed_over - 1)], rs_send)


def hand_over(*refs):
    sources, results = refs[0:4], refs[4:8]
    held, sems = refs[8:12], refs[12]
    steps = []
    for i, (source, result, slot) in enumerate(zip(sources, results, held)):
        parts = 4 if i < 2 else 1
        size = source.shape[0] // parts
        for j in range(parts):
            at = pl.ds(j * size, size)
            steps.append(
                (
                    pltpu.make_async_copy(source.at[at], slot.at[at], sems.at[0, i, j]),
                    pltpu.make_async_copy(slot.at[at], result.at[at], sems.at[1, i, j]),
                )
            )
    for load, _ in steps:
        load.start()
    for load, store in steps:
        load.wait()
        store.start()
    for _, store in steps:
        store.wait()


def on_device(
    hidden, queries, out_grad, key_weight, value_weight, seq_lengths, seq_group, loader_offsets
):
    group_size = lax.axis_size("grp")
    replica_count = lax.axis_size("dp")
    rows, width = hidden.shape[1:]
    total = rows * group_size
    heads = HQ // group_size
    kvw = KVH * HD
    piece = width // (group_size * replica_count)
    blocks = total // QBLK
    ys = replica_count // 4
    column = 2 * ys
    chunk = width // column
    tall = sum((b + 1) * QBLK for b in range(blocks))
    dma = pltpu.SemaphoreType.DMA
    scratch = [
        pltpu.VMEM((rows, width), LOW),
        pltpu.VMEM((width, kvw), LOW),
        pltpu.VMEM((width, kvw), LOW),
        pltpu.VMEM((heads, 2, total, HD), LOW),
        pltpu.VMEM((KVH, 2, rows, HD), LOW),
        pltpu.VMEM((2, total, HD), LOW),
        pltpu.VMEM((HD, total), LOW),
        pltpu.VMEM((column, chunk, rows), LOW),
        pltpu.VMEM((ys, chunk, 2 * rows), LOW),
        pltpu.VMEM((tall, QBLK), FULL),
        pltpu.VMEM((tall, QBLK), FULL),
        pltpu.VMEM((tall, QBLK), LOW),
        pltpu.VMEM((tall, QBLK), LOW),
        pltpu.VMEM((2, total, HD), FULL),
        pltpu.VMEM((group_size, rows, HD), LOW),
        pltpu.VMEM((heads, total, HD), LOW),
        pltpu.VMEM((group_size, 2, rows, HD), LOW),
        pltpu.VMEM((group_size, 2, rows, HD), LOW),
        pltpu.VMEM((group_size, 2, rows, HD), LOW),
        pltpu.VMEM((group_size, 2, rows, HD), LOW),
        pltpu.VMEM((column, PARTS, rows, PCOLS), LOW),
        pltpu.VMEM((PARTS, chunk, PCOLS), FULL),
        pltpu.VMEM((PARTS, chunk, PCOLS), LOW),
        pltpu.VMEM((PARTS, 2 * group_size, piece, PCOLS), LOW),
        pltpu.VMEM((rows, width), LOW),
        pltpu.VMEM((1, total), jnp.int32),
        pltpu.VMEM((8, QBLK), FULL),
        dma((3,)),
        dma,
        dma((heads, 2)),
        dma,
        dma,
        dma,
        dma,
        dma,
        dma,
        dma,
        dma,
        dma((2,)),
        dma,
        dma,
        dma,
        dma((PARTS, 3)),
        dma,
        dma((PARTS,)),
        dma,
        dma((PARTS, ys)),
        dma,
        dma((PARTS,)),
        dma,
    ]
    smem = pl.BlockSpec(memory_space=pltpu.SMEM)
    vmem = pl.BlockSpec(memory_space=pltpu.VMEM)
    anywhere = pl.BlockSpec(memory_space=pl.ANY)

    def kernel(*refs):
        layer_kernel(group_size, replica_count, *refs)

    out_shape = (
        jax.ShapeDtypeStruct((rows, HQ * HD), LOW),
        jax.ShapeDtypeStruct((rows, width), LOW),
        jax.ShapeDtypeStruct((piece, kvw), LOW),
        jax.ShapeDtypeStruct((piece, kvw), LOW),
    )
    results = pl.pallas_call(
        kernel,
        out_shape=out_shape,
        in_specs=[smem, smem, smem] + [anywhere] * 5,
        out_specs=(anywhere, anywhere, vmem, vmem),
        scratch_shapes=scratch,
        compiler_params=pltpu.CompilerParams(
            collective_id=0, has_side_effects=True, vmem_limit_bytes=56 * 1024 * 1024
        ),
        name="layer",
    )(
        seq_lengths,
        seq_group,
        loader_offsets,
        hidden[0],
        queries[0],
        out_grad[0],
        key_weight,
        value_weight,
    )
    grad_query, grad_hidden, grad_key, grad_value = pl.pallas_call(
        hand_over,
        out_shape=out_shape,
        in_specs=[anywhere] * 4,
        out_specs=[anywhere] * 4,
        scratch_shapes=[pltpu.VMEM(shape.shape, LOW) for shape in out_shape] + [dma((2, 4, 4))],
        name="hand_over",
    )(*results)
    return (grad_query[None], grad_hidden[None], grad_key, grad_value)


def solution(mesh):
    placed = (
        P("dp", "grp", None),
        P("dp", "grp", None),
        P("dp", "grp", None),
        P(),
        P(),
        P("dp", None),
        P("dp", None),
        P("dp", None),
    )
    return jax.shard_map(
        on_device,
        mesh=mesh,
        in_specs=placed,
        out_specs=(
            P("dp", "grp", None),
            P("dp", "grp", None),
            P(("grp", "dp"), None),
            P(("grp", "dp"), None),
        ),
        check_vma=False,
    )
```

```python
import math

import jax
import jax.numpy as jnp
from jax import lax
from jax.experimental import pallas as pl
from jax.experimental.pallas import tpu as pltpu
from jax.sharding import PartitionSpec as P

HQ = 32
KVH = 4
HD = 128
SLOTS = 8
QBLK = 256
ZS = 4
PARTS = 4
PCOLS = 2 * KVH * HD // PARTS
ORDER = (2, 3, 0, 1)
LOW = jnp.bfloat16
FULL = jnp.float32
MESH = pl.DeviceIdType.MESH
NT = (((1,), (1,)), ((), ()))


def each(first, last, step):
    def body(i, carry):
        step(i)
        return carry

    lax.fori_loop(first, last, body, 0)


def layer_kernel(
    group_size,
    replica_count,
    lengths,
    groups,
    offsets,
    hidden,
    queries,
    out_grad,
    key_weight,
    value_weight,
    grad_query,
    grad_hidden,
    grad_key,
    grad_value,
    hid_v,
    kw_v,
    vw_v,
    qd_r,
    kv_s,
    kv_r,
    kt_v,
    hid_s,
    hid_t,
    s_v,
    pg_v,
    wl_v,
    ds_v,
    acc,
    dq_s,
    dq_g,
    dl_s,
    dl_r,
    dg_s,
    dg_r,
    dkv_all,
    prod,
    prod_s,
    rs_r,
    gh_v,
    begin_v,
    inv_v,
    load_sem,
    in_send,
    in_recv,
    kv_send,
    kv_recv,
    hid_send,
    hid_recv,
    dq_send,
    dq_recv,
    dq_own,
    dl_send,
    dl_recv,
    dg_send,
    dg_recv,
    ya_send,
    ya_recv,
    yf_send,
    yf_recv,
    yc_send,
    yc_recv,
    rs_send,
    rs_recv,
    gh_sem,
):
    me = lax.axis_index("grp")
    rep = lax.axis_index("dp")
    x_lo, z = me // ZS, lax.rem(me, ZS)
    y, x_hi, core = rep // 4, lax.rem(rep // 2, 2), lax.rem(rep, 2)
    ys = replica_count // 4
    column = 2 * ys
    summed_over = 2 * group_size
    rows = hidden.shape[0]
    width = hidden.shape[1]
    total = rows * group_size
    heads = HQ // group_size
    wide = heads * HD
    kvw = KVH * HD
    piece = width // (group_size * replica_count)
    inv_root = 1.0 / math.sqrt(HD)
    exp_scale = inv_root / math.log(2.0)
    blocks = total // QBLK
    per_block = QBLK // rows

    def peer(o):
        return lax.rem(x_lo + o // ZS, 2) * ZS + lax.rem(z + o, ZS)

    def origin(o):
        return lax.rem(x_lo + o // ZS, 2) * ZS + lax.rem(z - o + 2 * ZS, ZS)

    def place(at_y, at_x_hi, at_core):
        return (at_y * 2 + at_x_hi) * 2 + at_core

    def first_col(device):
        return lax.rem(device, KVH) * (2 * wide) + (device // KVH) * wide

    def rows_of(block):
        return pl.ds(pl.multiple_of(block * rows, rows), rows)

    def cols(at, n):
        return pl.ds(pl.multiple_of(at, n), n)

    load_hid = pltpu.make_async_copy(hidden, hid_v, load_sem.at[0])
    load_kw = pltpu.make_async_copy(key_weight, kw_v, load_sem.at[1])
    load_vw = pltpu.make_async_copy(value_weight, vw_v, load_sem.at[2])
    load_hid.start()
    load_kw.start()
    load_vw.start()

    barrier = pltpu.get_barrier_semaphore()

    def column_peer(o):
        return place(lax.rem(y + o // 2, ys), x_hi, lax.rem(core + o, 2))

    def column_origin(o):
        return lax.rem(y - o // 2 + ys, ys), lax.rem(core + o, 2)

    def sum_peer(o):
        return {
            "grp": peer(lax.rem(o, group_size)),
            "dp": place(y, lax.rem(x_hi + o // group_size, 2), core),
        }

    each(
        1,
        column,
        lambda o: pl.semaphore_signal(
            barrier, inc=1, device_id={"dp": column_peer(o)}, device_id_type=MESH
        ),
    )
    each(
        1,
        summed_over,
        lambda o: pl.semaphore_signal(
            barrier, inc=1, device_id=sum_peer(o), device_id_type=MESH
        ),
    )

    def q_copy(h, o, to):
        dest = peer(o)
        at = rows_of(me if to else origin(o))
        return pltpu.make_async_remote_copy(
            src_ref=queries.at[:, cols(first_col(dest) + h * HD, HD)],
            dst_ref=qd_r.at[h, 0, at, :],
            send_sem=in_send,
            recv_sem=in_recv.at[h, 0],
            device_id={"grp": dest},
            device_id_type=MESH,
        )

    def do_copy(h, o, to):
        dest = peer(o)
        at = rows_of(me if to else origin(o))
        return pltpu.make_async_remote_copy(
            src_ref=out_grad.at[:, cols(first_col(dest) + h * HD, HD)],
            dst_ref=qd_r.at[h, 1, at, :],
            send_sem=in_send,
            recv_sem=in_recv.at[h, 1],
            device_id={"grp": dest},
            device_id_type=MESH,
        )

    def kv_copy(o, to):
        dest = peer(o)
        at = rows_of(me if to else origin(o))
        return pltpu.make_async_remote_copy(
            src_ref=kv_s.at[lax.rem(dest, KVH)],
            dst_ref=kv_r.at[:, at, :],
            send_sem=kv_send,
            recv_sem=kv_recv,
            device_id={"grp": dest},
            device_id_type=MESH,
        )

    def hid_copy(o, to):
        dest_y, dest_core = lax.rem(y + o // 2, ys), lax.rem(core + o, 2)
        from_y, from_core = (y, core) if to else column_origin(o)
        return pltpu.make_async_remote_copy(
            src_ref=hid_s.at[dest_y * 2 + dest_core],
            dst_ref=hid_t.at[from_y, :, cols(from_core * rows, rows)],
            send_sem=hid_send,
            recv_sem=hid_recv,
            device_id={"dp": column_peer(o)},
            device_id_type=MESH,
        )

    def dq_copy(h, o, to):
        dest = peer(o)
        at = first_col(me if to else origin(o)) + h * HD
        return pltpu.make_async_remote_copy(
            src_ref=dq_g.at[h, rows_of(dest), :],
            dst_ref=grad_query.at[:, cols(at, HD)],
            send_sem=dq_send,
            recv_sem=dq_recv,
            device_id={"grp": dest},
            device_id_type=MESH,
        )

    def dq_stay(h):
        return pltpu.make_async_copy(
            dq_g.at[h, rows_of(me), :],
            grad_query.at[:, cols(first_col(me) + h * HD, HD)],
            dq_own,
        )

    def dl_copy(part, dest):
        return pltpu.make_async_remote_copy(
            src_ref=dl_s.at[dest, part],
            dst_ref=dl_r.at[me, part],
            send_sem=dl_send,
            recv_sem=dl_recv.at[part],
            device_id={"grp": dest},
            device_id_type=MESH,
        )

    def dg_copy(o, to):
        dest = peer(o)
        return pltpu.make_async_remote_copy(
            src_ref=dg_s.at[dest],
            dst_ref=dg_r.at[me if to else origin(o)],
            send_sem=dg_send,
            recv_sem=dg_recv,
            device_id={"grp": dest},
            device_id_type=MESH,
        )

    def ya_copy(part, k, to):
        step = (1, ys - 1, 2)[k]
        at = (y if to else lax.rem(y + ys - step, ys)) * 2 + core
        return pltpu.make_async_remote_copy(
            src_ref=dkv_all.at[y * 2 + core, part],
            dst_ref=dkv_all.at[at, part],
            send_sem=ya_send,
            recv_sem=ya_recv.at[part, k],
            device_id={"dp": place(lax.rem(y + step, ys), x_hi, core)},
            device_id_type=MESH,
        )

    def yf_copy(part, k, to):
        step = ys - 1 if k else 1
        come = lax.rem(y + ys - step, ys) * 2 + core
        far = lax.rem(y + 2, ys) * 2 + core
        half = pl.ds(k * (rows // 2), rows // 2)
        return pltpu.make_async_remote_copy(
            src_ref=dkv_all.at[come, part, half],
            dst_ref=dkv_all.at[come if to else far, part, half],
            send_sem=yf_send,
            recv_sem=yf_recv.at[part],
            device_id={"dp": place(lax.rem(y + step, ys), x_hi, core)},
            device_id_type=MESH,
        )

    def yc_copy(part, k, to):
        from_y = lax.rem(y + k, ys)
        return pltpu.make_async_remote_copy(
            src_ref=dkv_all.at[from_y * 2 + core, part],
            dst_ref=dkv_all.at[from_y * 2 + (core if to else 1 - core), part],
            send_sem=yc_send,
            recv_sem=yc_recv.at[part, k],
            device_id={"dp": place(y, x_hi, 1 - core)},
            device_id_type=MESH,
        )

    def rs_copy(part, o):
        dest = sum_peer(o)
        at = dest["grp"] * 2 + lax.rem(x_hi + o // group_size, 2)
        return pltpu.make_async_remote_copy(
            src_ref=prod_s.at[part, pl.ds(pl.multiple_of(at * piece, piece), piece), :],
            dst_ref=rs_r.at[part, o],
            send_sem=rs_send,
            recv_sem=rs_recv.at[part],
            device_id=dest,
            device_id_type=MESH,
        )

    def settle(ref, sem):
        pltpu.make_async_copy(ref, ref, sem).wait()

    others = total - rows
    seven = pl.ds(0, group_size - 1)

    def own_q(h):
        return pltpu.make_async_copy(
            queries.at[:, cols(first_col(me) + h * HD, HD)],
            qd_r.at[h, 0, rows_of(me), :],
            in_recv.at[h, 0],
        )

    def own_do(h):
        return pltpu.make_async_copy(
            out_grad.at[:, cols(first_col(me) + h * HD, HD)],
            qd_r.at[h, 1, rows_of(me), :],
            in_recv.at[h, 1],
        )

    def send_head(h):
        each(1, group_size, lambda o: q_copy(h, o, True).start())
        each(1, group_size, lambda o: do_copy(h, o, True).start())

    pl.semaphore_wait(barrier, column - 1 + summed_over - 1)
    send_head(0)

    load_hid.wait()
    load_kw.wait()
    hid_rows = hid_v[...]

    def project(weight, which):
        for g in range(0, KVH, 2):
            both = jnp.dot(
                hid_rows, weight[:, g * HD : (g + 2) * HD], preferred_element_type=FULL
            ).astype(LOW)
            kv_s[g, which] = both[:, :HD]
            kv_s[g + 1, which] = both[:, HD:]

    project(kw_v, 0)
    load_vw.wait()
    project(vw_v, 1)

    each(1, group_size, lambda o: kv_copy(o, True).start())
    each(1, heads, send_head)
    for h in range(heads):
        own_q(h).start()
        own_do(h).start()
    kv_r[:, rows_of(me), :] = kv_s[lax.rem(me, KVH)]

    lanes = 4 * piece

    def turn(t):
        turned = hid_v[:, cols(t * lanes, lanes)].T
        g = t // ys
        to_y = lax.rem(t, ys)
        for xh in range(2):
            at = pl.ds(pl.multiple_of((g * 2 + xh) * piece, piece), piece)
            for c in range(2):
                hid_s[to_y * 2 + c, at, :] = turned[(xh * 2 + c) * piece :][:piece]

    each(0, width // lanes, turn)
    each(1, column, lambda o: hid_copy(o, True).start())
    hid_t[y, :, cols(core * rows, rows)] = hid_s[y * 2 + core]

    row_ids = lax.broadcasted_iota(jnp.int32, (1, total), 1)
    begin = jnp.zeros((1, total), jnp.int32)
    for s in range(SLOTS):
        at, size = offsets[0, s], lengths[0, s]
        begin = jnp.where((row_ids >= at) & (row_ids < at + size), at, begin)
    begin_v[...] = begin
    starts = []
    for s in range(SLOTS):
        start = jnp.int32(0)
        for t in range(SLOTS):
            if t < s:
                before = groups[0, t] <= groups[0, s]
            else:
                before = groups[0, t] < groups[0, s]
            if t != s:
                start = start + jnp.where(before, lengths[0, t], 0)
        starts.append(start)

    def source_block(row):
        found = jnp.int32(0)
        for s in range(SLOTS):
            inside = (row >= starts[s]) & (row < starts[s] + lengths[0, s])
            found = found + jnp.where(inside, offsets[0, s] + row - starts[s], 0)
        return found // rows

    sources = [source_block(b * rows) for b in range(group_size)]

    acc[...] = jnp.zeros_like(acc)
    settle(kv_r.at[:, pl.ds(0, others), :], kv_recv)
    kt_v[...] = kv_r[0].T

    key_ids = lax.broadcasted_iota(jnp.int32, (HD, QBLK), 0)
    lane_ids = lax.broadcasted_iota(jnp.int32, (HD, QBLK), 1)

    def fold(tile):
        return tile.reshape(HD // 8, 8, QBLK)

    def span(b):
        first = sum((i + 1) * QBLK for i in range(b))
        return first, (b + 1) * QBLK

    def weigh(h, b):
        r0 = b * QBLK
        first, keys = span(b)
        q_blk = qd_r[h, 0, r0 : r0 + QBLK, :]
        begin_row = begin_v[:, r0 : r0 + QBLK]
        top = jnp.full((8, QBLK), -1e30, FULL)
        for j in range(0, keys, QBLK):
            block = lax.dot_general(
                kv_r[0, j : j + QBLK, :], q_blk, NT, preferred_element_type=FULL
            )
            for i in range(j, j + QBLK, HD):
                seen = key_ids + i >= begin_row
                if j >= r0:
                    seen = seen & (key_ids + (i - r0) <= lane_ids)
                tile = jnp.where(seen, block[i - j : i - j + HD], -1e30)
                s_v[first + i : first + i + HD, :] = tile
                top = jnp.maximum(top, jnp.max(fold(tile), axis=0))
        top = jnp.max(top, axis=0, keepdims=True)
        mass = jnp.zeros((8, QBLK), FULL)
        for j in range(keys // HD):
            at = slice(first + j * HD, first + (j + 1) * HD)
            tile = jnp.exp2((s_v[at, :] - top) * exp_scale)
            s_v[at, :] = tile
            mass = mass + jnp.sum(fold(tile), axis=0)
        inverse = 1.0 / jnp.sum(mass, axis=0, keepdims=True)
        inv_v[b : b + 1, :] = inverse
        for j in range(keys // HD):
            at = slice(first + j * HD, first + (j + 1) * HD)
            wl_v[at, :] = (s_v[at, :] * inverse).astype(LOW)

    def value_grad(h, b):
        r0 = b * QBLK
        first, keys = span(b)
        acc[1, 0:keys, :] += jnp.dot(
            wl_v[first : first + keys, :],
            qd_r[h, 1, r0 : r0 + QBLK, :],
            preferred_element_type=FULL,
        )

    def send_terms(part, first_block, last_block):
        for j in range(first_block, last_block):
            term = acc[part, j * rows : (j + 1) * rows, :]
            if part == 0:
                term = term * inv_root
            dl_s[j, part] = term.astype(LOW)

            @pl.when(me != j)
            def _():
                dl_copy(part, j).start()

    def attend(h, b):
        r0 = b * QBLK
        first, keys = span(b)
        q_blk = qd_r[h, 0, r0 : r0 + QBLK, :]
        do_blk = qd_r[h, 1, r0 : r0 + QBLK, :]
        delta = jnp.zeros((8, QBLK), FULL)
        for j in range(0, keys, QBLK):
            at = slice(first + j, first + j + QBLK)
            block = lax.dot_general(
                kv_r[1, j : j + QBLK, :], do_blk, NT, preferred_element_type=FULL
            )
            pg_v[at, :] = block
            terms = wl_v[at, :].astype(FULL) * block
            delta = delta + jnp.sum(terms.reshape(QBLK // 8, 8, QBLK), axis=0)
        delta = jnp.sum(delta, axis=0, keepdims=True)
        inverse = inv_v[b : b + 1, :]
        for j in range(keys // HD):
            at = slice(first + j * HD, first + (j + 1) * HD)
            ds_v[at, :] = (s_v[at, :] * inverse * (pg_v[at, :] - delta)).astype(LOW)
        all_keys = slice(first, first + keys)
        acc[0, 0:keys, :] += jnp.dot(ds_v[all_keys, :], q_blk, preferred_element_type=FULL)

    def query_grad(b):
        r0 = b * QBLK
        first, keys = span(b)
        grad_t = jnp.dot(
            kt_v[:, 0:keys], ds_v[first : first + keys, :], preferred_element_type=FULL
        )
        grad_rows = (grad_t * inv_root).T.astype(LOW)
        for j in range(per_block):
            dq_s[r0 // rows + j] = grad_rows[j * rows : (j + 1) * rows, :]

    def send_dq(h):
        each(1, group_size, lambda o: dq_copy(h, o, True).start())
        dq_stay(h).start()

    def one_head(h):
        settle(qd_r.at[h, 0], in_recv.at[h, 0])
        for b in reversed(range(blocks)):
            weigh(h, b)
        settle(qd_r.at[h, 1], in_recv.at[h, 1])

        for b in reversed(range(blocks)):
            value_grad(h, b)

        @pl.when(h == heads - 1)
        def _():
            send_terms(1, 0, group_size)
            send_dq(0)

        for b in reversed(range(blocks)):
            attend(h, b)

            @pl.when(h == heads - 1)
            def _():
                send_terms(0, b * per_block, (b + 1) * per_block)

        for b in range(blocks):
            query_grad(b)
        for b in range(group_size):
            dq_g[h, b * rows : (b + 1) * rows, :] = dq_s[sources[b]]

    each(0, heads, one_head)

    dl_r[me] = dl_s[me]

    def merge(received, part, g):
        return (
            received[g, part].astype(FULL) + received[KVH + g, part].astype(FULL)
        ).astype(LOW)

    last = ORDER[-1]

    def gather(part):
        which = part * PCOLS // kvw
        for i in range(PCOLS // HD):
            dkv_all[y * 2 + core, part, :, i * HD : (i + 1) * HD] = merge(
                dl_r, which, (part * PCOLS % kvw) // HD + i
            )
        for k in range(3 if part == last else 2):
            ya_copy(part, k, True).start()
        yc_copy(part, 0, True).start()

    settle(dl_r.at[seven, 1], dl_recv.at[1])
    for part in ORDER[: PARTS // 2]:
        gather(part)
    for b in range(group_size):
        dg_s[b] = dl_s[sources[b]]
    settle(dl_r.at[seven, 0], dl_recv.at[0])
    for part in ORDER[PARTS // 2 :]:
        gather(part)

    each(1, group_size, lambda o: dg_copy(o, True).start())
    each(1, heads, send_dq)
    settle(kv_r.at[:, pl.ds(0, others), :], kv_send)
    settle(qd_r.at[:, :, pl.ds(0, others), :], in_send)
    settle(hid_s.at[pl.ds(0, column - 1)], hid_send)

    settle(hid_s.at[pl.ds(0, column - 1)], hid_recv)
    def pass_on(part):
        for k in range(2):
            ya_copy(part, k, False).wait_recv()
            if part != last:
                yf_copy(part, k, True).start()
            yc_copy(part, 1 if k else ys - 1, True).start()

    def hand_far(part):
        if part != last:
            settle(dkv_all.at[0, part], yf_recv.at[part])
        else:
            ya_copy(part, 2, False).wait_recv()
        yc_copy(part, 2, True).start()

    def multiply(part):
        for k in (0, 1, ys - 1, 2):
            yc_copy(part, k, False).wait_recv()
            from_y = lax.rem(y + k, ys)
            grads = dkv_all[pl.ds(from_y * 2, 2), part].reshape(2 * rows, PCOLS)
            term = jnp.dot(hid_t[from_y], grads, preferred_element_type=FULL)
            if k > 0:
                term = prod[part] + term
            prod[part] = term
            if k == 2:
                prod_s[part] = term.astype(LOW)
        each(1, summed_over, lambda o: rs_copy(part, o).start())

    pass_on(ORDER[0])
    for i, part in enumerate(ORDER):
        if i + 1 < PARTS:
            pass_on(ORDER[i + 1])
        hand_far(part)
        multiply(part)

    dg_r[me] = dg_s[me]
    settle(dg_r.at[seven], dg_recv)
    dk_rows = jnp.concatenate([merge(dg_r, 0, g) for g in range(KVH)], axis=1)
    dv_rows = jnp.concatenate([merge(dg_r, 1, g) for g in range(KVH)], axis=1)

    def hidden_tile(t):
        at = pl.ds(pl.multiple_of(t * 512, 512), 512)
        tile = lax.dot_general(
            dk_rows, kw_v[at, :], NT, preferred_element_type=FULL
        ) + lax.dot_general(dv_rows, vw_v[at, :], NT, preferred_element_type=FULL)
        gh_v[:, at] = tile.astype(LOW)

    each(0, width // 512, hidden_tile)
    gh_out = pltpu.make_async_copy(gh_v, grad_hidden, gh_sem)
    gh_out.start()

    settle(dg_s.at[seven], dg_send)
    settle(dl_s.at[seven], dl_send)
    settle(dq_g.at[:, pl.ds(0, others), :], dq_send)
    settle(dq_g.at[:, pl.ds(0, others), :], dq_recv)
    settle(dq_g.at[:, pl.ds(0, rows), :], dq_own)
    settle(dkv_all.at[pl.ds(0, 2)], ya_send)
    settle(dkv_all.at[0, 0], ya_send)
    settle(dkv_all.at[0, pl.ds(0, PARTS - 1)], yf_send)
    settle(dkv_all.at[pl.ds(0, ys)], yc_send)

    norm = 1.0 / math.sqrt(total * replica_count)
    own = pl.ds(pl.multiple_of((me * 2 + x_hi) * piece, piece), piece)
    for part in ORDER:
        settle(rs_r.at[part, pl.ds(0, summed_over - 1)], rs_recv.at[part])
        summed = prod[part, own, :]
        for o in range(1, summed_over):
            summed = summed + rs_r[part, o].astype(FULL)
        result = grad_value if part * PCOLS >= kvw else grad_key
        at = part * PCOLS % kvw
        result[:, at : at + PCOLS] = (summed * norm).astype(LOW)

    gh_out.wait()
    settle(rs_r.at[:, pl.ds(0, summed_over - 1)], rs_send)


def hand_over(*refs):
    sources, results = refs[0:4], refs[4:8]
    held, sems = refs[8:12], refs[12]
    steps = []
    for i, (source, result, slot) in enumerate(zip(sources, results, held)):
        parts = 4 if i < 2 else 1
        size = source.shape[0] // parts
        for j in range(parts):
            at = pl.ds(j * size, size)
            steps.append(
                (
                    pltpu.make_async_copy(source.at[at], slot.at[at], sems.at[0, i, j]),
                    pltpu.make_async_copy(slot.at[at], result.at[at], sems.at[1, i, j]),
                )
            )
    for load, _ in steps:
        load.start()
    for load, store in steps:
        load.wait()
        store.start()
    for _, store in steps:
        store.wait()


def on_device(
    hidden, queries, out_grad, key_weight, value_weight, seq_lengths, seq_group, loader_offsets
):
    group_size = lax.axis_size("grp")
    replica_count = lax.axis_size("dp")
    rows, width = hidden.shape[1:]
    total = rows * group_size
    heads = HQ // group_size
    kvw = KVH * HD
    piece = width // (group_size * replica_count)
    blocks = total // QBLK
    ys = replica_count // 4
    column = 2 * ys
    chunk = width // column
    tall = sum((b + 1) * QBLK for b in range(blocks))
    dma = pltpu.SemaphoreType.DMA
    scratch = [
        pltpu.VMEM((rows, width), LOW),
        pltpu.VMEM((width, kvw), LOW),
        pltpu.VMEM((width, kvw), LOW),
        pltpu.VMEM((heads, 2, total, HD), LOW),
        pltpu.VMEM((KVH, 2, rows, HD), LOW),
        pltpu.VMEM((2, total, HD), LOW),
        pltpu.VMEM((HD, total), LOW),
        pltpu.VMEM((column, chunk, rows), LOW),
        pltpu.VMEM((ys, chunk, 2 * rows), LOW),
        pltpu.VMEM((tall, QBLK), FULL),
        pltpu.VMEM((tall, QBLK), FULL),
        pltpu.VMEM((tall, QBLK), LOW),
        pltpu.VMEM((tall, QBLK), LOW),
        pltpu.VMEM((2, total, HD), FULL),
        pltpu.VMEM((group_size, rows, HD), LOW),
        pltpu.VMEM((heads, total, HD), LOW),
        pltpu.VMEM((group_size, 2, rows, HD), LOW),
        pltpu.VMEM((group_size, 2, rows, HD), LOW),
        pltpu.VMEM((group_size, 2, rows, HD), LOW),
        pltpu.VMEM((group_size, 2, rows, HD), LOW),
        pltpu.VMEM((column, PARTS, rows, PCOLS), LOW),
        pltpu.VMEM((PARTS, chunk, PCOLS), FULL),
        pltpu.VMEM((PARTS, chunk, PCOLS), LOW),
        pltpu.VMEM((PARTS, 2 * group_size, piece, PCOLS), LOW),
        pltpu.VMEM((rows, width), LOW),
        pltpu.VMEM((1, total), jnp.int32),
        pltpu.VMEM((8, QBLK), FULL),
        dma((3,)),
        dma,
        dma((heads, 2)),
        dma,
        dma,
        dma,
        dma,
        dma,
        dma,
        dma,
        dma,
        dma((2,)),
        dma,
        dma,
        dma,
        dma((PARTS, 3)),
        dma,
        dma((PARTS,)),
        dma,
        dma((PARTS, ys)),
        dma,
        dma((PARTS,)),
        dma,
    ]
    smem = pl.BlockSpec(memory_space=pltpu.SMEM)
    vmem = pl.BlockSpec(memory_space=pltpu.VMEM)
    anywhere = pl.BlockSpec(memory_space=pl.ANY)

    def kernel(*refs):
        layer_kernel(group_size, replica_count, *refs)

    out_shape = (
        jax.ShapeDtypeStruct((rows, HQ * HD), LOW),
        jax.ShapeDtypeStruct((rows, width), LOW),
        jax.ShapeDtypeStruct((piece, kvw), LOW),
        jax.ShapeDtypeStruct((piece, kvw), LOW),
    )
    results = pl.pallas_call(
        kernel,
        out_shape=out_shape,
        in_specs=[smem, smem, smem] + [anywhere] * 5,
        out_specs=(anywhere, anywhere, vmem, vmem),
        scratch_shapes=scratch,
        compiler_params=pltpu.CompilerParams(
            collective_id=0, has_side_effects=True, vmem_limit_bytes=56 * 1024 * 1024
        ),
        name="layer",
    )(
        seq_lengths,
        seq_group,
        loader_offsets,
        hidden[0],
        queries[0],
        out_grad[0],
        key_weight,
        value_weight,
    )
    grad_query, grad_hidden, grad_key, grad_value = pl.pallas_call(
        hand_over,
        out_shape=out_shape,
        in_specs=[anywhere] * 4,
        out_specs=[anywhere] * 4,
        scratch_shapes=[pltpu.VMEM(shape.shape, LOW) for shape in out_shape] + [dma((2, 4, 4))],
        name="hand_over",
    )(*results)
    return (grad_query[None], grad_hidden[None], grad_key, grad_value)


def solution(mesh):
    placed = (
        P("dp", "grp", None),
        P("dp", "grp", None),
        P("dp", "grp", None),
        P(),
        P(),
        P("dp", None),
        P("dp", None),
        P("dp", None),
    )
    return jax.shard_map(
        on_device,
        mesh=mesh,
        in_specs=placed,
        out_specs=(
            P("dp", "grp", None),
            P("dp", "grp", None),
            P(("grp", "dp"), None),
            P(("grp", "dp"), None),
        ),
        check_vma=False,
    )
```

```python
import math

import jax
import jax.numpy as jnp
from jax import lax
from jax.experimental import pallas as pl
from jax.experimental.pallas import tpu as pltpu
from jax.sharding import PartitionSpec as P

HQ = 32
KVH = 4
HD = 128
SLOTS = 8
QBLK = 256
ZS = 4
PARTS = 4
PCOLS = 2 * KVH * HD // PARTS
TWO_STEP = (2,)
ORDER = (2, 3, 0, 1)
LOW = jnp.bfloat16
FULL = jnp.float32
MESH = pl.DeviceIdType.MESH
NT = (((1,), (1,)), ((), ()))


def each(first, last, step):
    def body(i, carry):
        step(i)
        return carry

    lax.fori_loop(first, last, body, 0)


def layer_kernel(
    group_size,
    replica_count,
    lengths,
    groups,
    offsets,
    hidden,
    queries,
    out_grad,
    key_weight,
    value_weight,
    grad_query,
    grad_hidden,
    grad_key,
    grad_value,
    hid_v,
    kw_v,
    vw_v,
    qd_r,
    kv_s,
    kv_r,
    kt_v,
    hid_s,
    hid_t,
    s_v,
    pg_v,
    wl_v,
    ds_v,
    acc,
    dq_s,
    dq_g,
    dl_s,
    dl_r,
    dg_s,
    dg_r,
    dkv_all,
    prod,
    prod_s,
    rx_r,
    rs_r,
    gh_v,
    begin_v,
    inv_v,
    load_sem,
    in_send,
    in_recv,
    kv_send,
    kv_recv,
    hid_send,
    hid_recv,
    dq_send,
    dq_recv,
    dq_own,
    dl_send,
    dl_recv,
    dg_send,
    dg_recv,
    ya_send,
    ya_recv,
    yf_send,
    yf_recv,
    yc_send,
    yc_recv,
    rx_send,
    rx_recv,
    rs_send,
    rs_recv,
    gh_sem,
):
    me = lax.axis_index("grp")
    rep = lax.axis_index("dp")
    x_lo, z = me // ZS, lax.rem(me, ZS)
    y, x_hi, core = rep // 4, lax.rem(rep // 2, 2), lax.rem(rep, 2)
    ys = replica_count // 4
    column = 2 * ys
    summed_over = 2 * group_size
    rows = hidden.shape[0]
    width = hidden.shape[1]
    total = rows * group_size
    heads = HQ // group_size
    wide = heads * HD
    kvw = KVH * HD
    piece = width // (group_size * replica_count)
    half_rows = group_size * piece
    inv_root = 1.0 / math.sqrt(HD)
    exp_scale = inv_root / math.log(2.0)
    blocks = total // QBLK
    per_block = QBLK // rows

    def peer(o):
        return lax.rem(x_lo + o // ZS, 2) * ZS + lax.rem(z + o, ZS)

    def origin(o):
        return lax.rem(x_lo + o // ZS, 2) * ZS + lax.rem(z - o + 2 * ZS, ZS)

    def place(at_y, at_x_hi, at_core):
        return (at_y * 2 + at_x_hi) * 2 + at_core

    def first_col(device):
        return lax.rem(device, KVH) * (2 * wide) + (device // KVH) * wide

    def rows_of(block):
        return pl.ds(pl.multiple_of(block * rows, rows), rows)

    def cols(at, n):
        return pl.ds(pl.multiple_of(at, n), n)

    load_hid = pltpu.make_async_copy(hidden, hid_v, load_sem.at[0])
    load_kw = pltpu.make_async_copy(key_weight, kw_v, load_sem.at[1])
    load_vw = pltpu.make_async_copy(value_weight, vw_v, load_sem.at[2])
    load_hid.start()
    load_kw.start()
    load_vw.start()

    barrier = pltpu.get_barrier_semaphore()

    def column_peer(o):
        return place(lax.rem(y + o // 2, ys), x_hi, lax.rem(core + o, 2))

    def column_origin(o):
        return lax.rem(y - o // 2 + ys, ys), lax.rem(core + o, 2)

    def sum_peer(o):
        return {
            "grp": peer(lax.rem(o, group_size)),
            "dp": place(y, lax.rem(x_hi + o // group_size, 2), core),
        }

    each(
        1,
        column,
        lambda o: pl.semaphore_signal(
            barrier, inc=1, device_id={"dp": column_peer(o)}, device_id_type=MESH
        ),
    )
    each(
        1,
        summed_over,
        lambda o: pl.semaphore_signal(
            barrier, inc=1, device_id=sum_peer(o), device_id_type=MESH
        ),
    )

    across = {"grp": lax.rem(me + ZS, group_size), "dp": place(y, 1 - x_hi, core)}

    def q_copy(h, o, to):
        dest = peer(o)
        at = rows_of(me if to else origin(o))
        return pltpu.make_async_remote_copy(
            src_ref=queries.at[:, cols(first_col(dest) + h * HD, HD)],
            dst_ref=qd_r.at[h, 0, at, :],
            send_sem=in_send,
            recv_sem=in_recv.at[h, 0],
            device_id={"grp": dest},
            device_id_type=MESH,
        )

    def do_copy(h, o, to):
        dest = peer(o)
        at = rows_of(me if to else origin(o))
        return pltpu.make_async_remote_copy(
            src_ref=out_grad.at[:, cols(first_col(dest) + h * HD, HD)],
            dst_ref=qd_r.at[h, 1, at, :],
            send_sem=in_send,
            recv_sem=in_recv.at[h, 1],
            device_id={"grp": dest},
            device_id_type=MESH,
        )

    def kv_copy(o, to):
        dest = peer(o)
        at = rows_of(me if to else origin(o))
        return pltpu.make_async_remote_copy(
            src_ref=kv_s.at[lax.rem(dest, KVH)],
            dst_ref=kv_r.at[:, at, :],
            send_sem=kv_send,
            recv_sem=kv_recv,
            device_id={"grp": dest},
            device_id_type=MESH,
        )

    def hid_copy(o, to):
        dest_y, dest_core = lax.rem(y + o // 2, ys), lax.rem(core + o, 2)
        from_y, from_core = (y, core) if to else column_origin(o)
        return pltpu.make_async_remote_copy(
            src_ref=hid_s.at[dest_y * 2 + dest_core],
            dst_ref=hid_t.at[from_y, :, cols(from_core * rows, rows)],
            send_sem=hid_send,
            recv_sem=hid_recv,
            device_id={"dp": column_peer(o)},
            device_id_type=MESH,
        )

    def dq_copy(h, o, to):
        dest = peer(o)
        at = first_col(me if to else origin(o)) + h * HD
        return pltpu.make_async_remote_copy(
            src_ref=dq_g.at[h, rows_of(dest), :],
            dst_ref=grad_query.at[:, cols(at, HD)],
            send_sem=dq_send,
            recv_sem=dq_recv,
            device_id={"grp": dest},
            device_id_type=MESH,
        )

    def dq_stay(h):
        return pltpu.make_async_copy(
            dq_g.at[h, rows_of(me), :],
            grad_query.at[:, cols(first_col(me) + h * HD, HD)],
            dq_own,
        )

    def dl_copy(part, dest):
        return pltpu.make_async_remote_copy(
            src_ref=dl_s.at[dest, part],
            dst_ref=dl_r.at[me, part],
            send_sem=dl_send,
            recv_sem=dl_recv.at[part],
            device_id={"grp": dest},
            device_id_type=MESH,
        )

    def dg_copy(o, to):
        dest = peer(o)
        return pltpu.make_async_remote_copy(
            src_ref=dg_s.at[dest],
            dst_ref=dg_r.at[me if to else origin(o)],
            send_sem=dg_send,
            recv_sem=dg_recv,
            device_id={"grp": dest},
            device_id_type=MESH,
        )

    def ya_copy(part, k, to):
        step = (1, ys - 1, 2)[k]
        at = (y if to else lax.rem(y + ys - step, ys)) * 2 + core
        return pltpu.make_async_remote_copy(
            src_ref=dkv_all.at[y * 2 + core, part],
            dst_ref=dkv_all.at[at, part],
            send_sem=ya_send,
            recv_sem=ya_recv.at[part, k],
            device_id={"dp": place(lax.rem(y + step, ys), x_hi, core)},
            device_id_type=MESH,
        )

    def yf_copy(part, k, to):
        step = ys - 1 if k else 1
        come = lax.rem(y + ys - step, ys) * 2 + core
        far = lax.rem(y + 2, ys) * 2 + core
        half = pl.ds(k * (rows // 2), rows // 2)
        return pltpu.make_async_remote_copy(
            src_ref=dkv_all.at[come, part, half],
            dst_ref=dkv_all.at[come if to else far, part, half],
            send_sem=yf_send,
            recv_sem=yf_recv.at[part],
            device_id={"dp": place(lax.rem(y + step, ys), x_hi, core)},
            device_id_type=MESH,
        )

    def yc_copy(part, k, to):
        from_y = lax.rem(y + k, ys)
        return pltpu.make_async_remote_copy(
            src_ref=dkv_all.at[from_y * 2 + core, part],
            dst_ref=dkv_all.at[from_y * 2 + (core if to else 1 - core), part],
            send_sem=yc_send,
            recv_sem=yc_recv.at[part, k],
            device_id={"dp": place(y, x_hi, 1 - core)},
            device_id_type=MESH,
        )

    def rs_copy(part, o):
        dest = sum_peer(o)
        at = lax.rem(x_hi + o // group_size, 2) * group_size + dest["grp"]
        return pltpu.make_async_remote_copy(
            src_ref=prod_s.at[part, pl.ds(pl.multiple_of(at * piece, piece), piece), :],
            dst_ref=rs_r.at[part, o],
            send_sem=rs_send,
            recv_sem=rs_recv.at[part],
            device_id=dest,
            device_id_type=MESH,
        )

    def settle(ref, sem):
        pltpu.make_async_copy(ref, ref, sem).wait()

    others = total - rows
    seven = pl.ds(0, group_size - 1)

    def rx_copy(part):
        return pltpu.make_async_remote_copy(
            src_ref=prod_s.at[part, pl.ds((1 - x_hi) * half_rows, half_rows), :],
            dst_ref=rx_r.at[part],
            send_sem=rx_send,
            recv_sem=rx_recv.at[part],
            device_id=across,
            device_id_type=MESH,
        )

    def own_q(h):
        return pltpu.make_async_copy(
            queries.at[:, cols(first_col(me) + h * HD, HD)],
            qd_r.at[h, 0, rows_of(me), :],
            in_recv.at[h, 0],
        )

    def own_do(h):
        return pltpu.make_async_copy(
            out_grad.at[:, cols(first_col(me) + h * HD, HD)],
            qd_r.at[h, 1, rows_of(me), :],
            in_recv.at[h, 1],
        )

    def send_head(h):
        each(1, group_size, lambda o: q_copy(h, o, True).start())
        each(1, group_size, lambda o: do_copy(h, o, True).start())

    pl.semaphore_wait(barrier, column - 1 + summed_over - 1)
    send_head(0)

    load_hid.wait()
    load_kw.wait()
    hid_rows = hid_v[...]

    def project(weight, which):
        for g in range(0, KVH, 2):
            both = jnp.dot(
                hid_rows, weight[:, g * HD : (g + 2) * HD], preferred_element_type=FULL
            ).astype(LOW)
            kv_s[g, which] = both[:, :HD]
            kv_s[g + 1, which] = both[:, HD:]

    project(kw_v, 0)
    load_vw.wait()
    project(vw_v, 1)

    each(1, group_size, lambda o: kv_copy(o, True).start())
    each(1, heads, send_head)
    for h in range(heads):
        own_q(h).start()
        own_do(h).start()
    kv_r[:, rows_of(me), :] = kv_s[lax.rem(me, KVH)]

    lanes = 4 * piece

    def turn(t):
        turned = hid_v[:, cols(t * lanes, lanes)].T
        g = t // ys
        to_y = lax.rem(t, ys)
        for xh in range(2):
            at = pl.ds(pl.multiple_of((xh * group_size + g) * piece, piece), piece)
            for c in range(2):
                hid_s[to_y * 2 + c, at, :] = turned[(xh * 2 + c) * piece :][:piece]

    each(0, width // lanes, turn)
    each(1, column, lambda o: hid_copy(o, True).start())
    hid_t[y, :, cols(core * rows, rows)] = hid_s[y * 2 + core]

    row_ids = lax.broadcasted_iota(jnp.int32, (1, total), 1)
    begin = jnp.zeros((1, total), jnp.int32)
    for s in range(SLOTS):
        at, size = offsets[0, s], lengths[0, s]
        begin = jnp.where((row_ids >= at) & (row_ids < at + size), at, begin)
    begin_v[...] = begin
    starts = []
    for s in range(SLOTS):
        start = jnp.int32(0)
        for t in range(SLOTS):
            if t < s:
                before = groups[0, t] <= groups[0, s]
            else:
                before = groups[0, t] < groups[0, s]
            if t != s:
                start = start + jnp.where(before, lengths[0, t], 0)
        starts.append(start)

    def source_block(row):
        found = jnp.int32(0)
        for s in range(SLOTS):
            inside = (row >= starts[s]) & (row < starts[s] + lengths[0, s])
            found = found + jnp.where(inside, offsets[0, s] + row - starts[s], 0)
        return found // rows

    sources = [source_block(b * rows) for b in range(group_size)]

    acc[...] = jnp.zeros_like(acc)
    settle(kv_r.at[:, pl.ds(0, others), :], kv_recv)
    kt_v[...] = kv_r[0].T

    key_ids = lax.broadcasted_iota(jnp.int32, (HD, QBLK), 0)
    lane_ids = lax.broadcasted_iota(jnp.int32, (HD, QBLK), 1)

    def fold(tile):
        return tile.reshape(HD // 8, 8, QBLK)

    def span(b):
        first = sum((i + 1) * QBLK for i in range(b))
        return first, (b + 1) * QBLK

    def weigh(h, b):
        r0 = b * QBLK
        first, keys = span(b)
        q_blk = qd_r[h, 0, r0 : r0 + QBLK, :]
        begin_row = begin_v[:, r0 : r0 + QBLK]
        top = jnp.full((8, QBLK), -1e30, FULL)
        for j in range(0, keys, QBLK):
            block = lax.dot_general(
                kv_r[0, j : j + QBLK, :], q_blk, NT, preferred_element_type=FULL
            )
            for i in range(j, j + QBLK, HD):
                seen = key_ids + i >= begin_row
                if j >= r0:
                    seen = seen & (key_ids + (i - r0) <= lane_ids)
                tile = jnp.where(seen, block[i - j : i - j + HD], -1e30)
                s_v[first + i : first + i + HD, :] = tile
                top = jnp.maximum(top, jnp.max(fold(tile), axis=0))
        top = jnp.max(top, axis=0, keepdims=True)
        mass = jnp.zeros((8, QBLK), FULL)
        for j in range(keys // HD):
            at = slice(first + j * HD, first + (j + 1) * HD)
            tile = jnp.exp2((s_v[at, :] - top) * exp_scale)
            s_v[at, :] = tile
            mass = mass + jnp.sum(fold(tile), axis=0)
        inverse = 1.0 / jnp.sum(mass, axis=0, keepdims=True)
        inv_v[b : b + 1, :] = inverse
        for j in range(keys // HD):
            at = slice(first + j * HD, first + (j + 1) * HD)
            wl_v[at, :] = (s_v[at, :] * inverse).astype(LOW)

    def value_grad(h, b):
        r0 = b * QBLK
        first, keys = span(b)
        acc[1, 0:keys, :] += jnp.dot(
            wl_v[first : first + keys, :],
            qd_r[h, 1, r0 : r0 + QBLK, :],
            preferred_element_type=FULL,
        )

    def send_terms(part, first_block, last_block):
        for j in range(first_block, last_block):
            term = acc[part, j * rows : (j + 1) * rows, :]
            if part == 0:
                term = term * inv_root
            dl_s[j, part] = term.astype(LOW)

            @pl.when(me != j)
            def _():
                dl_copy(part, j).start()

    def attend(h, b):
        r0 = b * QBLK
        first, keys = span(b)
        q_blk = qd_r[h, 0, r0 : r0 + QBLK, :]
        do_blk = qd_r[h, 1, r0 : r0 + QBLK, :]
        delta = jnp.zeros((8, QBLK), FULL)
        for j in range(0, keys, QBLK):
            at = slice(first + j, first + j + QBLK)
            block = lax.dot_general(
                kv_r[1, j : j + QBLK, :], do_blk, NT, preferred_element_type=FULL
            )
            pg_v[at, :] = block
            terms = wl_v[at, :].astype(FULL) * block
            delta = delta + jnp.sum(terms.reshape(QBLK // 8, 8, QBLK), axis=0)
        delta = jnp.sum(delta, axis=0, keepdims=True)
        inverse = inv_v[b : b + 1, :]
        for j in range(keys // HD):
            at = slice(first + j * HD, first + (j + 1) * HD)
            ds_v[at, :] = (s_v[at, :] * inverse * (pg_v[at, :] - delta)).astype(LOW)
        all_keys = slice(first, first + keys)
        acc[0, 0:keys, :] += jnp.dot(ds_v[all_keys, :], q_blk, preferred_element_type=FULL)

    def query_grad(b):
        r0 = b * QBLK
        first, keys = span(b)
        grad_t = jnp.dot(
            kt_v[:, 0:keys], ds_v[first : first + keys, :], preferred_element_type=FULL
        )
        grad_rows = (grad_t * inv_root).T.astype(LOW)
        for j in range(per_block):
            dq_s[r0 // rows + j] = grad_rows[j * rows : (j + 1) * rows, :]

    def send_dq(h):
        each(1, group_size, lambda o: dq_copy(h, o, True).start())
        dq_stay(h).start()

    def one_head(h):
        settle(qd_r.at[h, 0], in_recv.at[h, 0])
        for b in reversed(range(blocks)):
            weigh(h, b)
        settle(qd_r.at[h, 1], in_recv.at[h, 1])

        for b in reversed(range(blocks)):
            value_grad(h, b)

        @pl.when(h == heads - 1)
        def _():
            send_terms(1, 0, group_size)

        for b in reversed(range(blocks)):
            attend(h, b)

            @pl.when(h == heads - 1)
            def _():
                send_terms(0, b * per_block, (b + 1) * per_block)

        for b in range(blocks):
            query_grad(b)
        for b in range(group_size):
            dq_g[h, b * rows : (b + 1) * rows, :] = dq_s[sources[b]]

    each(0, heads, one_head)

    send_dq(0)
    dl_r[me] = dl_s[me]

    def merge(received, part, g):
        return (
            received[g, part].astype(FULL) + received[KVH + g, part].astype(FULL)
        ).astype(LOW)

    last = ORDER[-1]

    def gather(part):
        which = part * PCOLS // kvw
        for i in range(PCOLS // HD):
            dkv_all[y * 2 + core, part, :, i * HD : (i + 1) * HD] = merge(
                dl_r, which, (part * PCOLS % kvw) // HD + i
            )
        for k in range(3 if part == last else 2):
            ya_copy(part, k, True).start()
        yc_copy(part, 0, True).start()

    settle(dl_r.at[seven, 1], dl_recv.at[1])
    for part in ORDER[: PARTS // 2]:
        gather(part)
    for b in range(group_size):
        dg_s[b] = dl_s[sources[b]]
    settle(dl_r.at[seven, 0], dl_recv.at[0])
    for part in ORDER[PARTS // 2 :]:
        gather(part)

    each(1, group_size, lambda o: dg_copy(o, True).start())
    each(1, heads, send_dq)
    settle(kv_r.at[:, pl.ds(0, others), :], kv_send)
    settle(qd_r.at[:, :, pl.ds(0, others), :], in_send)
    settle(hid_s.at[pl.ds(0, column - 1)], hid_send)

    settle(hid_s.at[pl.ds(0, column - 1)], hid_recv)
    def pass_on(part):
        for k in range(2):
            ya_copy(part, k, False).wait_recv()
            if part != last:
                yf_copy(part, k, True).start()
            yc_copy(part, 1 if k else ys - 1, True).start()

    def hand_far(part):
        if part != last:
            settle(dkv_all.at[0, part], yf_recv.at[part])
        else:
            ya_copy(part, 2, False).wait_recv()
        yc_copy(part, 2, True).start()

    def multiply(part):
        for k in (0, 1, ys - 1, 2):
            yc_copy(part, k, False).wait_recv()
            from_y = lax.rem(y + k, ys)
            grads = dkv_all[pl.ds(from_y * 2, 2), part].reshape(2 * rows, PCOLS)
            term = jnp.dot(hid_t[from_y], grads, preferred_element_type=FULL)
            if k > 0:
                term = prod[part] + term
            prod[part] = term
            if k == 2:
                prod_s[part] = term.astype(LOW)
        if part in TWO_STEP:
            rx_copy(part).start()
        else:
            each(1, summed_over, lambda o: rs_copy(part, o).start())

    def combine(part):
        settle(rx_r.at[part], rx_recv.at[part])
        at = pl.ds(x_hi * half_rows, half_rows)
        both = prod[part, at, :] + rx_r[part].astype(FULL)
        prod[part, at, :] = both
        prod_s[part, at, :] = both.astype(LOW)
        each(1, group_size, lambda o: rs_copy(part, o).start())

    pass_on(ORDER[0])
    for i, part in enumerate(ORDER):
        if i + 1 < PARTS:
            pass_on(ORDER[i + 1])
        hand_far(part)
        multiply(part)
        if i > 0 and ORDER[i - 1] in TWO_STEP:
            combine(ORDER[i - 1])

    dg_r[me] = dg_s[me]
    settle(dg_r.at[seven], dg_recv)
    dk_rows = jnp.concatenate([merge(dg_r, 0, g) for g in range(KVH)], axis=1)
    dv_rows = jnp.concatenate([merge(dg_r, 1, g) for g in range(KVH)], axis=1)

    def hidden_tile(t):
        at = pl.ds(pl.multiple_of(t * 512, 512), 512)
        tile = lax.dot_general(
            dk_rows, kw_v[at, :], NT, preferred_element_type=FULL
        ) + lax.dot_general(dv_rows, vw_v[at, :], NT, preferred_element_type=FULL)
        gh_v[:, at] = tile.astype(LOW)

    each(0, width // 512, hidden_tile)
    gh_out = pltpu.make_async_copy(gh_v, grad_hidden, gh_sem)
    gh_out.start()

    settle(dg_s.at[seven], dg_send)
    settle(dl_s.at[seven], dl_send)
    settle(dq_g.at[:, pl.ds(0, others), :], dq_send)
    settle(dq_g.at[:, pl.ds(0, others), :], dq_recv)
    settle(dq_g.at[:, pl.ds(0, rows), :], dq_own)
    settle(dkv_all.at[pl.ds(0, 2)], ya_send)
    settle(dkv_all.at[0, 0], ya_send)
    settle(dkv_all.at[0, pl.ds(0, PARTS - 1)], yf_send)
    settle(dkv_all.at[pl.ds(0, ys)], yc_send)

    norm = 1.0 / math.sqrt(total * replica_count)
    own = pl.ds(pl.multiple_of((x_hi * group_size + me) * piece, piece), piece)
    for part in ORDER:
        senders = group_size if part in TWO_STEP else summed_over
        settle(rs_r.at[part, pl.ds(0, senders - 1)], rs_recv.at[part])
        summed = prod[part, own, :]
        for o in range(1, senders):
            summed = summed + rs_r[part, o].astype(FULL)
        result = grad_value if part * PCOLS >= kvw else grad_key
        at = part * PCOLS % kvw
        result[:, at : at + PCOLS] = (summed * norm).astype(LOW)

    gh_out.wait()
    for part in range(PARTS):
        senders = group_size if part in TWO_STEP else summed_over
        settle(rs_r.at[part, pl.ds(0, senders - 1)], rs_send)
    for part in TWO_STEP:
        settle(rx_r.at[part], rx_send)


def hand_over(*refs):
    sources, results = refs[0:4], refs[4:8]
    held, sems = refs[8:12], refs[12]
    steps = []
    for i, (source, result, slot) in enumerate(zip(sources, results, held)):
        parts = 4 if i < 2 else 1
        size = source.shape[0] // parts
        for j in range(parts):
            at = pl.ds(j * size, size)
            steps.append(
                (
                    pltpu.make_async_copy(source.at[at], slot.at[at], sems.at[0, i, j]),
                    pltpu.make_async_copy(slot.at[at], result.at[at], sems.at[1, i, j]),
                )
            )
    for load, _ in steps:
        load.start()
    for load, store in steps:
        load.wait()
        store.start()
    for _, store in steps:
        store.wait()


def on_device(
    hidden, queries, out_grad, key_weight, value_weight, seq_lengths, seq_group, loader_offsets
):
    group_size = lax.axis_size("grp")
    replica_count = lax.axis_size("dp")
    rows, width = hidden.shape[1:]
    total = rows * group_size
    heads = HQ // group_size
    kvw = KVH * HD
    piece = width // (group_size * replica_count)
    blocks = total // QBLK
    ys = replica_count // 4
    column = 2 * ys
    chunk = width // column
    tall = sum((b + 1) * QBLK for b in range(blocks))
    dma = pltpu.SemaphoreType.DMA
    scratch = [
        pltpu.VMEM((rows, width), LOW),
        pltpu.VMEM((width, kvw), LOW),
        pltpu.VMEM((width, kvw), LOW),
        pltpu.VMEM((heads, 2, total, HD), LOW),
        pltpu.VMEM((KVH, 2, rows, HD), LOW),
        pltpu.VMEM((2, total, HD), LOW),
        pltpu.VMEM((HD, total), LOW),
        pltpu.VMEM((column, chunk, rows), LOW),
        pltpu.VMEM((ys, chunk, 2 * rows), LOW),
        pltpu.VMEM((tall, QBLK), FULL),
        pltpu.VMEM((tall, QBLK), FULL),
        pltpu.VMEM((tall, QBLK), LOW),
        pltpu.VMEM((tall, QBLK), LOW),
        pltpu.VMEM((2, total, HD), FULL),
        pltpu.VMEM((group_size, rows, HD), LOW),
        pltpu.VMEM((heads, total, HD), LOW),
        pltpu.VMEM((group_size, 2, rows, HD), LOW),
        pltpu.VMEM((group_size, 2, rows, HD), LOW),
        pltpu.VMEM((group_size, 2, rows, HD), LOW),
        pltpu.VMEM((group_size, 2, rows, HD), LOW),
        pltpu.VMEM((column, PARTS, rows, PCOLS), LOW),
        pltpu.VMEM((PARTS, chunk, PCOLS), FULL),
        pltpu.VMEM((PARTS, chunk, PCOLS), LOW),
        pltpu.VMEM((PARTS, chunk // 2, PCOLS), LOW),
        pltpu.VMEM((PARTS, 2 * group_size, piece, PCOLS), LOW),
        pltpu.VMEM((rows, width), LOW),
        pltpu.VMEM((1, total), jnp.int32),
        pltpu.VMEM((8, QBLK), FULL),
        dma((3,)),
        dma,
        dma((heads, 2)),
        dma,
        dma,
        dma,
        dma,
        dma,
        dma,
        dma,
        dma,
        dma((2,)),
        dma,
        dma,
        dma,
        dma((PARTS, 3)),
        dma,
        dma((PARTS,)),
        dma,
        dma((PARTS, ys)),
        dma,
        dma((PARTS,)),
        dma,
        dma((PARTS,)),
        dma,
    ]
    smem = pl.BlockSpec(memory_space=pltpu.SMEM)
    vmem = pl.BlockSpec(memory_space=pltpu.VMEM)
    anywhere = pl.BlockSpec(memory_space=pl.ANY)

    def kernel(*refs):
        layer_kernel(group_size, replica_count, *refs)

    out_shape = (
        jax.ShapeDtypeStruct((rows, HQ * HD), LOW),
        jax.ShapeDtypeStruct((rows, width), LOW),
        jax.ShapeDtypeStruct((piece, kvw), LOW),
        jax.ShapeDtypeStruct((piece, kvw), LOW),
    )
    results = pl.pallas_call(
        kernel,
        out_shape=out_shape,
        in_specs=[smem, smem, smem] + [anywhere] * 5,
        out_specs=(anywhere, anywhere, vmem, vmem),
        scratch_shapes=scratch,
        compiler_params=pltpu.CompilerParams(
            collective_id=0, has_side_effects=True, vmem_limit_bytes=56 * 1024 * 1024
        ),
        name="layer",
    )(
        seq_lengths,
        seq_group,
        loader_offsets,
        hidden[0],
        queries[0],
        out_grad[0],
        key_weight,
        value_weight,
    )
    grad_query, grad_hidden, grad_key, grad_value = pl.pallas_call(
        hand_over,
        out_shape=out_shape,
        in_specs=[anywhere] * 4,
        out_specs=[anywhere] * 4,
        scratch_shapes=[pltpu.VMEM(shape.shape, LOW) for shape in out_shape] + [dma((2, 4, 4))],
        name="hand_over",
    )(*results)
    return (grad_query[None], grad_hidden[None], grad_key, grad_value)


def solution(mesh):
    placed = (
        P("dp", "grp", None),
        P("dp", "grp", None),
        P("dp", "grp", None),
        P(),
        P(),
        P("dp", None),
        P("dp", None),
        P("dp", None),
    )
    return jax.shard_map(
        on_device,
        mesh=mesh,
        in_specs=placed,
        out_specs=(
            P("dp", "grp", None),
            P("dp", "grp", None),
            P(("grp", "dp"), None),
            P(("grp", "dp"), None),
        ),
        check_vma=False,
    )
```

```python
import math

import jax
import jax.numpy as jnp
from jax import lax
from jax.experimental import pallas as pl
from jax.experimental.pallas import tpu as pltpu
from jax.sharding import PartitionSpec as P

HQ = 32
KVH = 4
HD = 128
SLOTS = 8
QBLK = 256
ZS = 4
PARTS = 4
PCOLS = 2 * KVH * HD // PARTS
TWO_STEP = (2,)
ORDER = (2, 3, 0, 1)
LOW = jnp.bfloat16
FULL = jnp.float32
MESH = pl.DeviceIdType.MESH
NT = (((1,), (1,)), ((), ()))


def each(first, last, step):
    def body(i, carry):
        step(i)
        return carry

    lax.fori_loop(first, last, body, 0)


def layer_kernel(
    group_size,
    replica_count,
    lengths,
    groups,
    offsets,
    hidden,
    queries,
    out_grad,
    key_weight,
    value_weight,
    grad_query,
    grad_hidden,
    grad_key,
    grad_value,
    hid_v,
    kw_v,
    vw_v,
    qd_r,
    kv_s,
    kv_r,
    kt_v,
    hid_s,
    hid_t,
    s_v,
    pg_v,
    wl_v,
    ds_v,
    acc,
    dq_s,
    dq_g,
    dl_s,
    dl_r,
    dg_s,
    dg_r,
    dkv_all,
    prod,
    prod_s,
    rx_r,
    rs_r,
    gh_v,
    begin_v,
    inv_v,
    load_sem,
    in_send,
    in_recv,
    kv_send,
    kv_recv,
    hid_send,
    hid_recv,
    dq_send,
    dq_recv,
    dq_own,
    dl_send,
    dl_recv,
    dg_send,
    dg_recv,
    ya_send,
    ya_recv,
    yf_send,
    yf_recv,
    yc_send,
    yc_recv,
    rx_send,
    rx_recv,
    rs_send,
    rs_recv,
    gh_sem,
):
    me = lax.axis_index("grp")
    rep = lax.axis_index("dp")
    x_lo, z = me // ZS, lax.rem(me, ZS)
    y, x_hi, core = rep // 4, lax.rem(rep // 2, 2), lax.rem(rep, 2)
    ys = replica_count // 4
    column = 2 * ys
    summed_over = 2 * group_size
    rows = hidden.shape[0]
    width = hidden.shape[1]
    total = rows * group_size
    heads = HQ // group_size
    wide = heads * HD
    kvw = KVH * HD
    piece = width // (group_size * replica_count)
    half_rows = group_size * piece
    inv_root = 1.0 / math.sqrt(HD)
    exp_scale = inv_root / math.log(2.0)
    blocks = total // QBLK
    per_block = QBLK // rows

    def peer(o):
        return lax.rem(x_lo + o // ZS, 2) * ZS + lax.rem(z + o, ZS)

    def origin(o):
        return lax.rem(x_lo + o // ZS, 2) * ZS + lax.rem(z - o + 2 * ZS, ZS)

    def place(at_y, at_x_hi, at_core):
        return (at_y * 2 + at_x_hi) * 2 + at_core

    def first_col(device):
        return lax.rem(device, KVH) * (2 * wide) + (device // KVH) * wide

    def rows_of(block):
        return pl.ds(pl.multiple_of(block * rows, rows), rows)

    def cols(at, n):
        return pl.ds(pl.multiple_of(at, n), n)

    load_hid = pltpu.make_async_copy(hidden, hid_v, load_sem.at[0])
    load_kw = pltpu.make_async_copy(key_weight, kw_v, load_sem.at[1])
    load_vw = pltpu.make_async_copy(value_weight, vw_v, load_sem.at[2])
    load_hid.start()
    load_kw.start()
    load_vw.start()

    barrier = pltpu.get_barrier_semaphore()

    def column_peer(o):
        return place(lax.rem(y + o // 2, ys), x_hi, lax.rem(core + o, 2))

    def column_origin(o):
        return lax.rem(y - o // 2 + ys, ys), lax.rem(core + o, 2)

    def sum_peer(o):
        return {
            "grp": peer(lax.rem(o, group_size)),
            "dp": place(y, lax.rem(x_hi + o // group_size, 2), core),
        }

    each(
        1,
        column,
        lambda o: pl.semaphore_signal(
            barrier, inc=1, device_id={"dp": column_peer(o)}, device_id_type=MESH
        ),
    )
    each(
        1,
        summed_over,
        lambda o: pl.semaphore_signal(
            barrier, inc=1, device_id=sum_peer(o), device_id_type=MESH
        ),
    )

    across = {"grp": lax.rem(me + ZS, group_size), "dp": place(y, 1 - x_hi, core)}

    def q_copy(h, o, to):
        dest = peer(o)
        at = rows_of(me if to else origin(o))
        return pltpu.make_async_remote_copy(
            src_ref=queries.at[:, cols(first_col(dest) + h * HD, HD)],
            dst_ref=qd_r.at[h, 0, at, :],
            send_sem=in_send,
            recv_sem=in_recv.at[h, 0],
            device_id={"grp": dest},
            device_id_type=MESH,
        )

    def do_copy(h, o, to):
        dest = peer(o)
        at = rows_of(me if to else origin(o))
        return pltpu.make_async_remote_copy(
            src_ref=out_grad.at[:, cols(first_col(dest) + h * HD, HD)],
            dst_ref=qd_r.at[h, 1, at, :],
            send_sem=in_send,
            recv_sem=in_recv.at[h, 1],
            device_id={"grp": dest},
            device_id_type=MESH,
        )

    def kv_copy(o, to):
        dest = peer(o)
        at = rows_of(me if to else origin(o))
        return pltpu.make_async_remote_copy(
            src_ref=kv_s.at[lax.rem(dest, KVH)],
            dst_ref=kv_r.at[:, at, :],
            send_sem=kv_send,
            recv_sem=kv_recv,
            device_id={"grp": dest},
            device_id_type=MESH,
        )

    def hid_copy(o, to):
        dest_y, dest_core = lax.rem(y + o // 2, ys), lax.rem(core + o, 2)
        from_y, from_core = (y, core) if to else column_origin(o)
        return pltpu.make_async_remote_copy(
            src_ref=hid_s.at[dest_y * 2 + dest_core],
            dst_ref=hid_t.at[from_y, :, cols(from_core * rows, rows)],
            send_sem=hid_send,
            recv_sem=hid_recv,
            device_id={"dp": column_peer(o)},
            device_id_type=MESH,
        )

    def dq_copy(h, o, to):
        dest = peer(o)
        at = first_col(me if to else origin(o)) + h * HD
        return pltpu.make_async_remote_copy(
            src_ref=dq_g.at[h, rows_of(dest), :],
            dst_ref=grad_query.at[:, cols(at, HD)],
            send_sem=dq_send,
            recv_sem=dq_recv,
            device_id={"grp": dest},
            device_id_type=MESH,
        )

    def dq_stay(h):
        return pltpu.make_async_copy(
            dq_g.at[h, rows_of(me), :],
            grad_query.at[:, cols(first_col(me) + h * HD, HD)],
            dq_own,
        )

    def dl_copy(part, dest):
        return pltpu.make_async_remote_copy(
            src_ref=dl_s.at[dest, part],
            dst_ref=dl_r.at[me, part],
            send_sem=dl_send,
            recv_sem=dl_recv.at[part],
            device_id={"grp": dest},
            device_id_type=MESH,
        )

    def dg_copy(o, to):
        dest = peer(o)
        return pltpu.make_async_remote_copy(
            src_ref=dg_s.at[dest],
            dst_ref=dg_r.at[me if to else origin(o)],
            send_sem=dg_send,
            recv_sem=dg_recv,
            device_id={"grp": dest},
            device_id_type=MESH,
        )

    def ya_copy(part, k, to):
        step = (1, ys - 1, 2)[k]
        at = (y if to else lax.rem(y + ys - step, ys)) * 2 + core
        return pltpu.make_async_remote_copy(
            src_ref=dkv_all.at[y * 2 + core, part],
            dst_ref=dkv_all.at[at, part],
            send_sem=ya_send,
            recv_sem=ya_recv.at[part, k],
            device_id={"dp": place(lax.rem(y + step, ys), x_hi, core)},
            device_id_type=MESH,
        )

    def yf_copy(part, k, to):
        step = ys - 1 if k else 1
        come = lax.rem(y + ys - step, ys) * 2 + core
        far = lax.rem(y + 2, ys) * 2 + core
        half = pl.ds(k * (rows // 2), rows // 2)
        return pltpu.make_async_remote_copy(
            src_ref=dkv_all.at[come, part, half],
            dst_ref=dkv_all.at[come if to else far, part, half],
            send_sem=yf_send,
            recv_sem=yf_recv.at[part],
            device_id={"dp": place(lax.rem(y + step, ys), x_hi, core)},
            device_id_type=MESH,
        )

    def yc_copy(part, k, to):
        from_y = lax.rem(y + k, ys)
        return pltpu.make_async_remote_copy(
            src_ref=dkv_all.at[from_y * 2 + core, part],
            dst_ref=dkv_all.at[from_y * 2 + (core if to else 1 - core), part],
            send_sem=yc_send,
            recv_sem=yc_recv.at[part, k],
            device_id={"dp": place(y, x_hi, 1 - core)},
            device_id_type=MESH,
        )

    def rs_copy(part, o):
        dest = sum_peer(o)
        at = lax.rem(x_hi + o // group_size, 2) * group_size + dest["grp"]
        return pltpu.make_async_remote_copy(
            src_ref=prod_s.at[part, pl.ds(pl.multiple_of(at * piece, piece), piece), :],
            dst_ref=rs_r.at[part, o],
            send_sem=rs_send,
            recv_sem=rs_recv.at[part],
            device_id=dest,
            device_id_type=MESH,
        )

    def settle(ref, sem):
        pltpu.make_async_copy(ref, ref, sem).wait()

    others = total - rows
    seven = pl.ds(0, group_size - 1)

    def rx_copy(part):
        return pltpu.make_async_remote_copy(
            src_ref=prod_s.at[part, pl.ds((1 - x_hi) * half_rows, half_rows), :],
            dst_ref=rx_r.at[part],
            send_sem=rx_send,
            recv_sem=rx_recv.at[part],
            device_id=across,
            device_id_type=MESH,
        )

    def own_q(h):
        return pltpu.make_async_copy(
            queries.at[:, cols(first_col(me) + h * HD, HD)],
            qd_r.at[h, 0, rows_of(me), :],
            in_recv.at[h, 0],
        )

    def own_do(h):
        return pltpu.make_async_copy(
            out_grad.at[:, cols(first_col(me) + h * HD, HD)],
            qd_r.at[h, 1, rows_of(me), :],
            in_recv.at[h, 1],
        )

    def send_head(h):
        each(1, group_size, lambda o: q_copy(h, o, True).start())
        each(1, group_size, lambda o: do_copy(h, o, True).start())

    pl.semaphore_wait(barrier, column - 1 + summed_over - 1)
    send_head(0)

    load_hid.wait()
    load_kw.wait()
    hid_rows = hid_v[...]

    def project(weight, which):
        for g in range(0, KVH, 2):
            both = jnp.dot(
                hid_rows, weight[:, g * HD : (g + 2) * HD], preferred_element_type=FULL
            ).astype(LOW)
            kv_s[g, which] = both[:, :HD]
            kv_s[g + 1, which] = both[:, HD:]

    project(kw_v, 0)
    load_vw.wait()
    project(vw_v, 1)

    each(1, group_size, lambda o: kv_copy(o, True).start())
    each(1, heads, send_head)
    for h in range(heads):
        own_q(h).start()
        own_do(h).start()
    kv_r[:, rows_of(me), :] = kv_s[lax.rem(me, KVH)]

    lanes = 4 * piece

    def turn(t):
        turned = hid_v[:, cols(t * lanes, lanes)].T
        g = t // ys
        to_y = lax.rem(t, ys)
        for xh in range(2):
            at = pl.ds(pl.multiple_of((xh * group_size + g) * piece, piece), piece)
            for c in range(2):
                hid_s[to_y * 2 + c, at, :] = turned[(xh * 2 + c) * piece :][:piece]

    each(0, width // lanes, turn)
    each(1, column, lambda o: hid_copy(o, True).start())
    hid_t[y, :, cols(core * rows, rows)] = hid_s[y * 2 + core]

    row_ids = lax.broadcasted_iota(jnp.int32, (1, total), 1)
    begin = jnp.zeros((1, total), jnp.int32)
    for s in range(SLOTS):
        at, size = offsets[0, s], lengths[0, s]
        begin = jnp.where((row_ids >= at) & (row_ids < at + size), at, begin)
    begin_v[...] = begin
    starts = []
    for s in range(SLOTS):
        start = jnp.int32(0)
        for t in range(SLOTS):
            if t < s:
                before = groups[0, t] <= groups[0, s]
            else:
                before = groups[0, t] < groups[0, s]
            if t != s:
                start = start + jnp.where(before, lengths[0, t], 0)
        starts.append(start)

    def source_block(row):
        found = jnp.int32(0)
        for s in range(SLOTS):
            inside = (row >= starts[s]) & (row < starts[s] + lengths[0, s])
            found = found + jnp.where(inside, offsets[0, s] + row - starts[s], 0)
        return found // rows

    sources = [source_block(b * rows) for b in range(group_size)]

    acc[...] = jnp.zeros_like(acc)
    settle(kv_r.at[:, pl.ds(0, others), :], kv_recv)
    kt_v[...] = kv_r[0].T

    key_ids = lax.broadcasted_iota(jnp.int32, (HD, QBLK), 0)
    lane_ids = lax.broadcasted_iota(jnp.int32, (HD, QBLK), 1)

    def fold(tile):
        return tile.reshape(HD // 8, 8, QBLK)

    def span(b):
        first = sum((i + 1) * QBLK for i in range(b))
        return first, (b + 1) * QBLK

    def weigh(h, b):
        r0 = b * QBLK
        first, keys = span(b)
        q_blk = qd_r[h, 0, r0 : r0 + QBLK, :]
        begin_row = begin_v[:, r0 : r0 + QBLK]
        top = jnp.full((8, QBLK), -1e30, FULL)
        for j in range(0, keys, QBLK):
            block = lax.dot_general(
                kv_r[0, j : j + QBLK, :], q_blk, NT, preferred_element_type=FULL
            )
            for i in range(j, j + QBLK, HD):
                seen = key_ids + i >= begin_row
                if j >= r0:
                    seen = seen & (key_ids + (i - r0) <= lane_ids)
                tile = jnp.where(seen, block[i - j : i - j + HD], -1e30)
                s_v[first + i : first + i + HD, :] = tile
                top = jnp.maximum(top, jnp.max(fold(tile), axis=0))
        top = jnp.max(top, axis=0, keepdims=True)
        mass = jnp.zeros((8, QBLK), FULL)
        for j in range(keys // HD):
            at = slice(first + j * HD, first + (j + 1) * HD)
            tile = jnp.exp2((s_v[at, :] - top) * exp_scale)
            s_v[at, :] = tile
            mass = mass + jnp.sum(fold(tile), axis=0)
        inverse = 1.0 / jnp.sum(mass, axis=0, keepdims=True)
        inv_v[b : b + 1, :] = inverse
        for j in range(keys // HD):
            at = slice(first + j * HD, first + (j + 1) * HD)
            wl_v[at, :] = (s_v[at, :] * inverse).astype(LOW)

    def value_grad(h, b):
        r0 = b * QBLK
        first, keys = span(b)
        acc[1, 0:keys, :] += jnp.dot(
            wl_v[first : first + keys, :],
            qd_r[h, 1, r0 : r0 + QBLK, :],
            preferred_element_type=FULL,
        )

    def send_terms(part, first_block, last_block):
        for j in range(first_block, last_block):
            term = acc[part, j * rows : (j + 1) * rows, :]
            if part == 0:
                term = term * inv_root
            dl_s[j, part] = term.astype(LOW)

            @pl.when(me != j)
            def _():
                dl_copy(part, j).start()

    def attend(h, b):
        r0 = b * QBLK
        first, keys = span(b)
        q_blk = qd_r[h, 0, r0 : r0 + QBLK, :]
        do_blk = qd_r[h, 1, r0 : r0 + QBLK, :]
        delta = jnp.zeros((8, QBLK), FULL)
        for j in range(0, keys, QBLK):
            at = slice(first + j, first + j + QBLK)
            block = lax.dot_general(
                kv_r[1, j : j + QBLK, :], do_blk, NT, preferred_element_type=FULL
            )
            pg_v[at, :] = block
            terms = wl_v[at, :].astype(FULL) * block
            delta = delta + jnp.sum(terms.reshape(QBLK // 8, 8, QBLK), axis=0)
        delta = jnp.sum(delta, axis=0, keepdims=True)
        inverse = inv_v[b : b + 1, :]
        for j in range(keys // HD):
            at = slice(first + j * HD, first + (j + 1) * HD)
            ds_v[at, :] = (s_v[at, :] * inverse * (pg_v[at, :] - delta)).astype(LOW)
        all_keys = slice(first, first + keys)
        acc[0, 0:keys, :] += jnp.dot(ds_v[all_keys, :], q_blk, preferred_element_type=FULL)

    def query_grad(b):
        r0 = b * QBLK
        first, keys = span(b)
        grad_t = jnp.dot(
            kt_v[:, 0:keys], ds_v[first : first + keys, :], preferred_element_type=FULL
        )
        grad_rows = (grad_t * inv_root).T.astype(LOW)
        for j in range(per_block):
            dq_s[r0 // rows + j] = grad_rows[j * rows : (j + 1) * rows, :]

    def send_dq(h):
        each(1, group_size, lambda o: dq_copy(h, o, True).start())
        dq_stay(h).start()

    def one_head(h):
        settle(qd_r.at[h, 0], in_recv.at[h, 0])
        for b in reversed(range(blocks)):
            weigh(h, b)
        settle(qd_r.at[h, 1], in_recv.at[h, 1])

        for b in reversed(range(blocks)):
            value_grad(h, b)

        @pl.when(h == heads - 1)
        def _():
            send_terms(1, 0, group_size)

        for b in reversed(range(blocks)):
            attend(h, b)

            @pl.when(h == heads - 1)
            def _():
                send_terms(0, b * per_block, (b + 1) * per_block)

        for b in range(blocks):
            query_grad(b)
        for b in range(group_size):
            dq_g[h, b * rows : (b + 1) * rows, :] = dq_s[sources[b]]

    each(0, heads, one_head)

    each(0, 2, send_dq)
    for b in range(group_size):
        dg_s[b] = dl_s[sources[b]]
    each(1, group_size, lambda o: dg_copy(o, True).start())
    dl_r[me] = dl_s[me]

    def merge(received, part, g):
        return (
            received[g, part].astype(FULL) + received[KVH + g, part].astype(FULL)
        ).astype(LOW)

    last = ORDER[-1]

    def gather(part):
        which = part * PCOLS // kvw
        for i in range(PCOLS // HD):
            dkv_all[y * 2 + core, part, :, i * HD : (i + 1) * HD] = merge(
                dl_r, which, (part * PCOLS % kvw) // HD + i
            )
        for k in range(3 if part == last else 2):
            ya_copy(part, k, True).start()
        yc_copy(part, 0, True).start()

    settle(dl_r.at[seven, 1], dl_recv.at[1])
    for part in ORDER[: PARTS // 2]:
        gather(part)
    settle(dl_r.at[seven, 0], dl_recv.at[0])
    for part in ORDER[PARTS // 2 :]:
        gather(part)

    each(2, heads, send_dq)
    settle(kv_r.at[:, pl.ds(0, others), :], kv_send)
    settle(qd_r.at[:, :, pl.ds(0, others), :], in_send)
    settle(hid_s.at[pl.ds(0, column - 1)], hid_send)

    settle(hid_s.at[pl.ds(0, column - 1)], hid_recv)
    def pass_on(part):
        for k in range(2):
            ya_copy(part, k, False).wait_recv()
            if part != last:
                yf_copy(part, k, True).start()
            yc_copy(part, 1 if k else ys - 1, True).start()

    def hand_far(part):
        if part != last:
            settle(dkv_all.at[0, part], yf_recv.at[part])
        else:
            ya_copy(part, 2, False).wait_recv()
        yc_copy(part, 2, True).start()

    def multiply(part):
        for k in (0, 1, ys - 1, 2):
            yc_copy(part, k, False).wait_recv()
            from_y = lax.rem(y + k, ys)
            grads = dkv_all[pl.ds(from_y * 2, 2), part].reshape(2 * rows, PCOLS)
            term = jnp.dot(hid_t[from_y], grads, preferred_element_type=FULL)
            if k > 0:
                term = prod[part] + term
            prod[part] = term
            if k == 2:
                prod_s[part] = term.astype(LOW)
        if part in TWO_STEP:
            rx_copy(part).start()
        else:
            each(1, summed_over, lambda o: rs_copy(part, o).start())

    def combine(part):
        settle(rx_r.at[part], rx_recv.at[part])
        at = pl.ds(x_hi * half_rows, half_rows)
        both = prod[part, at, :] + rx_r[part].astype(FULL)
        prod[part, at, :] = both
        prod_s[part, at, :] = both.astype(LOW)
        each(1, group_size, lambda o: rs_copy(part, o).start())

    pass_on(ORDER[0])
    for i, part in enumerate(ORDER):
        if i + 1 < PARTS:
            pass_on(ORDER[i + 1])
        hand_far(part)
        multiply(part)
        if i > 0 and ORDER[i - 1] in TWO_STEP:
            combine(ORDER[i - 1])

    dg_r[me] = dg_s[me]
    settle(dg_r.at[seven], dg_recv)
    dk_rows = jnp.concatenate([merge(dg_r, 0, g) for g in range(KVH)], axis=1)
    dv_rows = jnp.concatenate([merge(dg_r, 1, g) for g in range(KVH)], axis=1)

    def hidden_tile(t):
        at = pl.ds(pl.multiple_of(t * 512, 512), 512)
        tile = lax.dot_general(
            dk_rows, kw_v[at, :], NT, preferred_element_type=FULL
        ) + lax.dot_general(dv_rows, vw_v[at, :], NT, preferred_element_type=FULL)
        gh_v[:, at] = tile.astype(LOW)

    each(0, width // 512, hidden_tile)
    gh_out = pltpu.make_async_copy(gh_v, grad_hidden, gh_sem)
    gh_out.start()

    settle(dg_s.at[seven], dg_send)
    settle(dl_s.at[seven], dl_send)
    settle(dq_g.at[:, pl.ds(0, others), :], dq_send)
    settle(dq_g.at[:, pl.ds(0, others), :], dq_recv)
    settle(dq_g.at[:, pl.ds(0, rows), :], dq_own)
    settle(dkv_all.at[pl.ds(0, 2)], ya_send)
    settle(dkv_all.at[0, 0], ya_send)
    settle(dkv_all.at[0, pl.ds(0, PARTS - 1)], yf_send)
    settle(dkv_all.at[pl.ds(0, ys)], yc_send)

    norm = 1.0 / math.sqrt(total * replica_count)
    own = pl.ds(pl.multiple_of((x_hi * group_size + me) * piece, piece), piece)
    for part in ORDER:
        senders = group_size if part in TWO_STEP else summed_over
        settle(rs_r.at[part, pl.ds(0, senders - 1)], rs_recv.at[part])
        summed = prod[part, own, :]
        for o in range(1, senders):
            summed = summed + rs_r[part, o].astype(FULL)
        result = grad_value if part * PCOLS >= kvw else grad_key
        at = part * PCOLS % kvw
        result[:, at : at + PCOLS] = (summed * norm).astype(LOW)

    gh_out.wait()
    for part in range(PARTS):
        senders = group_size if part in TWO_STEP else summed_over
        settle(rs_r.at[part, pl.ds(0, senders - 1)], rs_send)
    for part in TWO_STEP:
        settle(rx_r.at[part], rx_send)


def hand_over(*refs):
    sources, results = refs[0:4], refs[4:8]
    held, sems = refs[8:12], refs[12]
    steps = []
    for i, (source, result, slot) in enumerate(zip(sources, results, held)):
        parts = 4 if i < 2 else 1
        size = source.shape[0] // parts
        for j in range(parts):
            at = pl.ds(j * size, size)
            steps.append(
                (
                    pltpu.make_async_copy(source.at[at], slot.at[at], sems.at[0, i, j]),
                    pltpu.make_async_copy(slot.at[at], result.at[at], sems.at[1, i, j]),
                )
            )
    for load, _ in steps:
        load.start()
    for load, store in steps:
        load.wait()
        store.start()
    for _, store in steps:
        store.wait()


def on_device(
    hidden, queries, out_grad, key_weight, value_weight, seq_lengths, seq_group, loader_offsets
):
    group_size = lax.axis_size("grp")
    replica_count = lax.axis_size("dp")
    rows, width = hidden.shape[1:]
    total = rows * group_size
    heads = HQ // group_size
    kvw = KVH * HD
    piece = width // (group_size * replica_count)
    blocks = total // QBLK
    ys = replica_count // 4
    column = 2 * ys
    chunk = width // column
    tall = sum((b + 1) * QBLK for b in range(blocks))
    dma = pltpu.SemaphoreType.DMA
    scratch = [
        pltpu.VMEM((rows, width), LOW),
        pltpu.VMEM((width, kvw), LOW),
        pltpu.VMEM((width, kvw), LOW),
        pltpu.VMEM((heads, 2, total, HD), LOW),
        pltpu.VMEM((KVH, 2, rows, HD), LOW),
        pltpu.VMEM((2, total, HD), LOW),
        pltpu.VMEM((HD, total), LOW),
        pltpu.VMEM((column, chunk, rows), LOW),
        pltpu.VMEM((ys, chunk, 2 * rows), LOW),
        pltpu.VMEM((tall, QBLK), FULL),
        pltpu.VMEM((tall, QBLK), FULL),
        pltpu.VMEM((tall, QBLK), LOW),
        pltpu.VMEM((tall, QBLK), LOW),
        pltpu.VMEM((2, total, HD), FULL),
        pltpu.VMEM((group_size, rows, HD), LOW),
        pltpu.VMEM((heads, total, HD), LOW),
        pltpu.VMEM((group_size, 2, rows, HD), LOW),
        pltpu.VMEM((group_size, 2, rows, HD), LOW),
        pltpu.VMEM((group_size, 2, rows, HD), LOW),
        pltpu.VMEM((group_size, 2, rows, HD), LOW),
        pltpu.VMEM((column, PARTS, rows, PCOLS), LOW),
        pltpu.VMEM((PARTS, chunk, PCOLS), FULL),
        pltpu.VMEM((PARTS, chunk, PCOLS), LOW),
        pltpu.VMEM((PARTS, chunk // 2, PCOLS), LOW),
        pltpu.VMEM((PARTS, 2 * group_size, piece, PCOLS), LOW),
        pltpu.VMEM((rows, width), LOW),
        pltpu.VMEM((1, total), jnp.int32),
        pltpu.VMEM((8, QBLK), FULL),
        dma((3,)),
        dma,
        dma((heads, 2)),
        dma,
        dma,
        dma,
        dma,
        dma,
        dma,
        dma,
        dma,
        dma((2,)),
        dma,
        dma,
        dma,
        dma((PARTS, 3)),
        dma,
        dma((PARTS,)),
        dma,
        dma((PARTS, ys)),
        dma,
        dma((PARTS,)),
        dma,
        dma((PARTS,)),
        dma,
    ]
    smem = pl.BlockSpec(memory_space=pltpu.SMEM)
    vmem = pl.BlockSpec(memory_space=pltpu.VMEM)
    anywhere = pl.BlockSpec(memory_space=pl.ANY)

    def kernel(*refs):
        layer_kernel(group_size, replica_count, *refs)

    out_shape = (
        jax.ShapeDtypeStruct((rows, HQ * HD), LOW),
        jax.ShapeDtypeStruct((rows, width), LOW),
        jax.ShapeDtypeStruct((piece, kvw), LOW),
        jax.ShapeDtypeStruct((piece, kvw), LOW),
    )
    results = pl.pallas_call(
        kernel,
        out_shape=out_shape,
        in_specs=[smem, smem, smem] + [anywhere] * 5,
        out_specs=(anywhere, anywhere, vmem, vmem),
        scratch_shapes=scratch,
        compiler_params=pltpu.CompilerParams(
            collective_id=0, has_side_effects=True, vmem_limit_bytes=56 * 1024 * 1024
        ),
        name="layer",
    )(
        seq_lengths,
        seq_group,
        loader_offsets,
        hidden[0],
        queries[0],
        out_grad[0],
        key_weight,
        value_weight,
    )
    grad_query, grad_hidden, grad_key, grad_value = pl.pallas_call(
        hand_over,
        out_shape=out_shape,
        in_specs=[anywhere] * 4,
        out_specs=[anywhere] * 4,
        scratch_shapes=[pltpu.VMEM(shape.shape, LOW) for shape in out_shape] + [dma((2, 4, 4))],
        name="hand_over",
    )(*results)
    return (grad_query[None], grad_hidden[None], grad_key, grad_value)


def solution(mesh):
    placed = (
        P("dp", "grp", None),
        P("dp", "grp", None),
        P("dp", "grp", None),
        P(),
        P(),
        P("dp", None),
        P("dp", None),
        P("dp", None),
    )
    return jax.shard_map(
        on_device,
        mesh=mesh,
        in_specs=placed,
        out_specs=(
            P("dp", "grp", None),
            P("dp", "grp", None),
            P(("grp", "dp"), None),
            P(("grp", "dp"), None),
        ),
        check_vma=False,
    )
```

```python
import math

import jax
import jax.numpy as jnp
from jax import lax
from jax.experimental import pallas as pl
from jax.experimental.pallas import tpu as pltpu
from jax.sharding import PartitionSpec as P

HQ = 32
KVH = 4
HD = 128
SLOTS = 8
QBLK = 256
ZS = 4
PARTS = 4
PCOLS = 2 * KVH * HD // PARTS
TWO_STEP = (2,)
ORDER = (2, 3, 0, 1)
LOW = jnp.bfloat16
FULL = jnp.float32
MESH = pl.DeviceIdType.MESH
NT = (((1,), (1,)), ((), ()))


def each(first, last, step):
    def body(i, carry):
        step(i)
        return carry

    lax.fori_loop(first, last, body, 0)


def layer_kernel(
    group_size,
    replica_count,
    lengths,
    groups,
    offsets,
    hidden,
    queries,
    out_grad,
    key_weight,
    value_weight,
    grad_query,
    grad_hidden,
    grad_key,
    grad_value,
    hid_v,
    kw_v,
    vw_v,
    qd_r,
    kv_s,
    kv_r,
    kt_v,
    hid_s,
    hid_t,
    s_v,
    pg_v,
    wl_v,
    ds_v,
    acc,
    dq_s,
    dq_g,
    dl_s,
    dl_r,
    dg_s,
    dg_r,
    dkv_all,
    prod,
    prod_s,
    rx_r,
    rs_r,
    gh_v,
    begin_v,
    inv_v,
    load_sem,
    in_send,
    in_recv,
    kv_send,
    kv_recv,
    hid_send,
    hid_recv,
    dq_send,
    dq_recv,
    dq_own,
    dl_send,
    dl_recv,
    dg_send,
    dg_recv,
    ya_send,
    ya_recv,
    yf_send,
    yf_recv,
    yc_send,
    yc_recv,
    rx_send,
    rx_recv,
    rs_send,
    rs_recv,
    gh_sem,
):
    me = lax.axis_index("grp")
    rep = lax.axis_index("dp")
    x_lo, z = me // ZS, lax.rem(me, ZS)
    y, x_hi, core = rep // 4, lax.rem(rep // 2, 2), lax.rem(rep, 2)
    ys = replica_count // 4
    column = 2 * ys
    summed_over = 2 * group_size
    rows = hidden.shape[0]
    width = hidden.shape[1]
    total = rows * group_size
    heads = HQ // group_size
    wide = heads * HD
    kvw = KVH * HD
    piece = width // (group_size * replica_count)
    half_rows = group_size * piece
    inv_root = 1.0 / math.sqrt(HD)
    exp_scale = inv_root / math.log(2.0)
    blocks = total // QBLK
    per_block = QBLK // rows

    def peer(o):
        return lax.rem(x_lo + o // ZS, 2) * ZS + lax.rem(z + o, ZS)

    def origin(o):
        return lax.rem(x_lo + o // ZS, 2) * ZS + lax.rem(z - o + 2 * ZS, ZS)

    def place(at_y, at_x_hi, at_core):
        return (at_y * 2 + at_x_hi) * 2 + at_core

    def first_col(device):
        return lax.rem(device, KVH) * (2 * wide) + (device // KVH) * wide

    def rows_of(block):
        return pl.ds(pl.multiple_of(block * rows, rows), rows)

    def cols(at, n):
        return pl.ds(pl.multiple_of(at, n), n)

    load_hid = pltpu.make_async_copy(hidden, hid_v, load_sem.at[0])
    load_kw = pltpu.make_async_copy(key_weight, kw_v, load_sem.at[1])
    load_vw = pltpu.make_async_copy(value_weight, vw_v, load_sem.at[2])
    load_hid.start()
    load_kw.start()
    load_vw.start()

    barrier = pltpu.get_barrier_semaphore()

    def column_peer(o):
        return place(lax.rem(y + o // 2, ys), x_hi, lax.rem(core + o, 2))

    def column_origin(o):
        return lax.rem(y - o // 2 + ys, ys), lax.rem(core + o, 2)

    def sum_peer(o):
        return {
            "grp": peer(lax.rem(o, group_size)),
            "dp": place(y, lax.rem(x_hi + o // group_size, 2), core),
        }

    each(
        1,
        column,
        lambda o: pl.semaphore_signal(
            barrier, inc=1, device_id={"dp": column_peer(o)}, device_id_type=MESH
        ),
    )
    each(
        1,
        summed_over,
        lambda o: pl.semaphore_signal(
            barrier, inc=1, device_id=sum_peer(o), device_id_type=MESH
        ),
    )

    across = {"grp": lax.rem(me + ZS, group_size), "dp": place(y, 1 - x_hi, core)}

    def q_copy(h, o, to):
        dest = peer(o)
        at = rows_of(me if to else origin(o))
        return pltpu.make_async_remote_copy(
            src_ref=queries.at[:, cols(first_col(dest) + h * HD, HD)],
            dst_ref=qd_r.at[h, 0, at, :],
            send_sem=in_send,
            recv_sem=in_recv.at[h, 0],
            device_id={"grp": dest},
            device_id_type=MESH,
        )

    def do_copy(h, o, to):
        dest = peer(o)
        at = rows_of(me if to else origin(o))
        return pltpu.make_async_remote_copy(
            src_ref=out_grad.at[:, cols(first_col(dest) + h * HD, HD)],
            dst_ref=qd_r.at[h, 1, at, :],
            send_sem=in_send,
            recv_sem=in_recv.at[h, 1],
            device_id={"grp": dest},
            device_id_type=MESH,
        )

    def kv_copy(o, to):
        dest = peer(o)
        at = rows_of(me if to else origin(o))
        return pltpu.make_async_remote_copy(
            src_ref=kv_s.at[lax.rem(dest, KVH)],
            dst_ref=kv_r.at[:, at, :],
            send_sem=kv_send,
            recv_sem=kv_recv,
            device_id={"grp": dest},
            device_id_type=MESH,
        )

    def hid_copy(o, to):
        dest_y, dest_core = lax.rem(y + o // 2, ys), lax.rem(core + o, 2)
        from_y, from_core = (y, core) if to else column_origin(o)
        return pltpu.make_async_remote_copy(
            src_ref=hid_s.at[dest_y * 2 + dest_core],
            dst_ref=hid_t.at[from_y, :, cols(from_core * rows, rows)],
            send_sem=hid_send,
            recv_sem=hid_recv,
            device_id={"dp": column_peer(o)},
            device_id_type=MESH,
        )

    def dq_copy(h, o, to):
        dest = peer(o)
        at = first_col(me if to else origin(o)) + h * HD
        return pltpu.make_async_remote_copy(
            src_ref=dq_g.at[h, rows_of(dest), :],
            dst_ref=grad_query.at[:, cols(at, HD)],
            send_sem=dq_send,
            recv_sem=dq_recv,
            device_id={"grp": dest},
            device_id_type=MESH,
        )

    def dq_stay(h):
        return pltpu.make_async_copy(
            dq_g.at[h, rows_of(me), :],
            grad_query.at[:, cols(first_col(me) + h * HD, HD)],
            dq_own,
        )

    def dl_copy(part, dest):
        return pltpu.make_async_remote_copy(
            src_ref=dl_s.at[dest, part],
            dst_ref=dl_r.at[me, part],
            send_sem=dl_send,
            recv_sem=dl_recv.at[part],
            device_id={"grp": dest},
            device_id_type=MESH,
        )

    def dg_copy(o, to):
        dest = peer(o)
        return pltpu.make_async_remote_copy(
            src_ref=dg_s.at[dest],
            dst_ref=dg_r.at[me if to else origin(o)],
            send_sem=dg_send,
            recv_sem=dg_recv,
            device_id={"grp": dest},
            device_id_type=MESH,
        )

    def ya_copy(part, k, to):
        step = (1, ys - 1, 2)[k]
        at = (y if to else lax.rem(y + ys - step, ys)) * 2 + core
        return pltpu.make_async_remote_copy(
            src_ref=dkv_all.at[y * 2 + core, part],
            dst_ref=dkv_all.at[at, part],
            send_sem=ya_send,
            recv_sem=ya_recv.at[part, k],
            device_id={"dp": place(lax.rem(y + step, ys), x_hi, core)},
            device_id_type=MESH,
        )

    def yf_copy(part, k, to):
        step = ys - 1 if k else 1
        come = lax.rem(y + ys - step, ys) * 2 + core
        far = lax.rem(y + 2, ys) * 2 + core
        half = pl.ds(k * (rows // 2), rows // 2)
        return pltpu.make_async_remote_copy(
            src_ref=dkv_all.at[come, part, half],
            dst_ref=dkv_all.at[come if to else far, part, half],
            send_sem=yf_send,
            recv_sem=yf_recv.at[part],
            device_id={"dp": place(lax.rem(y + step, ys), x_hi, core)},
            device_id_type=MESH,
        )

    def yc_copy(part, k, to):
        from_y = lax.rem(y + k, ys)
        return pltpu.make_async_remote_copy(
            src_ref=dkv_all.at[from_y * 2 + core, part],
            dst_ref=dkv_all.at[from_y * 2 + (core if to else 1 - core), part],
            send_sem=yc_send,
            recv_sem=yc_recv.at[part, k],
            device_id={"dp": place(y, x_hi, 1 - core)},
            device_id_type=MESH,
        )

    def rs_copy(part, o):
        dest = sum_peer(o)
        at = lax.rem(x_hi + o // group_size, 2) * group_size + dest["grp"]
        return pltpu.make_async_remote_copy(
            src_ref=prod_s.at[part, pl.ds(pl.multiple_of(at * piece, piece), piece), :],
            dst_ref=rs_r.at[part, o],
            send_sem=rs_send,
            recv_sem=rs_recv.at[part],
            device_id=dest,
            device_id_type=MESH,
        )

    def settle(ref, sem):
        pltpu.make_async_copy(ref, ref, sem).wait()

    others = total - rows
    seven = pl.ds(0, group_size - 1)

    def rx_copy(part):
        return pltpu.make_async_remote_copy(
            src_ref=prod_s.at[part, pl.ds((1 - x_hi) * half_rows, half_rows), :],
            dst_ref=rx_r.at[part],
            send_sem=rx_send,
            recv_sem=rx_recv.at[part],
            device_id=across,
            device_id_type=MESH,
        )

    def own_q(h):
        return pltpu.make_async_copy(
            queries.at[:, cols(first_col(me) + h * HD, HD)],
            qd_r.at[h, 0, rows_of(me), :],
            in_recv.at[h, 0],
        )

    def own_do(h):
        return pltpu.make_async_copy(
            out_grad.at[:, cols(first_col(me) + h * HD, HD)],
            qd_r.at[h, 1, rows_of(me), :],
            in_recv.at[h, 1],
        )

    def send_head(h):
        each(1, group_size, lambda o: q_copy(h, o, True).start())
        each(1, group_size, lambda o: do_copy(h, o, True).start())

    pl.semaphore_wait(barrier, column - 1 + summed_over - 1)
    send_head(0)

    load_hid.wait()
    load_kw.wait()
    hid_rows = hid_v[...]

    def project(weight, which):
        for g in range(0, KVH, 2):
            both = jnp.dot(
                hid_rows, weight[:, g * HD : (g + 2) * HD], preferred_element_type=FULL
            ).astype(LOW)
            kv_s[g, which] = both[:, :HD]
            kv_s[g + 1, which] = both[:, HD:]

    project(kw_v, 0)
    load_vw.wait()
    project(vw_v, 1)

    each(1, group_size, lambda o: kv_copy(o, True).start())
    each(1, heads, send_head)
    for h in range(heads):
        own_q(h).start()
        own_do(h).start()
    kv_r[:, rows_of(me), :] = kv_s[lax.rem(me, KVH)]

    lanes = 4 * piece

    def turn(t):
        turned = hid_v[:, cols(t * lanes, lanes)].T
        g = t // ys
        to_y = lax.rem(t, ys)
        for xh in range(2):
            at = pl.ds(pl.multiple_of((xh * group_size + g) * piece, piece), piece)
            for c in range(2):
                hid_s[to_y * 2 + c, at, :] = turned[(xh * 2 + c) * piece :][:piece]

    each(0, width // lanes, turn)
    each(1, column, lambda o: hid_copy(o, True).start())
    hid_t[y, :, cols(core * rows, rows)] = hid_s[y * 2 + core]

    row_ids = lax.broadcasted_iota(jnp.int32, (1, total), 1)
    begin = jnp.zeros((1, total), jnp.int32)
    for s in range(SLOTS):
        at, size = offsets[0, s], lengths[0, s]
        begin = jnp.where((row_ids >= at) & (row_ids < at + size), at, begin)
    begin_v[...] = begin
    starts = []
    for s in range(SLOTS):
        start = jnp.int32(0)
        for t in range(SLOTS):
            if t < s:
                before = groups[0, t] <= groups[0, s]
            else:
                before = groups[0, t] < groups[0, s]
            if t != s:
                start = start + jnp.where(before, lengths[0, t], 0)
        starts.append(start)

    def source_block(row):
        found = jnp.int32(0)
        for s in range(SLOTS):
            inside = (row >= starts[s]) & (row < starts[s] + lengths[0, s])
            found = found + jnp.where(inside, offsets[0, s] + row - starts[s], 0)
        return found // rows

    sources = [source_block(b * rows) for b in range(group_size)]

    acc[...] = jnp.zeros_like(acc)
    settle(kv_r.at[:, pl.ds(0, others), :], kv_recv)
    kt_v[...] = kv_r[0].T

    key_ids = lax.broadcasted_iota(jnp.int32, (HD, QBLK), 0)
    lane_ids = lax.broadcasted_iota(jnp.int32, (HD, QBLK), 1)

    def fold(tile):
        return tile.reshape(HD // 8, 8, QBLK)

    def span(b):
        first = sum((i + 1) * QBLK for i in range(b))
        return first, (b + 1) * QBLK

    def weigh(h, b):
        r0 = b * QBLK
        first, keys = span(b)
        q_blk = qd_r[h, 0, r0 : r0 + QBLK, :]
        begin_row = begin_v[:, r0 : r0 + QBLK]
        top = jnp.full((8, QBLK), -1e30, FULL)
        for j in range(0, keys, QBLK):
            block = lax.dot_general(
                kv_r[0, j : j + QBLK, :], q_blk, NT, preferred_element_type=FULL
            )
            for i in range(j, j + QBLK, HD):
                seen = key_ids + i >= begin_row
                if j >= r0:
                    seen = seen & (key_ids + (i - r0) <= lane_ids)
                tile = jnp.where(seen, block[i - j : i - j + HD], -1e30)
                s_v[first + i : first + i + HD, :] = tile
                top = jnp.maximum(top, jnp.max(fold(tile), axis=0))
        top = jnp.max(top, axis=0, keepdims=True)
        mass = jnp.zeros((8, QBLK), FULL)
        for j in range(keys // HD):
            at = slice(first + j * HD, first + (j + 1) * HD)
            tile = jnp.exp2((s_v[at, :] - top) * exp_scale)
            s_v[at, :] = tile
            mass = mass + jnp.sum(fold(tile), axis=0)
        inverse = 1.0 / jnp.sum(mass, axis=0, keepdims=True)
        inv_v[b : b + 1, :] = inverse
        for j in range(keys // HD):
            at = slice(first + j * HD, first + (j + 1) * HD)
            wl_v[at, :] = (s_v[at, :] * inverse).astype(LOW)

    def value_grad(h, b):
        r0 = b * QBLK
        first, keys = span(b)
        acc[1, 0:keys, :] += jnp.dot(
            wl_v[first : first + keys, :],
            qd_r[h, 1, r0 : r0 + QBLK, :],
            preferred_element_type=FULL,
        )

    def send_terms(part, first_block, last_block):
        for j in range(first_block, last_block):
            term = acc[part, j * rows : (j + 1) * rows, :]
            if part == 0:
                term = term * inv_root
            dl_s[j, part] = term.astype(LOW)

            @pl.when(me != j)
            def _():
                dl_copy(part, j).start()

    def attend(h, b):
        r0 = b * QBLK
        first, keys = span(b)
        q_blk = qd_r[h, 0, r0 : r0 + QBLK, :]
        do_blk = qd_r[h, 1, r0 : r0 + QBLK, :]
        delta = jnp.zeros((8, QBLK), FULL)
        for j in range(0, keys, QBLK):
            at = slice(first + j, first + j + QBLK)
            block = lax.dot_general(
                kv_r[1, j : j + QBLK, :], do_blk, NT, preferred_element_type=FULL
            )
            pg_v[at, :] = block
            terms = wl_v[at, :].astype(FULL) * block
            delta = delta + jnp.sum(terms.reshape(QBLK // 8, 8, QBLK), axis=0)
        delta = jnp.sum(delta, axis=0, keepdims=True)
        inverse = inv_v[b : b + 1, :]
        for j in range(keys // HD):
            at = slice(first + j * HD, first + (j + 1) * HD)
            ds_v[at, :] = (s_v[at, :] * inverse * (pg_v[at, :] - delta)).astype(LOW)
        all_keys = slice(first, first + keys)
        acc[0, 0:keys, :] += jnp.dot(ds_v[all_keys, :], q_blk, preferred_element_type=FULL)

    def query_grad(b):
        r0 = b * QBLK
        first, keys = span(b)
        grad_t = jnp.dot(
            kt_v[:, 0:keys], ds_v[first : first + keys, :], preferred_element_type=FULL
        )
        grad_rows = (grad_t * inv_root).T.astype(LOW)
        for j in range(per_block):
            dq_s[r0 // rows + j] = grad_rows[j * rows : (j + 1) * rows, :]

    def send_dq(h):
        each(1, group_size, lambda o: dq_copy(h, o, True).start())
        dq_stay(h).start()

    def one_head(h):
        settle(qd_r.at[h, 0], in_recv.at[h, 0])
        for b in reversed(range(blocks)):
            weigh(h, b)
        settle(qd_r.at[h, 1], in_recv.at[h, 1])

        for b in reversed(range(blocks)):
            value_grad(h, b)

        @pl.when(h == heads - 1)
        def _():
            send_terms(1, 0, group_size)

        for b in reversed(range(blocks)):
            attend(h, b)

            @pl.when(h == heads - 1)
            def _():
                send_terms(0, b * per_block, (b + 1) * per_block)

        for b in range(blocks):
            query_grad(b)
        for b in range(group_size):
            dq_g[h, b * rows : (b + 1) * rows, :] = dq_s[sources[b]]

    each(0, heads, one_head)

    each(0, heads, send_dq)
    for b in range(group_size):
        dg_s[b] = dl_s[sources[b]]
    each(1, group_size, lambda o: dg_copy(o, True).start())
    dl_r[me] = dl_s[me]

    def merge(received, part, g):
        return (
            received[g, part].astype(FULL) + received[KVH + g, part].astype(FULL)
        ).astype(LOW)

    last = ORDER[-1]

    def gather(part):
        which = part * PCOLS // kvw
        for i in range(PCOLS // HD):
            dkv_all[y * 2 + core, part, :, i * HD : (i + 1) * HD] = merge(
                dl_r, which, (part * PCOLS % kvw) // HD + i
            )
        for k in range(3 if part == last else 2):
            ya_copy(part, k, True).start()
        yc_copy(part, 0, True).start()

    settle(dl_r.at[seven, 1], dl_recv.at[1])
    for part in ORDER[: PARTS // 2]:
        gather(part)
    settle(dl_r.at[seven, 0], dl_recv.at[0])
    for part in ORDER[PARTS // 2 :]:
        gather(part)

    settle(kv_r.at[:, pl.ds(0, others), :], kv_send)
    settle(qd_r.at[:, :, pl.ds(0, others), :], in_send)
    settle(hid_s.at[pl.ds(0, column - 1)], hid_send)

    settle(hid_s.at[pl.ds(0, column - 1)], hid_recv)
    def pass_on(part):
        for k in range(2):
            ya_copy(part, k, False).wait_recv()
            if part != last:
                yf_copy(part, k, True).start()
            yc_copy(part, 1 if k else ys - 1, True).start()

    def hand_far(part):
        if part != last:
            settle(dkv_all.at[0, part], yf_recv.at[part])
        else:
            ya_copy(part, 2, False).wait_recv()
        yc_copy(part, 2, True).start()

    def multiply(part):
        for k in (0, 1, ys - 1, 2):
            yc_copy(part, k, False).wait_recv()
            from_y = lax.rem(y + k, ys)
            grads = dkv_all[pl.ds(from_y * 2, 2), part].reshape(2 * rows, PCOLS)
            term = jnp.dot(hid_t[from_y], grads, preferred_element_type=FULL)
            if k > 0:
                term = prod[part] + term
            prod[part] = term
            if k == 2:
                prod_s[part] = term.astype(LOW)
        if part in TWO_STEP:
            rx_copy(part).start()
        else:
            each(1, summed_over, lambda o: rs_copy(part, o).start())

    def combine(part):
        settle(rx_r.at[part], rx_recv.at[part])
        at = pl.ds(x_hi * half_rows, half_rows)
        both = prod[part, at, :] + rx_r[part].astype(FULL)
        prod[part, at, :] = both
        prod_s[part, at, :] = both.astype(LOW)
        each(1, group_size, lambda o: rs_copy(part, o).start())

    pass_on(ORDER[0])
    for i, part in enumerate(ORDER):
        if i + 1 < PARTS:
            pass_on(ORDER[i + 1])
        hand_far(part)
        multiply(part)
        if i > 0 and ORDER[i - 1] in TWO_STEP:
            combine(ORDER[i - 1])

    dg_r[me] = dg_s[me]
    settle(dg_r.at[seven], dg_recv)
    dk_rows = jnp.concatenate([merge(dg_r, 0, g) for g in range(KVH)], axis=1)
    dv_rows = jnp.concatenate([merge(dg_r, 1, g) for g in range(KVH)], axis=1)

    def hidden_tile(t):
        at = pl.ds(pl.multiple_of(t * 512, 512), 512)
        tile = lax.dot_general(
            dk_rows, kw_v[at, :], NT, preferred_element_type=FULL
        ) + lax.dot_general(dv_rows, vw_v[at, :], NT, preferred_element_type=FULL)
        gh_v[:, at] = tile.astype(LOW)

    each(0, width // 512, hidden_tile)
    gh_out = pltpu.make_async_copy(gh_v, grad_hidden, gh_sem)
    gh_out.start()

    settle(dg_s.at[seven], dg_send)
    settle(dl_s.at[seven], dl_send)
    settle(dq_g.at[:, pl.ds(0, others), :], dq_send)
    settle(dq_g.at[:, pl.ds(0, others), :], dq_recv)
    settle(dq_g.at[:, pl.ds(0, rows), :], dq_own)
    settle(dkv_all.at[pl.ds(0, 2)], ya_send)
    settle(dkv_all.at[0, 0], ya_send)
    settle(dkv_all.at[0, pl.ds(0, PARTS - 1)], yf_send)
    settle(dkv_all.at[pl.ds(0, ys)], yc_send)

    norm = 1.0 / math.sqrt(total * replica_count)
    own = pl.ds(pl.multiple_of((x_hi * group_size + me) * piece, piece), piece)
    for part in ORDER:
        senders = group_size if part in TWO_STEP else summed_over
        settle(rs_r.at[part, pl.ds(0, senders - 1)], rs_recv.at[part])
        summed = prod[part, own, :]
        for o in range(1, senders):
            summed = summed + rs_r[part, o].astype(FULL)
        result = grad_value if part * PCOLS >= kvw else grad_key
        at = part * PCOLS % kvw
        result[:, at : at + PCOLS] = (summed * norm).astype(LOW)

    gh_out.wait()
    for part in range(PARTS):
        senders = group_size if part in TWO_STEP else summed_over
        settle(rs_r.at[part, pl.ds(0, senders - 1)], rs_send)
    for part in TWO_STEP:
        settle(rx_r.at[part], rx_send)


def hand_over(*refs):
    sources, results = refs[0:4], refs[4:8]
    held, sems = refs[8:12], refs[12]
    steps = []
    for i, (source, result, slot) in enumerate(zip(sources, results, held)):
        parts = 4 if i < 2 else 1
        size = source.shape[0] // parts
        for j in range(parts):
            at = pl.ds(j * size, size)
            steps.append(
                (
                    pltpu.make_async_copy(source.at[at], slot.at[at], sems.at[0, i, j]),
                    pltpu.make_async_copy(slot.at[at], result.at[at], sems.at[1, i, j]),
                )
            )
    for load, _ in steps:
        load.start()
    for load, store in steps:
        load.wait()
        store.start()
    for _, store in steps:
        store.wait()


def on_device(
    hidden, queries, out_grad, key_weight, value_weight, seq_lengths, seq_group, loader_offsets
):
    group_size = lax.axis_size("grp")
    replica_count = lax.axis_size("dp")
    rows, width = hidden.shape[1:]
    total = rows * group_size
    heads = HQ // group_size
    kvw = KVH * HD
    piece = width // (group_size * replica_count)
    blocks = total // QBLK
    ys = replica_count // 4
    column = 2 * ys
    chunk = width // column
    tall = sum((b + 1) * QBLK for b in range(blocks))
    dma = pltpu.SemaphoreType.DMA
    scratch = [
        pltpu.VMEM((rows, width), LOW),
        pltpu.VMEM((width, kvw), LOW),
        pltpu.VMEM((width, kvw), LOW),
        pltpu.VMEM((heads, 2, total, HD), LOW),
        pltpu.VMEM((KVH, 2, rows, HD), LOW),
        pltpu.VMEM((2, total, HD), LOW),
        pltpu.VMEM((HD, total), LOW),
        pltpu.VMEM((column, chunk, rows), LOW),
        pltpu.VMEM((ys, chunk, 2 * rows), LOW),
        pltpu.VMEM((tall, QBLK), FULL),
        pltpu.VMEM((tall, QBLK), FULL),
        pltpu.VMEM((tall, QBLK), LOW),
        pltpu.VMEM((tall, QBLK), LOW),
        pltpu.VMEM((2, total, HD), FULL),
        pltpu.VMEM((group_size, rows, HD), LOW),
        pltpu.VMEM((heads, total, HD), LOW),
        pltpu.VMEM((group_size, 2, rows, HD), LOW),
        pltpu.VMEM((group_size, 2, rows, HD), LOW),
        pltpu.VMEM((group_size, 2, rows, HD), LOW),
        pltpu.VMEM((group_size, 2, rows, HD), LOW),
        pltpu.VMEM((column, PARTS, rows, PCOLS), LOW),
        pltpu.VMEM((PARTS, chunk, PCOLS), FULL),
        pltpu.VMEM((PARTS, chunk, PCOLS), LOW),
        pltpu.VMEM((PARTS, chunk // 2, PCOLS), LOW),
        pltpu.VMEM((PARTS, 2 * group_size, piece, PCOLS), LOW),
        pltpu.VMEM((rows, width), LOW),
        pltpu.VMEM((1, total), jnp.int32),
        pltpu.VMEM((8, QBLK), FULL),
        dma((3,)),
        dma,
        dma((heads, 2)),
        dma,
        dma,
        dma,
        dma,
        dma,
        dma,
        dma,
        dma,
        dma((2,)),
        dma,
        dma,
        dma,
        dma((PARTS, 3)),
        dma,
        dma((PARTS,)),
        dma,
        dma((PARTS, ys)),
        dma,
        dma((PARTS,)),
        dma,
        dma((PARTS,)),
        dma,
    ]
    smem = pl.BlockSpec(memory_space=pltpu.SMEM)
    vmem = pl.BlockSpec(memory_space=pltpu.VMEM)
    anywhere = pl.BlockSpec(memory_space=pl.ANY)

    def kernel(*refs):
        layer_kernel(group_size, replica_count, *refs)

    out_shape = (
        jax.ShapeDtypeStruct((rows, HQ * HD), LOW),
        jax.ShapeDtypeStruct((rows, width), LOW),
        jax.ShapeDtypeStruct((piece, kvw), LOW),
        jax.ShapeDtypeStruct((piece, kvw), LOW),
    )
    results = pl.pallas_call(
        kernel,
        out_shape=out_shape,
        in_specs=[smem, smem, smem] + [anywhere] * 5,
        out_specs=(anywhere, anywhere, vmem, vmem),
        scratch_shapes=scratch,
        compiler_params=pltpu.CompilerParams(
            collective_id=0, has_side_effects=True, vmem_limit_bytes=56 * 1024 * 1024
        ),
        name="layer",
    )(
        seq_lengths,
        seq_group,
        loader_offsets,
        hidden[0],
        queries[0],
        out_grad[0],
        key_weight,
        value_weight,
    )
    grad_query, grad_hidden, grad_key, grad_value = pl.pallas_call(
        hand_over,
        out_shape=out_shape,
        in_specs=[anywhere] * 4,
        out_specs=[anywhere] * 4,
        scratch_shapes=[pltpu.VMEM(shape.shape, LOW) for shape in out_shape] + [dma((2, 4, 4))],
        name="hand_over",
    )(*results)
    return (grad_query[None], grad_hidden[None], grad_key, grad_value)


def solution(mesh):
    placed = (
        P("dp", "grp", None),
        P("dp", "grp", None),
        P("dp", "grp", None),
        P(),
        P(),
        P("dp", None),
        P("dp", None),
        P("dp", None),
    )
    return jax.shard_map(
        on_device,
        mesh=mesh,
        in_specs=placed,
        out_specs=(
            P("dp", "grp", None),
            P("dp", "grp", None),
            P(("grp", "dp"), None),
            P(("grp", "dp"), None),
        ),
        check_vma=False,
    )
```
